512 devices in a mesh: stream: 64 (over z, y), head: 8 (over x, core).
Axes of the slice: x: 4, y: 8, z: 8, core: 2. Of those that a mesh axis runs over, the one named last changes fastest.
Arguments:
- queries: bfloat16 [64, 3, 8192], P('stream', None, 'head'), may hold values from -7 to 7
- new_kv: bfloat16 [64, 3, 2048], P('stream', None, 'head'), may hold values from -6 to 6
- cache_kv: bfloat16 [64, 2048, 2048], P('stream', None, 'head'), may hold values from -6 to 6
- cache_fill: int32 [64], P('stream'), may hold values from 1 to 2048, 65536 in all
- fresh_kv: bfloat16 [64, 1024, 2048], P(None, 'stream', 'head'), may hold values from -6 to 6
- fresh_len: int32 [64], replicated, may hold values from 1 to 1024, 32768 in all
- owner_slot: int32 [64], replicated, may hold values from 0 to 63, each once
- out_weight: bfloat16 [8192, 5120], P('head', 'stream'), may hold values from -0.0625 to 0.0625
Outputs:
- decoded: bfloat16 [64, 3, 5120], P(None, None, 'stream')
The draws below stay inside these ranges and needn't reach their ends.
Inputs may be any that keep to these rules, and one draw needn't show every extreme that they name: `fresh_len`: one segment has exactly 1024 frames, every segment at least one.
All inputs are finite; a program needn't handle non-finite values. No bound on the sum of `cache_fill` on one device may be relied on, other than what follows from the above.
Results may differ from the reference program's by a relative error of at most 0.0055.
Values may be sent and summed in bfloat16 or wider, within the bound.
A program may use at most 64 MiB of HBM per device.

```python
import math
import jax
import jax.numpy as jnp
import numpy as np
from jax import lax

D = 5120
Q_HEADS = 64
KV_HEADS = 8
D_HEAD = 128
GROUP = 8
TRACKS = 64
STEPS = 3
MEAN_LEN = 512
FRESH_MAX = 1024
CACHE = 2048
CBLK = 512
N_STREAM = 64


def draw_queries(key, part):
    key = jax.random.fold_in(key, 11)
    array_shape = (TRACKS, STEPS, Q_HEADS, D_HEAD)
    values = jnp.clip(jax.random.normal(key, array_shape, jnp.float32), -6.0, 6.0)
    return values.reshape(TRACKS, STEPS, Q_HEADS * D_HEAD).astype(jnp.bfloat16)


def draw_cache_kv(key, part):
    key = jax.random.fold_in(key, 12)
    array_shape = (TRACKS, CACHE, KV_HEADS, 2, D_HEAD)
    values = jnp.clip(jax.random.normal(key, array_shape, jnp.float32), -6.0, 6.0)
    return values.reshape(TRACKS, CACHE, KV_HEADS * 2 * D_HEAD).astype(jnp.bfloat16)


def level_of(own_key, shape, pieces, low, high):
    factor_of = 1.0
    for dim, parts in pieces:
        draws = jax.random.uniform(jax.random.fold_in(jax.random.fold_in(own_key, 6), dim), (parts,), jnp.float32, low / len(pieces), high / len(pieces))
        factor_of = factor_of * jnp.repeat(jnp.exp(draws), shape[dim] // parts).reshape((-1,) + (1,) * (len(shape) - 1 - dim))
    return factor_of


def length_profile(amount, total, bound, slope):
    weights = [(1 << 20) // math.isqrt(standing ** slope) + 1 for standing in range(2, amount + 1)]
    rest, counts = total - bound - (amount - 1), [1] * (amount - 1)
    while rest > 0:
        movable = [i for i in range(amount - 1) if counts[i] < bound]
        whole, remaining = sum([weights[i] for i in movable]), rest
        for i in movable:
            extra = min(bound - counts[i], max(1, remaining * weights[i] // whole), rest)
            counts[i] = counts[i] + extra
            rest = rest - extra
    return np.array([bound] + counts)


def ragged_sizes(key, count, total, bound, slope):
    if count == 2:
        one = jax.random.randint(key, (), max(1, total - bound), min(bound, total - 1) + 1)
        return jnp.stack([one, total - one])
    lengths = jnp.asarray(length_profile(count, total, bound, slope), jnp.int32)
    couples = (count - 1) // 2
    source_of, taker = lengths[1:1 + 2 * couples:2], lengths[2:2 + 2 * couples:2]
    margin = jnp.minimum(source_of - 1, bound - taker)
    shifted = jax.random.randint(jax.random.fold_in(key, 1), (couples,), 0, 1 << 20) % (margin + 1)
    lengths = lengths.at[1:1 + 2 * couples:2].set(source_of - shifted).at[2:2 + 2 * couples:2].set(taker + shifted)
    return lengths[jax.random.permutation(jax.random.fold_in(key, 2), count)]


def gaussian(rng, extent, scale, reach, pieces=(), kind=jnp.bfloat16):
    drawn = jax.random.normal(rng, extent, jnp.float32) * scale
    if len(pieces) > 0:
        drawn = level_of(rng, extent, pieces, -0.22, 0.18) * drawn
    return jnp.clip(drawn, min=-reach, max=reach).astype(kind)


def setup_inputs(seed: int = 0) -> dict:
    arg_keys = jax.random.split(jax.random.key(seed), 9)
    queries = draw_queries(jax.random.fold_in(arg_keys[8], 71), 0)
    new_kv = gaussian(arg_keys[1], (TRACKS, STEPS, KV_HEADS * 2 * D_HEAD), 1.0, 6.0, ((0, 64), (2, 8)))
    cache_kv = draw_cache_kv(jax.random.fold_in(arg_keys[8], 71), 0)
    cache_fill = ragged_sizes(arg_keys[3], TRACKS, TRACKS * CACHE // 2, CACHE, 1).astype(jnp.int32)
    fresh_kv = gaussian(arg_keys[4], (TRACKS, FRESH_MAX, KV_HEADS * 2 * D_HEAD), 1.0, 6.0, ((1, 64), (2, 8)))
    fresh_len = ragged_sizes(arg_keys[5], TRACKS, TRACKS * MEAN_LEN, FRESH_MAX, 2).astype(jnp.int32)
    owner_slot = jax.random.permutation(arg_keys[6], TRACKS).astype(jnp.int32)
    out_weight = gaussian(arg_keys[7], (Q_HEADS * D_HEAD, D), (Q_HEADS * D_HEAD) ** -0.5, 0.0625, ((0, 8), (1, 64)))
    return {"queries": queries, "new_kv": new_kv, "cache_kv": cache_kv, "cache_fill": cache_fill, "fresh_kv": fresh_kv, "fresh_len": fresh_len, "owner_slot": owner_slot, "out_weight": out_weight}


def split_pairs(packed, heads_here):
    shaped = packed.reshape(packed.shape[0], packed.shape[1], heads_here, 2, packed.shape[2] // (2 * heads_here))
    return shaped[:, :, :, 0], shaped[:, :, :, 1]


def block_pieces(query_matrix_rows, key_matrix_rows, value_rows, valid_mask, block_size):
    logit_scores = jnp.einsum("xwve,xowe->xwvo", query_matrix_rows, key_matrix_rows) * (query_matrix_rows.shape[-1] ** -0.5)
    track_count, head_count, row_count, key_count = logit_scores.shape
    nblocks = key_count // block_size
    grouped = logit_scores.reshape(track_count, head_count, row_count, nblocks, block_size)
    allowed = jnp.broadcast_to(valid_mask, (track_count, 1, row_count, key_count)).reshape(track_count, 1, row_count, nblocks, block_size)
    highest = jnp.max(jnp.where(allowed, grouped, -1e30), axis=-1)
    weights = jnp.where(allowed, jnp.exp(grouped - highest[..., None]), 0.0)
    totals = jnp.sum(weights, axis=-1)
    rounded = lax.optimization_barrier(weights.astype(jnp.bfloat16)).astype(jnp.float32)
    values_grouped = value_rows.reshape(track_count, nblocks, block_size, head_count, value_rows.shape[-1])
    outputs = jnp.einsum("shrnb,snbhd->shrnd", rounded, values_grouped)
    return highest, totals, outputs


def combine_parts(portions):
    highest = jnp.concatenate([portion[0] for portion in portions], axis=3)
    totals = jnp.concatenate([portion[1] for portion in portions], axis=3)
    outputs = jnp.concatenate([portion[2] for portion in portions], axis=3)
    top_value = jnp.max(highest, axis=3, keepdims=True)
    factor = jnp.exp(highest - top_value)
    return jnp.sum(factor[..., None] * outputs, axis=3) / jnp.sum(factor * totals, axis=3)[..., None]


def reference(queries, new_kv, cache_kv, cache_fill, fresh_kv, fresh_len, owner_slot, out_weight):
    numbers = jnp.arange(TRACKS, dtype=jnp.int32)
    inverse_permutation_map = jnp.zeros((TRACKS,), jnp.int32).at[owner_slot].set(numbers)
    row_count = STEPS * GROUP
    block_size = FRESH_MAX // N_STREAM
    step_of_row = jnp.arange(row_count, dtype=jnp.int32) // GROUP
    new_valid = (jnp.arange(STEPS, dtype=jnp.int32)[None, :] <= step_of_row[:, None]).reshape(1, 1, row_count, STEPS)

    def attend_one(slot):
        track = inverse_permutation_map[slot]
        query_block = lax.dynamic_slice_in_dim(queries, slot, 1, 0).astype(jnp.float32)
        query_matrix_rows = query_block.reshape(1, STEPS, KV_HEADS, GROUP, D_HEAD).transpose(0, 2, 1, 3, 4).reshape(1, KV_HEADS, row_count, D_HEAD)
        cache_block = lax.dynamic_slice_in_dim(cache_kv, slot, 1, 0).astype(jnp.float32)
        fresh_block = lax.dynamic_slice_in_dim(fresh_kv, track, 1, 0).astype(jnp.float32)
        new_block = lax.dynamic_slice_in_dim(new_kv, slot, 1, 0).astype(jnp.float32)
        cache_keys, cache_values = split_pairs(cache_block, KV_HEADS)
        fresh_keys, fresh_values = split_pairs(fresh_block, KV_HEADS)
        new_keys, new_values = split_pairs(new_block, KV_HEADS)
        cache_valid = (jnp.arange(CACHE, dtype=jnp.int32) < cache_fill[slot]).reshape(1, 1, 1, CACHE)
        fresh_valid = (jnp.arange(FRESH_MAX, dtype=jnp.int32) < fresh_len[track]).reshape(1, 1, 1, FRESH_MAX)
        portions = [
            block_pieces(query_matrix_rows, cache_keys, cache_values, cache_valid, CBLK),
            block_pieces(query_matrix_rows, new_keys, new_values, new_valid, STEPS),
            block_pieces(query_matrix_rows, fresh_keys, fresh_values, fresh_valid, block_size),
        ]
        merged = combine_parts(portions)
        return merged.reshape(KV_HEADS, STEPS, GROUP, D_HEAD).transpose(1, 0, 2, 3).reshape(STEPS, Q_HEADS * D_HEAD).astype(jnp.bfloat16)

    attention = lax.map(attend_one, numbers)
    flat = attention.reshape(TRACKS * STEPS, Q_HEADS * D_HEAD)
    projected = jnp.dot(flat, out_weight, preferred_element_type=jnp.float32).astype(jnp.bfloat16)
    return projected.reshape(TRACKS, STEPS, D)[owner_slot]
```

```python
import functools

import jax
import jax.numpy as jnp
from jax import lax
from jax.experimental import pallas as pl
from jax.experimental.pallas import tpu as pltpu
from jax.sharding import PartitionSpec as P

D_HEAD = 128
GROUP = 8
STEPS = 3
ROWS = STEPS * GROUP
PAD = 32
CBLK = 512
SIDE = 8
HALF = 4
NONE = -1e30
SCALE = D_HEAD**-0.5
FAR_FIRST = (4, 3, 5, 2, 6, 1, 7)
MESH = pl.DeviceIdType.MESH


def remote(src, dst, send_sem, recv_sem, device):
    return pltpu.make_async_remote_copy(
        src_ref=src,
        dst_ref=dst,
        send_sem=send_sem,
        recv_sem=recv_sem,
        device_id=device,
        device_id_type=MESH,
    )


def attend(query_rows, keys, values, valid):
    scores = (
        lax.dot_general(
            query_rows, keys, (((1,), (1,)), ((), ())), preferred_element_type=jnp.float32
        )
        * SCALE
    )
    highest = jnp.max(jnp.where(valid, scores, NONE), axis=1, keepdims=True)
    weights = jnp.where(valid, jnp.exp(scores - highest), 0.0)
    total = jnp.sum(weights, axis=1, keepdims=True)
    output = jnp.dot(weights.astype(jnp.bfloat16), values, preferred_element_type=jnp.float32)
    return highest, total, output


def merge(parts):
    top = functools.reduce(jnp.maximum, [part[0] for part in parts])
    factors = [jnp.exp(part[0] - top) for part in parts]
    total = sum(f * part[1] for f, part in zip(factors, parts))
    output = sum(f * part[2] for f, part in zip(factors, parts))
    return top, total, output


def kernel(
    owner_row_ref,
    owner_ref,
    len_ref,
    fill_ref,
    query_ref,
    new_ref,
    cache_hbm,
    fresh_hbm,
    weight_hbm,
    out_ref,
    cache,
    fresh,
    weight,
    table,
    table_smem,
    query_f32,
    query_all,
    send_kv,
    recv_kv,
    state_m,
    state_l,
    state_o,
    pieces,
    gathered,
    stage,
    ordered,
    partial,
    from_core,
    from_x,
    final,
    local_sem,
    q_send,
    q_recv,
    kv_send,
    kv_recv,
    o_send,
    o_recv,
    g_send,
    g_recv,
    c_send,
    c_recv,
    x_send,
    x_recv,
):
    stream = lax.axis_index("stream")
    head = lax.axis_index("head")
    z, y = stream // SIDE, stream % SIDE
    x, core = head // 2, head % 2
    me = (z, y)

    def at(zz, yy):
        return {"stream": lax.rem(zz, SIDE) * SIDE + lax.rem(yy, SIDE)}

    def along(axis, step):
        return at(z + step, y) if axis == 0 else at(z, y + step)

    def x_peer(step):
        return {"head": lax.rem(x + step, 4) * 2 + core}

    other_core = {"head": x * 2 + 1 - core}

    barrier = pltpu.get_barrier_semaphore()
    peers = [along(axis, step) for step in FAR_FIRST for axis in (0, 1)]
    peers += [x_peer(step) for step in (2, 1, 3)] + [other_core]
    for peer in peers:
        pl.semaphore_signal(barrier, inc=1, device_id=peer, device_id_type=MESH)

    load_fresh = pltpu.make_async_copy(fresh_hbm, fresh, local_sem.at[0])
    load_cache = pltpu.make_async_copy(cache_hbm, cache, local_sem.at[1])
    load_weight = pltpu.make_async_copy(weight_hbm, weight, local_sem.at[2])
    load_fresh.start()
    load_cache.start()
    load_weight.start()

    n_tracks = owner_row_ref.shape[1]
    owner = owner_row_ref[...]
    slot_of = lax.broadcasted_iota(jnp.int32, (n_tracks, n_tracks), 0)
    lane_of = lax.broadcasted_iota(jnp.int32, (n_tracks, n_tracks), 1)
    track_column = jnp.max(jnp.where(owner == slot_of, lane_of, 0), axis=1, keepdims=True)
    track_row = jnp.max(jnp.where(slot_of == lane_of, track_column, 0), axis=0, keepdims=True)
    owner_z, owner_y = owner // SIDE, owner % SIDE
    place_row = jnp.where(
        (owner_z + owner_y) % 2 == 0,
        owner_z * HALF + owner_y // 2,
        SIDE * HALF + owner_y * HALF + owner_z // 2,
    )
    table[...] = jnp.zeros_like(table)
    table[0:1, 0:n_tracks] = track_row
    table[1:2, 0:n_tracks] = place_row
    load_table = pltpu.make_async_copy(table, table_smem, local_sem.at[3])
    load_table.start()

    query_f32[...] = jnp.zeros_like(query_f32)
    query_flat = query_ref[0].astype(jnp.float32)
    for g in range(GROUP):
        query_f32[pl.ds(g, STEPS, stride=GROUP), :] = query_flat[
            :, g * D_HEAD : (g + 1) * D_HEAD
        ]
    parity = (z + y) % 2
    mine = jnp.where(parity == 0, y // 2, HALF + z // 2)
    my_query = query_f32[...].astype(jnp.bfloat16)
    query_all[mine] = my_query
    state_m[...] = jnp.full_like(state_m, NONE)
    state_l[...] = jnp.zeros_like(state_l)
    state_o[...] = jnp.zeros_like(state_o)
    partial[...] = jnp.zeros_like(partial)

    load_table.wait()
    load_fresh.wait()

    def slot_at(kind, place, i):
        if kind == 0:
            return place * SIDE + 2 * i + place % 2
        return (2 * i + 1 - place % 2) * SIDE + place

    for kind in (0, 1):
        for place in range(SIDE):
            for i in range(HALF):
                send_kv[kind, place, i] = fresh[table_smem[0, slot_at(kind, place, i)]]
    for kind in (0, 1):
        recv_kv[kind, me[kind]] = send_kv[kind, me[kind]]

    pl.semaphore_wait(barrier, len(peers))

    q_copies = []
    for n, step in enumerate(FAR_FIRST):
        peer = at(z + step * parity, y + step * (1 - parity))
        q_copies.append(
            remote(query_all.at[mine], query_all.at[mine], q_send.at[n], q_recv.at[mine], peer)
        )
        q_copies[-1].start()
    kv_copies = []
    for n, step in enumerate(FAR_FIRST):
        for kind in (0, 1):
            there = lax.rem(me[kind] + step, SIDE)
            kv_copies.append(
                remote(
                    send_kv.at[kind, there],
                    recv_kv.at[kind, me[kind]],
                    kv_send.at[kind, n],
                    kv_recv.at[kind, me[kind]],
                    along(kind, step),
                )
            )
            kv_copies[-1].start()

    load_cache.wait()
    parts = []
    fill = fill_ref[0]
    for block in range(cache.shape[0] // CBLK):
        rows = pl.ds(block * CBLK, CBLK)
        position = block * CBLK + lax.broadcasted_iota(jnp.int32, (PAD, CBLK), 1)
        parts.append(
            attend(my_query, cache[rows, :D_HEAD], cache[rows, D_HEAD:], position < fill)
        )
    query_full = query_f32[...]
    new_rows = new_ref[0].astype(jnp.float32)
    step_of_row = lax.broadcasted_iota(jnp.int32, (PAD, 1), 0) // GROUP
    new_scores = [
        jnp.where(
            u <= step_of_row,
            jnp.sum(query_full * new_rows[u : u + 1, :D_HEAD], axis=1, keepdims=True) * SCALE,
            NONE,
        )
        for u in range(STEPS)
    ]
    new_top = functools.reduce(jnp.maximum, new_scores)
    new_weights = [
        jnp.where(u <= step_of_row, jnp.exp(new_scores[u] - new_top), 0.0) for u in range(STEPS)
    ]
    new_output = sum(
        new_weights[u].astype(jnp.bfloat16).astype(jnp.float32) * new_rows[u : u + 1, D_HEAD:]
        for u in range(STEPS)
    )
    parts.append((new_top, sum(new_weights), new_output))
    top, total, output = merge(parts)
    state_m[mine] = jnp.broadcast_to(top, (PAD, D_HEAD))
    state_l[mine] = jnp.broadcast_to(total, (PAD, D_HEAD))
    state_o[mine] = output

    index_of_mine = lax.rem(mine, HALF)
    for n in range(2 * HALF - 1):
        if n < HALF - 1:
            came = parity * HALF + lax.rem(index_of_mine + 1 + n, HALF)
        else:
            came = (1 - parity) * HALF + n - (HALF - 1)
        remote(
            query_all.at[came], query_all.at[came], q_send.at[n], q_recv.at[came], other_core
        ).wait_recv()
    for step in FAR_FIRST[::-1]:
        for kind in (0, 1):
            there = lax.rem(me[kind] + step, SIDE)
            remote(
                send_kv.at[kind, there],
                recv_kv.at[kind, there],
                kv_send.at[kind, 0],
                kv_recv.at[kind, there],
                other_core,
            ).wait_recv()

    span = SIDE * 16
    lane = lax.broadcasted_iota(jnp.int32, (1, span), 1)
    positions = ((lane // 16) * SIDE * 16 + y * 16 + lane % 16, z * span + lane)
    row_id = lax.broadcasted_iota(jnp.int32, (PAD, D_HEAD), 0)
    lane_id = lax.broadcasted_iota(jnp.int32, (PAD, D_HEAD), 1)
    diagonal = row_id == lane_id
    row8 = lax.broadcasted_iota(jnp.int32, (8, D_HEAD), 0)
    for kind in (0, 1):
        for i in range(HALF):
            n = kind * HALF + i
            if kind == 0:
                slot = z * SIDE + 2 * i + z % 2
            else:
                slot = (2 * i + 1 - y % 2) * SIDE + y
            length = len_ref[table_smem[0, slot]]
            keys = recv_kv[kind, :, i, :, :D_HEAD].reshape(span, D_HEAD)
            values = recv_kv[kind, :, i, :, D_HEAD:].reshape(span, D_HEAD)
            top, total, output = merge(
                [
                    attend(query_all[n], keys, values, positions[kind] < length),
                    (state_m[n], state_l[n], state_o[n]),
                ]
            )
            log_sum = top + jnp.log(jnp.maximum(total, 0.5))
            output = output / jnp.maximum(total, 0.5)
            line = jnp.sum(jnp.where(diagonal, log_sum, 0.0), axis=0, keepdims=True)
            first = line.astype(jnp.bfloat16).astype(jnp.float32)
            second = (line - first).astype(jnp.bfloat16).astype(jnp.float32)
            third = line - first - second
            lines = jnp.where(
                row8 == 0,
                first,
                jnp.where(row8 == 1, second, jnp.where(row8 == 2, third, 0.0)),
            )
            pieces[kind, me[1 - kind], i] = jnp.concatenate(
                [output[:ROWS], lines], axis=0
            ).astype(jnp.bfloat16)

    o_copies = []
    for n, step in enumerate(FAR_FIRST):
        for kind in (0, 1):
            mine_here = me[1 - kind]
            o_copies.append(
                remote(
                    pieces.at[kind, mine_here],
                    pieces.at[kind, mine_here],
                    o_send.at[kind, n],
                    o_recv.at[kind, mine_here],
                    along(1 - kind, step),
                )
            )
            o_copies[-1].start()
    for step in FAR_FIRST[::-1]:
        for kind in (0, 1):
            there = lax.rem(me[1 - kind] + step, SIDE)
            remote(
                pieces.at[kind, there],
                pieces.at[kind, there],
                o_send.at[kind, 0],
                o_recv.at[kind, there],
                other_core,
            ).wait_recv()

    for kind in (0, 1):
        rows = []
        for i in range(HALF):
            arrived = [pieces[kind, src, i].astype(jnp.float32) for src in range(SIDE)]
            logs = [jnp.sum(a[ROWS:], axis=0, keepdims=True) for a in arrived]
            top = functools.reduce(jnp.maximum, logs)
            shares = [jnp.exp(log - top) for log in logs]
            total = sum(shares)
            acc = None
            for a, share in zip(arrived, shares):
                column = jnp.sum(
                    jnp.where(diagonal[:ROWS], share / total, 0.0), axis=1, keepdims=True
                )
                term = column * a[:ROWS]
                acc = term if acc is None else acc + term
            rows.append(acc)
        gathered[kind, me[kind]] = jnp.concatenate(rows, axis=0).astype(jnp.bfloat16)

    g_copies = []
    for n, step in enumerate(FAR_FIRST):
        for kind in (0, 1):
            g_copies.append(
                remote(
                    gathered.at[kind, me[kind]],
                    gathered.at[kind, me[kind]],
                    g_send.at[kind, n],
                    g_recv.at[kind, me[kind]],
                    along(kind, step),
                )
            )
            g_copies[-1].start()
    load_weight.wait()
    for step in (0,) + FAR_FIRST[::-1]:
        for kind in (0, 1):
            there = lax.rem(me[kind] + step, SIDE)
            if step:
                remote(
                    gathered.at[kind, there],
                    gathered.at[kind, there],
                    g_send.at[kind, 0],
                    g_recv.at[kind, there],
                    other_core,
                ).wait_recv()
            stage[pl.ds((kind * SIDE + there) * HALF, HALF)] = (
                gathered[kind, there].astype(jnp.float32).reshape(HALF, ROWS, D_HEAD)
            )

    for track in range(n_tracks):
        rows = stage[table_smem[1, track]]
        for t in range(STEPS):
            ordered[pl.ds((t * n_tracks + track) * GROUP, GROUP), :] = rows[
                t * GROUP : (t + 1) * GROUP
            ]
    width = weight.shape[0]
    product = None
    for g in range(GROUP):
        left = ordered[pl.ds(g, n_tracks * STEPS, stride=GROUP), :].astype(jnp.bfloat16)
        term = lax.dot_general(
            left,
            weight[:, g * D_HEAD : (g + 1) * D_HEAD],
            (((1,), (1,)), ((), ())),
            preferred_element_type=jnp.float32,
        )
        product = term if product is None else product + term
    half = n_tracks * STEPS // 2
    partial[0, :, :width] = product[:half]
    partial[1, :, :width] = product[half:]

    swap = remote(
        partial.at[1 - core], from_core, c_send.at[0], c_recv.at[0], other_core
    )
    swap.start()
    swap.wait_recv()
    from_x[x] = (partial[core] + from_core[...]).astype(jnp.bfloat16)
    x_copies = []
    for n, step in enumerate((2, 1, 3)):
        x_copies.append(
            remote(from_x.at[x], from_x.at[x], x_send.at[n], x_recv.at[x], x_peer(step))
        )
        x_copies[-1].start()
    for step in (1, 3, 2):
        there = lax.rem(x + step, 4)
        remote(
            from_x.at[there], from_x.at[there], x_send.at[0], x_recv.at[there], other_core
        ).wait_recv()
    summed = from_x[0].astype(jnp.float32)
    for there in range(1, 4):
        summed = summed + from_x[there].astype(jnp.float32)
    final[core] = summed.astype(jnp.bfloat16)
    give = remote(final.at[core], final.at[core], c_send.at[1], c_recv.at[1 + core], other_core)
    give.start()
    remote(
        final.at[1 - core], final.at[1 - core], c_send.at[1], c_recv.at[2 - core], other_core
    ).wait_recv()
    out_ref[0:half] = final[0][:, :width]
    out_ref[half:] = final[1][:, :width]

    for copy in q_copies + kv_copies + o_copies + g_copies + [swap] + x_copies + [give]:
        copy.wait_send()


def shards(queries, new_kv, cache_kv, cache_fill, fresh_kv, fresh_len, owner_slot, out_weight):
    n_tracks, depth = fresh_kv.shape[0], fresh_kv.shape[1]
    width = out_weight.shape[1]
    half = n_tracks * STEPS // 2
    vmem = pl.BlockSpec(memory_space=pltpu.VMEM)
    smem = pl.BlockSpec(memory_space=pltpu.SMEM)
    anywhere = pl.BlockSpec(memory_space=pl.ANY)
    bf16, f32 = jnp.bfloat16, jnp.float32
    dma = pltpu.SemaphoreType.DMA
    out = pl.pallas_call(
        kernel,
        name="handoff_decode",
        out_shape=jax.ShapeDtypeStruct((n_tracks * STEPS, width), bf16),
        in_specs=[vmem, smem, smem, smem, vmem, vmem, anywhere, anywhere, anywhere],
        out_specs=vmem,
        scratch_shapes=[
            pltpu.VMEM(cache_kv.shape[1:], bf16),
            pltpu.VMEM(fresh_kv.shape, bf16),
            pltpu.VMEM(out_weight.shape[::-1], bf16),
            pltpu.VMEM((8, 128), jnp.int32),
            pltpu.SMEM((8, 128), jnp.int32),
            pltpu.VMEM((PAD, D_HEAD), f32),
            pltpu.VMEM((2 * HALF, PAD, D_HEAD), bf16),
            pltpu.VMEM((2, SIDE, HALF, depth, 2 * D_HEAD), bf16),
            pltpu.VMEM((2, SIDE, HALF, depth, 2 * D_HEAD), bf16),
            pltpu.VMEM((2 * HALF, PAD, D_HEAD), f32),
            pltpu.VMEM((2 * HALF, PAD, D_HEAD), f32),
            pltpu.VMEM((2 * HALF, PAD, D_HEAD), f32),
            pltpu.VMEM((2, SIDE, HALF, PAD, D_HEAD), bf16),
            pltpu.VMEM((2, SIDE, HALF * ROWS, D_HEAD), bf16),
            pltpu.VMEM((n_tracks, ROWS, D_HEAD), f32),
            pltpu.VMEM((n_tracks * ROWS, D_HEAD), f32),
            pltpu.VMEM((2, half, 128), f32),
            pltpu.VMEM((half, 128), f32),
            pltpu.VMEM((4, half, 128), bf16),
            pltpu.VMEM((2, half, 128), bf16),
            dma((4,)),
            dma((SIDE - 1,)),
            dma((2 * HALF,)),
            dma((2, SIDE - 1)),
            dma((2, SIDE)),
            dma((2, SIDE - 1)),
            dma((2, SIDE)),
            dma((2, SIDE - 1)),
            dma((2, SIDE)),
            dma((2,)),
            dma((3,)),
            dma((3,)),
            dma((4,)),
        ],
        compiler_params=pltpu.CompilerParams(
            collective_id=0, has_side_effects=True, vmem_limit_bytes=32 * 1024 * 1024
        ),
    )(
        owner_slot[None, :],
        owner_slot,
        fresh_len,
        cache_fill,
        queries,
        new_kv,
        cache_kv[0],
        fresh_kv,
        out_weight.T,
    )
    return out.reshape(STEPS, n_tracks, width).transpose(1, 0, 2)


def solution(mesh):
    in_specs = (
        P("stream", None, "head"),
        P("stream", None, "head"),
        P("stream", None, "head"),
        P("stream"),
        P(None, "stream", "head"),
        P(),
        P(),
        P("head", "stream"),
    )
    out_specs = P(None, None, "stream")
    return jax.shard_map(shards, mesh=mesh, in_specs=in_specs, out_specs=out_specs, check_vma=False)
```

```python
import functools

import jax
import jax.numpy as jnp
from jax import lax
from jax.experimental import pallas as pl
from jax.experimental.pallas import tpu as pltpu
from jax.sharding import PartitionSpec as P

D_HEAD = 128
GROUP = 8
STEPS = 3
ROWS = STEPS * GROUP
PAD = 32
CBLK = 512
SIDE = 8
HALF = 4
BAND = HALF * ROWS
PIECE = BAND + 16
NONE = -1e30
SCALE = D_HEAD**-0.5
FAR_FIRST = (4, 3, 5, 2, 6, 1, 7)
HEAD_ORDER = (4, 5, 2, 3, 6, 7, 1)
MESH = pl.DeviceIdType.MESH


def remote(src, dst, send_sem, recv_sem, device):
    return pltpu.make_async_remote_copy(
        src_ref=src,
        dst_ref=dst,
        send_sem=send_sem,
        recv_sem=recv_sem,
        device_id=device,
        device_id_type=MESH,
    )


def attend(query_rows, keys, values, valid):
    scores = (
        lax.dot_general(
            query_rows, keys, (((1,), (1,)), ((), ())), preferred_element_type=jnp.float32
        )
        * SCALE
    )
    highest = jnp.max(jnp.where(valid, scores, NONE), axis=1, keepdims=True)
    weights = jnp.where(valid, jnp.exp(scores - highest), 0.0)
    total = jnp.sum(weights, axis=1, keepdims=True)
    output = jnp.dot(weights.astype(jnp.bfloat16), values, preferred_element_type=jnp.float32)
    return highest, total, output


def merge(parts):
    top = functools.reduce(jnp.maximum, [part[0] for part in parts])
    factors = [jnp.exp(part[0] - top) for part in parts]
    total = sum(f * part[1] for f, part in zip(factors, parts))
    output = sum(f * part[2] for f, part in zip(factors, parts))
    return top, total, output


def kernel(
    fill_ref,
    owner_hbm,
    len_hbm,
    query_hbm,
    new_hbm,
    cache_hbm,
    fresh_hbm,
    weight_hbm,
    out_ref,
    owner_row_ref,
    len_ref,
    query_ref,
    new_ref,
    cache,
    fresh,
    weight,
    table,
    table_smem,
    query_f32,
    query_all,
    send_kv,
    recv_kv,
    cache_out,
    cache_log,
    pieces,
    gathered,
    stage,
    ordered,
    sums,
    local_sem,
    q_send,
    q_recv,
    kv_send,
    kv_recv,
    o_send,
    o_recv,
    g_send,
    g_recv,
    s_send,
    s_recv,
):
    stream = lax.axis_index("stream")
    head = lax.axis_index("head")
    z, y = stream // SIDE, stream % SIDE
    n_heads = 8
    me = (z, y)

    def at(zz, yy):
        return {"stream": lax.rem(zz, SIDE) * SIDE + lax.rem(yy, SIDE)}

    def along(axis, step):
        return at(z + step, y) if axis == 0 else at(z, y + step)

    def head_peer(step):
        return {"head": lax.rem(head + step, n_heads)}

    any_peer = head_peer(1)

    load_owner = pltpu.make_async_copy(owner_hbm, owner_row_ref, local_sem.at[0])
    load_owner.start()
    barrier = pltpu.get_barrier_semaphore()
    peers = [along(axis, step) for step in FAR_FIRST for axis in (0, 1)]
    peers += [head_peer(step) for step in range(1, n_heads)]
    for peer in peers:
        pl.semaphore_signal(barrier, inc=1, device_id=peer, device_id_type=MESH)

    loads = [
        pltpu.make_async_copy(src, dst, local_sem.at[1 + n])
        for n, (src, dst) in enumerate(
            (
                (fresh_hbm, fresh),
                (query_hbm, query_ref),
                (new_hbm, new_ref),
                (cache_hbm, cache),
                (len_hbm, len_ref),
                (weight_hbm, weight.at[pl.ds(0, weight_hbm.shape[0])]),
            )
        )
    ]
    for load in loads:
        load.start()
    load_fresh, load_query, load_new, load_cache, load_len, load_weight = loads

    n_tracks = owner_row_ref.shape[1]
    load_owner.wait()
    owner = owner_row_ref[...]
    slot_of = lax.broadcasted_iota(jnp.int32, (n_tracks, n_tracks), 0)
    lane_of = lax.broadcasted_iota(jnp.int32, (n_tracks, n_tracks), 1)
    track_column = jnp.max(jnp.where(owner == slot_of, lane_of, 0), axis=1, keepdims=True)
    track_row = jnp.max(jnp.where(slot_of == lane_of, track_column, 0), axis=0, keepdims=True)
    owner_z, owner_y = owner // SIDE, owner % SIDE
    place_row = jnp.where(
        (owner_z + owner_y) % 2 == 0,
        owner_z * HALF + owner_y // 2,
        SIDE * HALF + owner_y * HALF + owner_z // 2,
    )
    table[...] = jnp.zeros_like(table)
    table[0:1, 0:n_tracks] = track_row
    table[1:2, 0:n_tracks] = place_row
    load_table = pltpu.make_async_copy(table, table_smem, local_sem.at[7])
    load_table.start()

    query_f32[...] = jnp.zeros_like(query_f32)
    load_query.wait()
    query_flat = query_ref[0].astype(jnp.float32)
    for g in range(GROUP):
        query_f32[pl.ds(g, STEPS, stride=GROUP), :] = query_flat[
            :, g * D_HEAD : (g + 1) * D_HEAD
        ]
    parity = (z + y) % 2
    mine = jnp.where(parity == 0, y // 2, HALF + z // 2)
    my_query = query_f32[...].astype(jnp.bfloat16)
    query_all[mine] = my_query
    width = weight_hbm.shape[0]
    weight[width:] = jnp.zeros((weight.shape[0] - width, weight.shape[1]), weight.dtype)

    load_table.wait()
    load_fresh.wait()

    def slot_at(kind, place, i):
        if kind == 0:
            return place * SIDE + 2 * i + place % 2
        return (2 * i + 1 - place % 2) * SIDE + place

    for kind in (0, 1):
        for place in range(SIDE):
            for i in range(HALF):
                send_kv[kind, place, i] = fresh[table_smem[0, slot_at(kind, place, i)]]
    for kind in (0, 1):
        recv_kv[kind, me[kind]] = send_kv[kind, me[kind]]

    pl.semaphore_wait(barrier, len(peers))

    q_copies = []
    for n, step in enumerate(FAR_FIRST):
        peer = at(z + step * parity, y + step * (1 - parity))
        q_copies.append(
            remote(query_all.at[mine], query_all.at[mine], q_send.at[n], q_recv.at[mine], peer)
        )
        q_copies[-1].start()
    kv_copies = []
    for n, step in enumerate(FAR_FIRST):
        for kind in (0, 1):
            there = lax.rem(me[kind] + step, SIDE)
            kv_copies.append(
                remote(
                    send_kv.at[kind, there],
                    recv_kv.at[kind, me[kind]],
                    kv_send.at[kind, n],
                    kv_recv.at[kind, me[kind]],
                    along(kind, step),
                )
            )
            kv_copies[-1].start()

    load_cache.wait()
    load_new.wait()
    load_len.wait()
    parts = []
    fill = fill_ref[0]
    for block in range(cache.shape[0] // CBLK):
        rows = pl.ds(block * CBLK, CBLK)
        position = block * CBLK + lax.broadcasted_iota(jnp.int32, (PAD, CBLK), 1)
        parts.append(
            attend(my_query, cache[rows, :D_HEAD], cache[rows, D_HEAD:], position < fill)
        )
    query_full = query_f32[...]
    new_rows = new_ref[0].astype(jnp.float32)
    step_of_row = lax.broadcasted_iota(jnp.int32, (PAD, 1), 0) // GROUP
    new_scores = [
        jnp.where(
            u <= step_of_row,
            jnp.sum(query_full * new_rows[u : u + 1, :D_HEAD], axis=1, keepdims=True) * SCALE,
            NONE,
        )
        for u in range(STEPS)
    ]
    new_top = functools.reduce(jnp.maximum, new_scores)
    new_weights = [
        jnp.where(u <= step_of_row, jnp.exp(new_scores[u] - new_top), 0.0) for u in range(STEPS)
    ]
    new_output = sum(
        new_weights[u].astype(jnp.bfloat16).astype(jnp.float32) * new_rows[u : u + 1, D_HEAD:]
        for u in range(STEPS)
    )
    parts.append((new_top, sum(new_weights), new_output))
    top, total, output = merge(parts)
    row_id = lax.broadcasted_iota(jnp.int32, (PAD, D_HEAD), 0)
    lane_id = lax.broadcasted_iota(jnp.int32, (PAD, D_HEAD), 1)
    index_of_mine = lax.rem(mine, HALF)
    own_lane = lane_id == row_id + index_of_mine * PAD
    cache_out[...] = output / total
    own_log = jnp.sum(
        jnp.where(own_lane, top + jnp.log(total), 0.0), axis=0, keepdims=True
    )
    own_lanes = lane_id[:1] // PAD == index_of_mine
    for kind in (0, 1):
        cache_log[kind : kind + 1] = jnp.where(
            jnp.logical_and(own_lanes, parity == kind), own_log, NONE
        )

    for n in range(2 * HALF - 1):
        if n < HALF - 1:
            came = parity * HALF + lax.rem(index_of_mine + 1 + n, HALF)
        else:
            came = (1 - parity) * HALF + n - (HALF - 1)
        remote(
            query_all.at[came], query_all.at[came], q_send.at[n], q_recv.at[came], any_peer
        ).wait_recv()
    for step in FAR_FIRST[::-1]:
        for kind in (0, 1):
            there = lax.rem(me[kind] + step, SIDE)
            remote(
                send_kv.at[kind, there],
                recv_kv.at[kind, there],
                kv_send.at[kind, 0],
                kv_recv.at[kind, there],
                any_peer,
            ).wait_recv()

    span = SIDE * 16
    position_id = lax.broadcasted_iota(jnp.int32, (span, D_HEAD), 0)
    positions = (
        (position_id // 16) * span + y * 16 + position_id % 16,
        z * span + position_id,
    )
    lane_slot = lax.broadcasted_iota(jnp.int32, (1, D_HEAD), 1) // PAD
    row8 = lax.broadcasted_iota(jnp.int32, (16, D_HEAD), 0)
    results = []
    own_shares = []
    for kind in (0, 1):
        lengths = jnp.zeros((1, D_HEAD), jnp.int32)
        for i in range(HALF):
            if kind == 0:
                slot = z * SIDE + 2 * i + z % 2
            else:
                slot = (2 * i + 1 - y % 2) * SIDE + y
            lengths = jnp.where(lane_slot == i, len_ref[table_smem[0, slot]], lengths)
        queries = query_all[kind * HALF : (kind + 1) * HALF].reshape(HALF * PAD, D_HEAD)
        every = lax.dot_general(
            recv_kv[kind, :, :, :, :D_HEAD].reshape(HALF * span, D_HEAD),
            queries,
            (((1,), (1,)), ((), ())),
            preferred_element_type=jnp.float32,
        ).reshape(SIDE, HALF, 16, D_HEAD)
        scores = every[:, 0]
        for i in range(1, HALF):
            scores = jnp.where(lane_slot[None] == i, every[:, i], scores)
        scores = scores.reshape(span, D_HEAD) * SCALE
        valid = positions[kind] < lengths
        own = cache_log[kind : kind + 1]
        top = jnp.maximum(
            jnp.max(jnp.where(valid, scores, NONE), axis=0, keepdims=True), own
        )
        weights = jnp.where(valid, jnp.exp(scores - top), 0.0)
        own_weight = jnp.exp(own - top)
        total = jnp.sum(weights, axis=0, keepdims=True) + own_weight
        share = 1.0 / total
        own_shares.append(own_weight * share)
        shares = (weights * share).T.astype(jnp.bfloat16)
        outputs = [
            jnp.dot(
                shares[i * PAD : (i + 1) * PAD],
                recv_kv[kind, :, i, :, D_HEAD:].reshape(span, D_HEAD),
                preferred_element_type=jnp.float32,
            )[:ROWS]
            for i in range(HALF)
        ]
        line = top + jnp.log(total)
        first = line.astype(jnp.bfloat16).astype(jnp.float32)
        second = (line - first).astype(jnp.bfloat16).astype(jnp.float32)
        third = line - first - second
        lines = jnp.where(
            row8 == 0,
            first,
            jnp.where(row8 == 1, second, jnp.where(row8 == 2, third, 0.0)),
        )
        results.append((outputs, lines))
    own_share = jnp.where(parity == 0, own_shares[0], own_shares[1])
    own_column = jnp.sum(jnp.where(own_lane, own_share, 0.0), axis=1, keepdims=True)
    own_part = (own_column * cache_out[...])[:ROWS]
    for kind in (0, 1):
        outputs, lines = results[kind]
        pieces[kind, me[1 - kind]] = jnp.concatenate(
            [
                jnp.where(mine == kind * HALF + i, own_part, 0.0) + outputs[i]
                for i in range(HALF)
            ]
            + [lines],
            axis=0,
        ).astype(jnp.bfloat16)

    o_copies = []
    for n, step in enumerate(FAR_FIRST):
        for kind in (0, 1):
            mine_here = me[1 - kind]
            o_copies.append(
                remote(
                    pieces.at[kind, mine_here],
                    pieces.at[kind, mine_here],
                    o_send.at[kind, n],
                    o_recv.at[kind, mine_here],
                    along(1 - kind, step),
                )
            )
            o_copies[-1].start()
    for step in FAR_FIRST[::-1]:
        for kind in (0, 1):
            there = lax.rem(me[1 - kind] + step, SIDE)
            remote(
                pieces.at[kind, there],
                pieces.at[kind, there],
                o_send.at[kind, 0],
                o_recv.at[kind, there],
                any_peer,
            ).wait_recv()

    for kind in (0, 1):
        arrived = [pieces[kind, src].astype(jnp.float32) for src in range(SIDE)]
        logs = jnp.concatenate(
            [jnp.sum(a[BAND:], axis=0, keepdims=True) for a in arrived], axis=0
        )
        weights = jnp.exp(logs - jnp.max(logs, axis=0, keepdims=True))
        weights = weights / jnp.sum(weights, axis=0, keepdims=True)
        columns = jnp.concatenate(
            [weights, jnp.zeros((D_HEAD - SIDE, D_HEAD), jnp.float32)], axis=0
        ).T
        rows = []
        for i in range(HALF):
            acc = None
            for src in range(SIDE):
                term = (
                    columns[i * PAD : i * PAD + ROWS, src : src + 1]
                    * arrived[src][i * ROWS : (i + 1) * ROWS]
                )
                acc = term if acc is None else acc + term
            rows.append(acc)
        gathered[kind, me[kind]] = jnp.concatenate(rows, axis=0).astype(jnp.bfloat16)

    g_copies = []
    for n, step in enumerate(FAR_FIRST):
        for kind in (0, 1):
            g_copies.append(
                remote(
                    gathered.at[kind, me[kind]],
                    gathered.at[kind, me[kind]],
                    g_send.at[kind, n],
                    g_recv.at[kind, me[kind]],
                    along(kind, step),
                )
            )
            g_copies[-1].start()
    load_weight.wait()
    for step in (0,) + FAR_FIRST[::-1]:
        for kind in (0, 1):
            there = lax.rem(me[kind] + step, SIDE)
            if step:
                remote(
                    gathered.at[kind, there],
                    gathered.at[kind, there],
                    g_send.at[kind, 0],
                    g_recv.at[kind, there],
                    any_peer,
                ).wait_recv()
            stage[pl.ds((kind * SIDE + there) * HALF, HALF)] = (
                gathered[kind, there].astype(jnp.float32).reshape(HALF, ROWS, D_HEAD)
            )

    for track in range(n_tracks):
        rows = stage[table_smem[1, track]]
        for t in range(STEPS):
            ordered[pl.ds((t * n_tracks + track) * GROUP, GROUP), :] = rows[
                t * GROUP : (t + 1) * GROUP
            ]
    product = None
    for g in range(GROUP):
        left = ordered[pl.ds(g, n_tracks * STEPS, stride=GROUP), :].astype(jnp.bfloat16)
        term = lax.dot_general(
            left,
            weight[:, g * D_HEAD : (g + 1) * D_HEAD],
            (((1,), (1,)), ((), ())),
            preferred_element_type=jnp.float32,
        )
        product = term if product is None else product + term
    parts = [product[t * n_tracks : (t + 1) * n_tracks] for t in range(STEPS)]
    lane = lax.broadcasted_iota(jnp.int32, (n_tracks, 128), 1)
    middle = pltpu.roll(parts[1], width, 1)
    last = pltpu.roll(parts[2], 2 * width - 128, 1)
    sums[head, :, :128] = jnp.where(lane < width, parts[0], middle).astype(jnp.bfloat16)
    sums[head, :, 128:] = jnp.where(lane < 2 * width - 128, middle, last).astype(jnp.bfloat16)

    s_copies = []
    for n, step in enumerate(HEAD_ORDER):
        s_copies.append(
            remote(sums.at[head], sums.at[head], s_send.at[n], s_recv.at[head], head_peer(step))
        )
        s_copies[-1].start()
    for step in HEAD_ORDER[::-1]:
        there = lax.rem(head + step, n_heads)
        remote(
            sums.at[there], sums.at[there], s_send.at[0], s_recv.at[there], any_peer
        ).wait_recv()
    summed = sums[0].astype(jnp.float32)
    for there in range(1, n_heads):
        summed = summed + sums[there].astype(jnp.float32)
    left, right = summed[:, :128], summed[:, 128:]
    split = 128 - width
    middle = jnp.where(lane < split, pltpu.roll(left, split, 1), pltpu.roll(right, split, 1))
    last = pltpu.roll(right, 256 - 2 * width, 1)
    for t, rows in enumerate((left, middle, last)):
        out_ref[t * n_tracks : (t + 1) * n_tracks] = rows[:, :width].astype(out_ref.dtype)

    for copy in q_copies + kv_copies + o_copies + g_copies + s_copies:
        copy.wait_send()


def shards(queries, new_kv, cache_kv, cache_fill, fresh_kv, fresh_len, owner_slot, out_weight):
    n_tracks, depth = fresh_kv.shape[0], fresh_kv.shape[1]
    width = out_weight.shape[1]
    vmem = pl.BlockSpec(memory_space=pltpu.VMEM)
    hbm = pl.BlockSpec(memory_space=pltpu.HBM)
    bf16, f32 = jnp.bfloat16, jnp.float32
    dma = pltpu.SemaphoreType.DMA
    out = pl.pallas_call(
        kernel,
        name="handoff_decode",
        out_shape=pltpu.VMEM((n_tracks * STEPS, width), bf16),
        in_specs=[pl.BlockSpec(memory_space=pltpu.SMEM)] + [hbm] * 7,
        out_specs=vmem,
        scratch_shapes=[
            pltpu.VMEM((1, n_tracks), jnp.int32),
            pltpu.SMEM((n_tracks,), jnp.int32),
            pltpu.VMEM(queries.shape, bf16),
            pltpu.VMEM(new_kv.shape, bf16),
            pltpu.VMEM(cache_kv.shape[1:], bf16),
            pltpu.VMEM(fresh_kv.shape, bf16),
            pltpu.VMEM((128, out_weight.shape[0]), bf16),
            pltpu.VMEM((8, 128), jnp.int32),
            pltpu.SMEM((8, 128), jnp.int32),
            pltpu.VMEM((PAD, D_HEAD), f32),
            pltpu.VMEM((2 * HALF, PAD, D_HEAD), bf16),
            pltpu.VMEM((2, SIDE, HALF, depth, 2 * D_HEAD), bf16),
            pltpu.VMEM((2, SIDE, HALF, depth, 2 * D_HEAD), bf16),
            pltpu.VMEM((PAD, D_HEAD), f32),
            pltpu.VMEM((8, D_HEAD), f32),
            pltpu.VMEM((2, SIDE, PIECE, D_HEAD), bf16),
            pltpu.VMEM((2, SIDE, HALF * ROWS, D_HEAD), bf16),
            pltpu.VMEM((n_tracks, ROWS, D_HEAD), f32),
            pltpu.VMEM((n_tracks * ROWS, D_HEAD), f32),
            pltpu.VMEM((8, n_tracks, 256), bf16),
            dma((8,)),
            dma((SIDE - 1,)),
            dma((2 * HALF,)),
            dma((2, SIDE - 1)),
            dma((2, SIDE)),
            dma((2, SIDE - 1)),
            dma((2, SIDE)),
            dma((2, SIDE - 1)),
            dma((2, SIDE)),
            dma((7,)),
            dma((8,)),
        ],
        compiler_params=pltpu.CompilerParams(
            collective_id=0, has_side_effects=True, vmem_limit_bytes=32 * 1024 * 1024
        ),
    )(
        cache_fill,
        *(
            pltpu.with_memory_space_constraint(operand, pltpu.HBM)
            for operand in (
                owner_slot[None, :],
                fresh_len,
                queries,
                new_kv,
                cache_kv[0],
                fresh_kv,
                out_weight.T,
            )
        )
    )
    return out.reshape(STEPS, n_tracks, width).transpose(1, 0, 2)


def solution(mesh):
    in_specs = (
        P("stream", None, "head"),
        P("stream", None, "head"),
        P("stream", None, "head"),
        P("stream"),
        P(None, "stream", "head"),
        P(),
        P(),
        P("head", "stream"),
    )
    out_specs = P(None, None, "stream")
    return jax.shard_map(shards, mesh=mesh, in_specs=in_specs, out_specs=out_specs, check_vma=False)
```

```python
import functools

import jax
import jax.numpy as jnp
from jax import lax
from jax.experimental import pallas as pl
from jax.experimental.pallas import tpu as pltpu
from jax.sharding import PartitionSpec as P

D_HEAD = 128
GROUP = 8
STEPS = 3
ROWS = STEPS * GROUP
PAD = 32
CBLK = 512
SIDE = 8
HALF = 4
PAIR = 2
CHUNKS = HALF // PAIR
BAND = PAIR * ROWS
PIECE = BAND + 16
NONE = -1e30
SCALE = D_HEAD**-0.5
FAR_FIRST = (4, 3, 5, 2, 6, 1, 7)
HEAD_ORDER = (4, 5, 2, 3, 6, 7, 1)
MESH = pl.DeviceIdType.MESH


def remote(src, dst, send_sem, recv_sem, device):
    return pltpu.make_async_remote_copy(
        src_ref=src,
        dst_ref=dst,
        send_sem=send_sem,
        recv_sem=recv_sem,
        device_id=device,
        device_id_type=MESH,
    )


def attend(query_rows, keys, values, valid):
    scores = (
        lax.dot_general(
            query_rows, keys, (((1,), (1,)), ((), ())), preferred_element_type=jnp.float32
        )
        * SCALE
    )
    highest = jnp.max(jnp.where(valid, scores, NONE), axis=1, keepdims=True)
    weights = jnp.where(valid, jnp.exp(scores - highest), 0.0)
    total = jnp.sum(weights, axis=1, keepdims=True)
    output = jnp.dot(weights.astype(jnp.bfloat16), values, preferred_element_type=jnp.float32)
    return highest, total, output


def merge(parts):
    top = functools.reduce(jnp.maximum, [part[0] for part in parts])
    factors = [jnp.exp(part[0] - top) for part in parts]
    total = sum(f * part[1] for f, part in zip(factors, parts))
    output = sum(f * part[2] for f, part in zip(factors, parts))
    return top, total, output


def kernel(
    fill_ref,
    owner_hbm,
    len_hbm,
    query_hbm,
    new_hbm,
    cache_hbm,
    fresh_hbm,
    weight_hbm,
    out_ref,
    owner_row_ref,
    len_ref,
    query_ref,
    new_ref,
    cache,
    fresh,
    weight,
    table,
    table_smem,
    query_f32,
    query_all,
    send_kv,
    recv_kv,
    cache_out,
    cache_log,
    pieces,
    gathered,
    stage,
    ordered,
    sums,
    local_sem,
    q_send,
    q_recv,
    kv_send,
    kv_recv,
    o_send,
    o_recv,
    g_send,
    g_recv,
    s_send,
    s_recv,
):
    stream = lax.axis_index("stream")
    head = lax.axis_index("head")
    z, y = stream // SIDE, stream % SIDE
    n_heads = 8
    me = (z, y)

    def at(zz, yy):
        return {"stream": lax.rem(zz, SIDE) * SIDE + lax.rem(yy, SIDE)}

    def along(axis, step):
        return at(z + step, y) if axis == 0 else at(z, y + step)

    def head_peer(step):
        return {"head": lax.rem(head + step, n_heads)}

    any_peer = head_peer(1)

    load_owner = pltpu.make_async_copy(owner_hbm, owner_row_ref, local_sem.at[0])
    load_owner.start()
    barrier = pltpu.get_barrier_semaphore()
    peers = [along(axis, step) for step in FAR_FIRST for axis in (0, 1)]
    peers += [head_peer(step) for step in range(1, n_heads)]
    for peer in peers:
        pl.semaphore_signal(barrier, inc=1, device_id=peer, device_id_type=MESH)

    loads = [
        pltpu.make_async_copy(src, dst, local_sem.at[1 + n])
        for n, (src, dst) in enumerate(
            (
                (fresh_hbm, fresh),
                (query_hbm, query_ref),
                (new_hbm, new_ref),
                (cache_hbm, cache),
                (len_hbm, len_ref),
                (weight_hbm, weight.at[pl.ds(0, weight_hbm.shape[0])]),
            )
        )
    ]
    for load in loads:
        load.start()
    load_fresh, load_query, load_new, load_cache, load_len, load_weight = loads

    n_tracks = owner_row_ref.shape[1]
    load_owner.wait()
    owner = owner_row_ref[...]
    slot_of = lax.broadcasted_iota(jnp.int32, (n_tracks, n_tracks), 0)
    lane_of = lax.broadcasted_iota(jnp.int32, (n_tracks, n_tracks), 1)
    track_column = jnp.max(jnp.where(owner == slot_of, lane_of, 0), axis=1, keepdims=True)
    track_row = jnp.max(jnp.where(slot_of == lane_of, track_column, 0), axis=0, keepdims=True)
    owner_z, owner_y = owner // SIDE, owner % SIDE
    place_row = jnp.where(
        (owner_z + owner_y) % 2 == 0,
        owner_y // 4 * 32 + owner_z * PAIR + owner_y // 2 % PAIR,
        owner_z // 4 * 32 + 16 + owner_y * PAIR + owner_z // 2 % PAIR,
    )
    table[...] = jnp.zeros_like(table)
    table[0:1, 0:n_tracks] = track_row
    table[1:2, 0:n_tracks] = place_row
    load_table = pltpu.make_async_copy(table, table_smem, local_sem.at[7])
    load_table.start()

    query_f32[...] = jnp.zeros_like(query_f32)
    load_query.wait()
    query_flat = query_ref[0].astype(jnp.float32)
    for g in range(GROUP):
        query_f32[pl.ds(g, STEPS, stride=GROUP), :] = query_flat[
            :, g * D_HEAD : (g + 1) * D_HEAD
        ]
    parity = (z + y) % 2
    my_index = jnp.where(parity == 0, y // 2, z // 2)
    my_chunk, my_group = my_index // PAIR, parity * PAIR + my_index % PAIR
    mine = my_chunk * 2 * PAIR + my_group
    my_query = query_f32[...].astype(jnp.bfloat16)
    query_all[mine] = my_query
    width = weight_hbm.shape[0]
    weight[width:] = jnp.zeros((weight.shape[0] - width, weight.shape[1]), weight.dtype)

    load_table.wait()
    load_fresh.wait()

    def slot_at(kind, place, i):
        if kind == 0:
            return place * SIDE + 2 * i + place % 2
        return (2 * i + 1 - place % 2) * SIDE + place

    for chunk in range(CHUNKS):
        for kind in (0, 1):
            for place in range(SIDE):
                for j in range(PAIR):
                    slot = slot_at(kind, place, chunk * PAIR + j)
                    send_kv[chunk, kind, place, j] = fresh[table_smem[0, slot]]
    for chunk in range(CHUNKS):
        for kind in (0, 1):
            recv_kv[chunk, kind, me[kind]] = send_kv[chunk, kind, me[kind]]

    pl.semaphore_wait(barrier, len(peers))

    q_copies = []
    for n, step in enumerate(FAR_FIRST):
        peer = at(z + step * parity, y + step * (1 - parity))
        q_copies.append(
            remote(query_all.at[mine], query_all.at[mine], q_send.at[n], q_recv.at[mine], peer)
        )
        q_copies[-1].start()
    def spread(buffer, source, chunk, send_sems, recv_sems, turn):
        copies = []
        for n, step in enumerate(FAR_FIRST):
            for kind in (0, 1):
                axis = kind ^ turn
                here = me[axis]
                from_ref = (
                    buffer.at[chunk, kind, here]
                    if source is None
                    else source.at[chunk, kind, lax.rem(here + step, SIDE)]
                )
                copies.append(
                    remote(
                        from_ref,
                        buffer.at[chunk, kind, here],
                        send_sems.at[chunk, kind, n],
                        recv_sems.at[chunk, kind, here],
                        along(axis, step),
                    )
                )
                copies[-1].start()
        return copies

    def arrival(buffer, chunk, kind, there, send_sems, recv_sems):
        block = buffer.at[chunk, kind, there]
        remote(
            block, block, send_sems.at[chunk, kind, 0], recv_sems.at[chunk, kind, there], any_peer
        ).wait_recv()

    def collect(buffer, chunk, send_sems, recv_sems, turn):
        for step in FAR_FIRST[::-1]:
            for kind in (0, 1):
                there = lax.rem(me[kind ^ turn] + step, SIDE)
                arrival(buffer, chunk, kind, there, send_sems, recv_sems)

    kv_copies = []
    for chunk in range(CHUNKS):
        kv_copies += spread(recv_kv, send_kv, chunk, kv_send, kv_recv, 0)

    load_cache.wait()
    load_new.wait()
    load_len.wait()
    parts = []
    fill = fill_ref[0]
    for block in range(cache.shape[0] // CBLK):
        rows = pl.ds(block * CBLK, CBLK)
        position = block * CBLK + lax.broadcasted_iota(jnp.int32, (PAD, CBLK), 1)
        parts.append(
            attend(my_query, cache[rows, :D_HEAD], cache[rows, D_HEAD:], position < fill)
        )
    query_full = query_f32[...]
    new_rows = new_ref[0].astype(jnp.float32)
    step_of_row = lax.broadcasted_iota(jnp.int32, (PAD, 1), 0) // GROUP
    new_scores = [
        jnp.where(
            u <= step_of_row,
            jnp.sum(query_full * new_rows[u : u + 1, :D_HEAD], axis=1, keepdims=True) * SCALE,
            NONE,
        )
        for u in range(STEPS)
    ]
    new_top = functools.reduce(jnp.maximum, new_scores)
    new_weights = [
        jnp.where(u <= step_of_row, jnp.exp(new_scores[u] - new_top), 0.0) for u in range(STEPS)
    ]
    new_output = sum(
        new_weights[u].astype(jnp.bfloat16).astype(jnp.float32) * new_rows[u : u + 1, D_HEAD:]
        for u in range(STEPS)
    )
    parts.append((new_top, sum(new_weights), new_output))
    top, total, output = merge(parts)
    row_id = lax.broadcasted_iota(jnp.int32, (PAD, D_HEAD), 0)
    lane_id = lax.broadcasted_iota(jnp.int32, (PAD, D_HEAD), 1)
    own_lane = lane_id == row_id + my_group * PAD
    cache_out[...] = output / total
    own_log = jnp.sum(
        jnp.where(own_lane, top + jnp.log(total), 0.0), axis=0, keepdims=True
    )
    own_lanes = lane_id[:1] // PAD == my_group
    for chunk in range(CHUNKS):
        cache_log[chunk : chunk + 1] = jnp.where(
            jnp.logical_and(own_lanes, my_chunk == chunk), own_log, NONE
        )

    for n in range(2 * HALF - 1):
        came = lax.rem(mine + 1 + n, 2 * HALF)
        remote(
            query_all.at[came], query_all.at[came], q_send.at[n], q_recv.at[came], any_peer
        ).wait_recv()

    span = SIDE * 16
    position_id = lax.broadcasted_iota(jnp.int32, (span, D_HEAD), 0)
    lane_group = lax.broadcasted_iota(jnp.int32, (1, D_HEAD), 1) // PAD
    positions = jnp.where(
        lane_group < PAIR,
        (position_id // 16) * span + y * 16 + position_id % 16,
        z * span + position_id,
    )
    row16 = lax.broadcasted_iota(jnp.int32, (16, D_HEAD), 0)
    groups = [(kind, j) for kind in (0, 1) for j in range(PAIR)]
    o_copies = []
    for chunk in range(CHUNKS):
        lengths = jnp.zeros((1, D_HEAD), jnp.int32)
        for n, (kind, j) in enumerate(groups):
            i = chunk * PAIR + j
            if kind == 0:
                slot = z * SIDE + 2 * i + z % 2
            else:
                slot = (2 * i + 1 - y % 2) * SIDE + y
            lengths = jnp.where(lane_group == n, len_ref[table_smem[0, slot]], lengths)
        valid = positions < lengths
        collect(recv_kv, chunk, kv_send, kv_recv, 0)
        every = lax.dot_general(
            recv_kv[chunk, :, :, :, :, :D_HEAD].reshape(2 * PAIR * span, D_HEAD),
            query_all[chunk * 2 * PAIR : (chunk + 1) * 2 * PAIR].reshape(D_HEAD, D_HEAD),
            (((1,), (1,)), ((), ())),
            preferred_element_type=jnp.float32,
        ).reshape(2, SIDE, PAIR, 16, D_HEAD)
        scores = every[0, :, 0]
        for n, (kind, j) in enumerate(groups[1:]):
            scores = jnp.where(lane_group[None] == n + 1, every[kind, :, j], scores)
        scores = scores.reshape(span, D_HEAD) * SCALE
        own = cache_log[chunk : chunk + 1]
        top = jnp.maximum(
            jnp.max(jnp.where(valid, scores, NONE), axis=0, keepdims=True), own
        )
        weights = jnp.where(valid, jnp.exp(scores - top), 0.0)
        own_weight = jnp.exp(own - top)
        total = jnp.sum(weights, axis=0, keepdims=True) + own_weight
        share = 1.0 / total
        shares = (weights * share).T.astype(jnp.bfloat16)
        outputs = [
            jnp.dot(
                shares[n * PAD : (n + 1) * PAD],
                recv_kv[chunk, kind, :, j, :, D_HEAD:].reshape(span, D_HEAD),
                preferred_element_type=jnp.float32,
            )[:ROWS]
            for n, (kind, j) in enumerate(groups)
        ]
        own_column = jnp.sum(
            jnp.where(own_lane, own_weight * share, 0.0), axis=1, keepdims=True
        )
        own_part = (own_column * cache_out[...])[:ROWS]
        outputs = [
            output + jnp.where(mine == chunk * 2 * PAIR + n, own_part, 0.0)
            for n, output in enumerate(outputs)
        ]
        line = top + jnp.log(total)
        first = line.astype(jnp.bfloat16).astype(jnp.float32)
        second = (line - first).astype(jnp.bfloat16).astype(jnp.float32)
        third = line - first - second
        lines = jnp.where(
            row16 == 0,
            first,
            jnp.where(row16 == 1, second, jnp.where(row16 == 2, third, 0.0)),
        )
        for kind in (0, 1):
            pieces[chunk, kind, me[1 - kind]] = jnp.concatenate(
                outputs[kind * PAIR : (kind + 1) * PAIR] + [lines], axis=0
            ).astype(jnp.bfloat16)
        o_copies += spread(pieces, None, chunk, o_send, o_recv, 1)

    g_copies = []
    for chunk in range(CHUNKS):
        collect(pieces, chunk, o_send, o_recv, 1)
        arrived = [
            [pieces[chunk, kind, src].astype(jnp.float32) for src in range(SIDE)]
            for kind in (0, 1)
        ]
        logs = [
            jnp.concatenate([jnp.sum(a[BAND:], axis=0, keepdims=True) for a in some], axis=0)
            for some in arrived
        ]
        logs = jnp.where(lane_group < PAIR, logs[0], logs[1])
        weights = jnp.exp(logs - jnp.max(logs, axis=0, keepdims=True))
        weights = weights / jnp.sum(weights, axis=0, keepdims=True)
        columns = jnp.concatenate(
            [weights, jnp.zeros((D_HEAD - SIDE, D_HEAD), jnp.float32)], axis=0
        ).T
        rows = []
        for n, (kind, j) in enumerate(groups):
            acc = None
            for src in range(SIDE):
                term = (
                    columns[n * PAD : n * PAD + ROWS, src : src + 1]
                    * arrived[kind][src][j * ROWS : (j + 1) * ROWS]
                )
                acc = term if acc is None else acc + term
            rows.append(acc)
        for kind in (0, 1):
            gathered[chunk, kind, me[kind]] = jnp.concatenate(
                rows[kind * PAIR : (kind + 1) * PAIR], axis=0
            ).astype(jnp.bfloat16)
        g_copies += spread(gathered, None, chunk, g_send, g_recv, 0)

    load_weight.wait()
    for chunk in range(CHUNKS):
        for step in (0,) + FAR_FIRST[::-1]:
            for kind in (0, 1):
                there = lax.rem(me[kind] + step, SIDE)
                if step:
                    arrival(gathered, chunk, kind, there, g_send, g_recv)
                place = ((chunk * 2 + kind) * SIDE + there) * PAIR
                stage[pl.ds(place, PAIR)] = (
                    gathered[chunk, kind, there].astype(jnp.float32).reshape(PAIR, ROWS, D_HEAD)
                )

    for track in range(n_tracks):
        rows = stage[table_smem[1, track]]
        for t in range(STEPS):
            ordered[pl.ds((t * n_tracks + track) * GROUP, GROUP), :] = rows[
                t * GROUP : (t + 1) * GROUP
            ]
    product = None
    for g in range(GROUP):
        left = ordered[pl.ds(g, n_tracks * STEPS, stride=GROUP), :].astype(jnp.bfloat16)
        term = lax.dot_general(
            left,
            weight[:, g * D_HEAD : (g + 1) * D_HEAD],
            (((1,), (1,)), ((), ())),
            preferred_element_type=jnp.float32,
        )
        product = term if product is None else product + term
    parts = [product[t * n_tracks : (t + 1) * n_tracks] for t in range(STEPS)]
    lane = lax.broadcasted_iota(jnp.int32, (n_tracks, 128), 1)
    middle = pltpu.roll(parts[1], width, 1)
    last = pltpu.roll(parts[2], 2 * width - 128, 1)
    sums[head, :, :128] = jnp.where(lane < width, parts[0], middle).astype(jnp.bfloat16)
    sums[head, :, 128:] = jnp.where(lane < 2 * width - 128, middle, last).astype(jnp.bfloat16)

    s_copies = []
    for n, step in enumerate(HEAD_ORDER):
        s_copies.append(
            remote(sums.at[head], sums.at[head], s_send.at[n], s_recv.at[head], head_peer(step))
        )
        s_copies[-1].start()
    for step in HEAD_ORDER[::-1]:
        there = lax.rem(head + step, n_heads)
        remote(
            sums.at[there], sums.at[there], s_send.at[0], s_recv.at[there], any_peer
        ).wait_recv()
    summed = sums[0].astype(jnp.float32)
    for there in range(1, n_heads):
        summed = summed + sums[there].astype(jnp.float32)
    left, right = summed[:, :128], summed[:, 128:]
    split = 128 - width
    middle = jnp.where(lane < split, pltpu.roll(left, split, 1), pltpu.roll(right, split, 1))
    last = pltpu.roll(right, 256 - 2 * width, 1)
    for t, rows in enumerate((left, middle, last)):
        out_ref[t * n_tracks : (t + 1) * n_tracks] = rows[:, :width].astype(out_ref.dtype)

    for copy in q_copies + kv_copies + o_copies + g_copies + s_copies:
        copy.wait_send()


def shards(queries, new_kv, cache_kv, cache_fill, fresh_kv, fresh_len, owner_slot, out_weight):
    n_tracks, depth = fresh_kv.shape[0], fresh_kv.shape[1]
    width = out_weight.shape[1]
    vmem = pl.BlockSpec(memory_space=pltpu.VMEM)
    hbm = pl.BlockSpec(memory_space=pltpu.HBM)
    bf16, f32 = jnp.bfloat16, jnp.float32
    dma = pltpu.SemaphoreType.DMA
    out = pl.pallas_call(
        kernel,
        name="handoff_decode",
        out_shape=pltpu.VMEM((n_tracks * STEPS, width), bf16),
        in_specs=[pl.BlockSpec(memory_space=pltpu.SMEM)] + [hbm] * 7,
        out_specs=vmem,
        scratch_shapes=[
            pltpu.VMEM((1, n_tracks), jnp.int32),
            pltpu.SMEM((n_tracks,), jnp.int32),
            pltpu.VMEM(queries.shape, bf16),
            pltpu.VMEM(new_kv.shape, bf16),
            pltpu.VMEM(cache_kv.shape[1:], bf16),
            pltpu.VMEM(fresh_kv.shape, bf16),
            pltpu.VMEM((128, out_weight.shape[0]), bf16),
            pltpu.VMEM((8, 128), jnp.int32),
            pltpu.SMEM((8, 128), jnp.int32),
            pltpu.VMEM((PAD, D_HEAD), f32),
            pltpu.VMEM((2 * HALF, PAD, D_HEAD), bf16),
            pltpu.VMEM((CHUNKS, 2, SIDE, PAIR, depth, 2 * D_HEAD), bf16),
            pltpu.VMEM((CHUNKS, 2, SIDE, PAIR, depth, 2 * D_HEAD), bf16),
            pltpu.VMEM((PAD, D_HEAD), f32),
            pltpu.VMEM((8, D_HEAD), f32),
            pltpu.VMEM((CHUNKS, 2, SIDE, PIECE, D_HEAD), bf16),
            pltpu.VMEM((CHUNKS, 2, SIDE, BAND, D_HEAD), bf16),
            pltpu.VMEM((n_tracks, ROWS, D_HEAD), f32),
            pltpu.VMEM((n_tracks * ROWS, D_HEAD), f32),
            pltpu.VMEM((8, n_tracks, 256), bf16),
            dma((8,)),
            dma((SIDE - 1,)),
            dma((2 * HALF,)),
            dma((CHUNKS, 2, SIDE - 1)),
            dma((CHUNKS, 2, SIDE)),
            dma((CHUNKS, 2, SIDE - 1)),
            dma((CHUNKS, 2, SIDE)),
            dma((CHUNKS, 2, SIDE - 1)),
            dma((CHUNKS, 2, SIDE)),
            dma((7,)),
            dma((8,)),
        ],
        compiler_params=pltpu.CompilerParams(
            collective_id=0, has_side_effects=True, vmem_limit_bytes=32 * 1024 * 1024
        ),
    )(
        cache_fill,
        *(
            pltpu.with_memory_space_constraint(operand, pltpu.HBM)
            for operand in (
                owner_slot[None, :],
                fresh_len,
                queries,
                new_kv,
                cache_kv[0],
                fresh_kv,
                out_weight.T,
            )
        )
    )
    return out.reshape(STEPS, n_tracks, width).transpose(1, 0, 2)


def solution(mesh):
    in_specs = (
        P("stream", None, "head"),
        P("stream", None, "head"),
        P("stream", None, "head"),
        P("stream"),
        P(None, "stream", "head"),
        P(),
        P(),
        P("head", "stream"),
    )
    out_specs = P(None, None, "stream")
    return jax.shard_map(shards, mesh=mesh, in_specs=in_specs, out_specs=out_specs, check_vma=False)
```

```python
import functools

import jax
import jax.numpy as jnp
from jax import lax
from jax.experimental import pallas as pl
from jax.experimental.pallas import tpu as pltpu
from jax.sharding import PartitionSpec as P

D_HEAD = 128
GROUP = 8
STEPS = 3
ROWS = STEPS * GROUP
PAD = 32
CBLK = 512
SIDE = 8
HALF = 4
PAIR = 2
CHUNKS = HALF // PAIR
BAND = PAIR * ROWS
PIECE = BAND + 16
NONE = -1e30
SCALE = D_HEAD**-0.5
FAR_FIRST = (4, 3, 5, 2, 6, 1, 7)
HEAD_ORDER = (4, 5, 2, 3, 6, 7, 1)
MESH = pl.DeviceIdType.MESH


def remote(src, dst, send_sem, recv_sem, device):
    return pltpu.make_async_remote_copy(
        src_ref=src,
        dst_ref=dst,
        send_sem=send_sem,
        recv_sem=recv_sem,
        device_id=device,
        device_id_type=MESH,
    )


def attend(query_rows, keys, values, valid):
    scores = (
        lax.dot_general(
            query_rows, keys, (((1,), (1,)), ((), ())), preferred_element_type=jnp.float32
        )
        * SCALE
    )
    highest = jnp.max(jnp.where(valid, scores, NONE), axis=1, keepdims=True)
    weights = jnp.where(valid, jnp.exp(scores - highest), 0.0)
    total = jnp.sum(weights, axis=1, keepdims=True)
    output = jnp.dot(weights.astype(jnp.bfloat16), values, preferred_element_type=jnp.float32)
    return highest, total, output


def merge(parts):
    top = functools.reduce(jnp.maximum, [part[0] for part in parts])
    factors = [jnp.exp(part[0] - top) for part in parts]
    total = sum(f * part[1] for f, part in zip(factors, parts))
    output = sum(f * part[2] for f, part in zip(factors, parts))
    return top, total, output


def kernel(
    fill_ref,
    owner_hbm,
    len_hbm,
    query_hbm,
    new_hbm,
    cache_hbm,
    fresh_hbm,
    weight_hbm,
    out_ref,
    owner_row_ref,
    len_ref,
    query_ref,
    new_ref,
    cache,
    fresh,
    weight,
    table,
    table_smem,
    query_f32,
    query_all,
    send_kv,
    recv_kv,
    cache_out,
    cache_log,
    pieces,
    gathered,
    stage,
    sums,
    pick,
    local_sem,
    q_send,
    q_recv,
    kv_send,
    kv_recv,
    o_send,
    o_recv,
    g_send,
    g_recv,
    s_send,
    s_recv,
):
    stream = lax.axis_index("stream")
    head = lax.axis_index("head")
    z, y = stream // SIDE, stream % SIDE
    n_heads = 8
    me = (z, y)

    def at(zz, yy):
        return {"stream": lax.rem(zz, SIDE) * SIDE + lax.rem(yy, SIDE)}

    def along(axis, step):
        return at(z + step, y) if axis == 0 else at(z, y + step)

    def head_peer(step):
        return {"head": lax.rem(head + step, n_heads)}

    any_peer = head_peer(1)

    load_owner = pltpu.make_async_copy(owner_hbm, owner_row_ref, local_sem.at[0])
    load_owner.start()
    barrier = pltpu.get_barrier_semaphore()
    peers = [along(axis, step) for step in FAR_FIRST for axis in (0, 1)]
    peers += [head_peer(step) for step in range(1, n_heads)]
    for peer in peers:
        pl.semaphore_signal(barrier, inc=1, device_id=peer, device_id_type=MESH)

    loads = [
        pltpu.make_async_copy(src, dst, local_sem.at[1 + n])
        for n, (src, dst) in enumerate(
            (
                (fresh_hbm, fresh),
                (query_hbm, query_ref),
                (new_hbm, new_ref),
                (cache_hbm, cache),
                (len_hbm, len_ref),
                (weight_hbm, weight.at[pl.ds(0, weight_hbm.shape[0])]),
            )
        )
    ]
    for load in loads:
        load.start()
    load_fresh, load_query, load_new, load_cache, load_len, load_weight = loads

    n_tracks = owner_row_ref.shape[1]
    load_owner.wait()
    owner = owner_row_ref[...]
    slot_of = lax.broadcasted_iota(jnp.int32, (n_tracks, n_tracks), 0)
    lane_of = lax.broadcasted_iota(jnp.int32, (n_tracks, n_tracks), 1)
    track_column = jnp.max(jnp.where(owner == slot_of, lane_of, 0), axis=1, keepdims=True)
    track_row = jnp.max(jnp.where(slot_of == lane_of, track_column, 0), axis=0, keepdims=True)
    owner_z, owner_y = owner // SIDE, owner % SIDE
    place_row = jnp.where(
        (owner_z + owner_y) % 2 == 0,
        owner_y // 4 * 32 + owner_z * PAIR + owner_y // 2 % PAIR,
        owner_z // 4 * 32 + 16 + owner_y * PAIR + owner_z // 2 % PAIR,
    )
    table[...] = track_row
    load_table = pltpu.make_async_copy(table, table_smem, local_sem.at[7])
    load_table.start()
    picked = slot_of == place_row
    pick[...] = picked.astype(jnp.float32).T.astype(jnp.bfloat16)

    query_f32[...] = jnp.zeros_like(query_f32)
    load_query.wait()
    query_flat = query_ref[0].astype(jnp.float32)
    for g in range(GROUP):
        query_f32[pl.ds(g, STEPS, stride=GROUP), :] = query_flat[
            :, g * D_HEAD : (g + 1) * D_HEAD
        ]
    parity = (z + y) % 2
    my_index = jnp.where(parity == 0, y // 2, z // 2)
    my_chunk, my_group = my_index // PAIR, parity * PAIR + my_index % PAIR
    mine = my_chunk * 2 * PAIR + my_group
    my_query = query_f32[...].astype(jnp.bfloat16)
    query_all[mine] = my_query
    width = weight_hbm.shape[0]
    weight[width:] = jnp.zeros((weight.shape[0] - width, weight.shape[1]), weight.dtype)

    load_table.wait()
    load_fresh.wait()

    def slot_at(kind, place, i):
        if kind == 0:
            return place * SIDE + 2 * i + place % 2
        return (2 * i + 1 - place % 2) * SIDE + place

    for chunk in range(CHUNKS):
        for kind in (0, 1):
            for place in range(SIDE):
                for j in range(PAIR):
                    slot = slot_at(kind, place, chunk * PAIR + j)
                    send_kv[chunk, kind, place, j] = fresh[table_smem[0, slot]]
    for chunk in range(CHUNKS):
        for kind in (0, 1):
            recv_kv[chunk, kind, me[kind]] = send_kv[chunk, kind, me[kind]]

    pl.semaphore_wait(barrier, len(peers))

    q_copies = []
    for n, step in enumerate(FAR_FIRST):
        peer = at(z + step * parity, y + step * (1 - parity))
        q_copies.append(
            remote(query_all.at[mine], query_all.at[mine], q_send.at[n], q_recv.at[mine], peer)
        )
        q_copies[-1].start()
    def spread(buffer, source, chunk, send_sems, recv_sems, turn):
        copies = []
        for n, step in enumerate(FAR_FIRST):
            for kind in (0, 1):
                axis = kind ^ turn
                here = me[axis]
                from_ref = (
                    buffer.at[chunk, kind, here]
                    if source is None
                    else source.at[chunk, kind, lax.rem(here + step, SIDE)]
                )
                copies.append(
                    remote(
                        from_ref,
                        buffer.at[chunk, kind, here],
                        send_sems.at[chunk, kind, n],
                        recv_sems.at[chunk, kind, here],
                        along(axis, step),
                    )
                )
                copies[-1].start()
        return copies

    def arrival(buffer, chunk, kind, there, send_sems, recv_sems):
        block = buffer.at[chunk, kind, there]
        remote(
            block, block, send_sems.at[chunk, kind, 0], recv_sems.at[chunk, kind, there], any_peer
        ).wait_recv()

    def collect(buffer, chunk, send_sems, recv_sems, turn):
        for step in FAR_FIRST[::-1]:
            for kind in (0, 1):
                there = lax.rem(me[kind ^ turn] + step, SIDE)
                arrival(buffer, chunk, kind, there, send_sems, recv_sems)

    kv_copies = []
    for chunk in range(CHUNKS):
        kv_copies += spread(recv_kv, send_kv, chunk, kv_send, kv_recv, 0)

    load_cache.wait()
    load_new.wait()
    load_len.wait()
    parts = []
    fill = fill_ref[0]
    for block in range(cache.shape[0] // CBLK):
        rows = pl.ds(block * CBLK, CBLK)
        position = block * CBLK + lax.broadcasted_iota(jnp.int32, (PAD, CBLK), 1)
        parts.append(
            attend(my_query, cache[rows, :D_HEAD], cache[rows, D_HEAD:], position < fill)
        )
    query_full = query_f32[...]
    new_rows = new_ref[0].astype(jnp.float32)
    step_of_row = lax.broadcasted_iota(jnp.int32, (PAD, 1), 0) // GROUP
    new_scores = [
        jnp.where(
            u <= step_of_row,
            jnp.sum(query_full * new_rows[u : u + 1, :D_HEAD], axis=1, keepdims=True) * SCALE,
            NONE,
        )
        for u in range(STEPS)
    ]
    new_top = functools.reduce(jnp.maximum, new_scores)
    new_weights = [
        jnp.where(u <= step_of_row, jnp.exp(new_scores[u] - new_top), 0.0) for u in range(STEPS)
    ]
    new_output = sum(
        new_weights[u].astype(jnp.bfloat16).astype(jnp.float32) * new_rows[u : u + 1, D_HEAD:]
        for u in range(STEPS)
    )
    parts.append((new_top, sum(new_weights), new_output))
    top, total, output = merge(parts)
    row_id = lax.broadcasted_iota(jnp.int32, (PAD, D_HEAD), 0)
    lane_id = lax.broadcasted_iota(jnp.int32, (PAD, D_HEAD), 1)
    own_lane = lane_id == row_id + my_group * PAD
    cache_out[...] = output / total
    own_log = jnp.sum(
        jnp.where(own_lane, top + jnp.log(total), 0.0), axis=0, keepdims=True
    )
    own_lanes = lane_id[:1] // PAD == my_group
    for chunk in range(CHUNKS):
        cache_log[chunk : chunk + 1] = jnp.where(
            jnp.logical_and(own_lanes, my_chunk == chunk), own_log, NONE
        )

    for n in range(2 * HALF - 1):
        came = lax.rem(mine + 1 + n, 2 * HALF)
        remote(
            query_all.at[came], query_all.at[came], q_send.at[n], q_recv.at[came], any_peer
        ).wait_recv()

    span = SIDE * 16
    position_id = lax.broadcasted_iota(jnp.int32, (span, D_HEAD), 0)
    lane_group = lax.broadcasted_iota(jnp.int32, (1, D_HEAD), 1) // PAD
    positions = jnp.where(
        lane_group < PAIR,
        (position_id // 16) * span + y * 16 + position_id % 16,
        z * span + position_id,
    )
    row16 = lax.broadcasted_iota(jnp.int32, (16, D_HEAD), 0)
    groups = [(kind, j) for kind in (0, 1) for j in range(PAIR)]
    o_copies = []
    for chunk in range(CHUNKS):
        lengths = jnp.zeros((1, D_HEAD), jnp.int32)
        for n, (kind, j) in enumerate(groups):
            i = chunk * PAIR + j
            if kind == 0:
                slot = z * SIDE + 2 * i + z % 2
            else:
                slot = (2 * i + 1 - y % 2) * SIDE + y
            lengths = jnp.where(lane_group == n, len_ref[table_smem[0, slot]], lengths)
        valid = positions < lengths
        collect(recv_kv, chunk, kv_send, kv_recv, 0)
        every = lax.dot_general(
            recv_kv[chunk, :, :, :, :, :D_HEAD].reshape(2 * PAIR * span, D_HEAD),
            query_all[chunk * 2 * PAIR : (chunk + 1) * 2 * PAIR].reshape(D_HEAD, D_HEAD),
            (((1,), (1,)), ((), ())),
            preferred_element_type=jnp.float32,
        ).reshape(2, SIDE, PAIR, 16, D_HEAD)
        scores = every[0, :, 0]
        for n, (kind, j) in enumerate(groups[1:]):
            scores = jnp.where(lane_group[None] == n + 1, every[kind, :, j], scores)
        scores = scores.reshape(span, D_HEAD) * SCALE
        own = cache_log[chunk : chunk + 1]
        top = jnp.maximum(
            jnp.max(jnp.where(valid, scores, NONE), axis=0, keepdims=True), own
        )
        weights = jnp.where(valid, jnp.exp(scores - top), 0.0)
        own_weight = jnp.exp(own - top)
        total = jnp.sum(weights, axis=0, keepdims=True) + own_weight
        share = 1.0 / total
        shares = (weights * share).T.astype(jnp.bfloat16)
        outputs = [
            jnp.dot(
                shares[n * PAD : (n + 1) * PAD],
                recv_kv[chunk, kind, :, j, :, D_HEAD:].reshape(span, D_HEAD),
                preferred_element_type=jnp.float32,
            )[:ROWS]
            for n, (kind, j) in enumerate(groups)
        ]
        own_column = jnp.sum(
            jnp.where(own_lane, own_weight * share, 0.0), axis=1, keepdims=True
        )
        own_part = (own_column * cache_out[...])[:ROWS]
        outputs = [
            output + jnp.where(mine == chunk * 2 * PAIR + n, own_part, 0.0)
            for n, output in enumerate(outputs)
        ]
        line = top + jnp.log(total)
        first = line.astype(jnp.bfloat16).astype(jnp.float32)
        second = (line - first).astype(jnp.bfloat16).astype(jnp.float32)
        third = line - first - second
        lines = jnp.where(
            row16 == 0,
            first,
            jnp.where(row16 == 1, second, jnp.where(row16 == 2, third, 0.0)),
        )
        for kind in (0, 1):
            pieces[chunk, kind, me[1 - kind]] = jnp.concatenate(
                outputs[kind * PAIR : (kind + 1) * PAIR] + [lines], axis=0
            ).astype(jnp.bfloat16)
        o_copies += spread(pieces, None, chunk, o_send, o_recv, 1)

    g_copies = []
    for chunk in range(CHUNKS):
        collect(pieces, chunk, o_send, o_recv, 1)
        arrived = [
            [pieces[chunk, kind, src].astype(jnp.float32) for src in range(SIDE)]
            for kind in (0, 1)
        ]
        logs = [
            jnp.concatenate([jnp.sum(a[BAND:], axis=0, keepdims=True) for a in some], axis=0)
            for some in arrived
        ]
        logs = jnp.where(lane_group < PAIR, logs[0], logs[1])
        weights = jnp.exp(logs - jnp.max(logs, axis=0, keepdims=True))
        weights = weights / jnp.sum(weights, axis=0, keepdims=True)
        columns = jnp.concatenate(
            [weights, jnp.zeros((D_HEAD - SIDE, D_HEAD), jnp.float32)], axis=0
        ).T
        rows = []
        for n, (kind, j) in enumerate(groups):
            acc = None
            for src in range(SIDE):
                term = (
                    columns[n * PAD : n * PAD + ROWS, src : src + 1]
                    * arrived[kind][src][j * ROWS : (j + 1) * ROWS]
                )
                acc = term if acc is None else acc + term
            rows.append(acc)
        for kind in (0, 1):
            gathered[chunk, kind, me[kind]] = jnp.concatenate(
                rows[kind * PAIR : (kind + 1) * PAIR], axis=0
            ).astype(jnp.bfloat16)
        g_copies += spread(gathered, None, chunk, g_send, g_recv, 0)

    load_weight.wait()
    s_copies = []
    per_chunk = n_tracks // CHUNKS
    lane = lax.broadcasted_iota(jnp.int32, (per_chunk, 128), 1)
    for chunk in range(CHUNKS):
        for step in (0,) + FAR_FIRST[::-1]:
            for kind in (0, 1):
                there = lax.rem(me[kind] + step, SIDE)
                if step:
                    arrival(gathered, chunk, kind, there, g_send, g_recv)
                place = ((chunk * 2 + kind) * SIDE + there) * BAND
                stage[pl.ds(place, BAND), :] = gathered[chunk, kind, there].astype(jnp.float32)
        product = None
        for g in range(GROUP):
            left = jnp.concatenate(
                [
                    stage[
                        pl.ds(chunk * per_chunk * ROWS + t * GROUP + g, per_chunk, stride=ROWS), :
                    ]
                    for t in range(STEPS)
                ],
                axis=0,
            ).astype(jnp.bfloat16)
            term = lax.dot_general(
                left,
                weight[:, g * D_HEAD : (g + 1) * D_HEAD],
                (((1,), (1,)), ((), ())),
                preferred_element_type=jnp.float32,
            )
            product = term if product is None else product + term
        parts = [product[t * per_chunk : (t + 1) * per_chunk] for t in range(STEPS)]
        middle = pltpu.roll(parts[1], width, 1)
        last = pltpu.roll(parts[2], 2 * width - 128, 1)
        sums[chunk, head, :, :128] = jnp.where(lane < width, parts[0], middle).astype(jnp.bfloat16)
        sums[chunk, head, :, 128:] = jnp.where(lane < 2 * width - 128, middle, last).astype(
            jnp.bfloat16
        )
        for n, step in enumerate(HEAD_ORDER):
            s_copies.append(
                remote(
                    sums.at[chunk, head],
                    sums.at[chunk, head],
                    s_send.at[chunk, n],
                    s_recv.at[chunk, head],
                    head_peer(step),
                )
            )
            s_copies[-1].start()

    decoded = None
    for chunk in range(CHUNKS):
        for step in HEAD_ORDER[::-1]:
            there = lax.rem(head + step, n_heads)
            remote(
                sums.at[chunk, there],
                sums.at[chunk, there],
                s_send.at[chunk, 0],
                s_recv.at[chunk, there],
                any_peer,
            ).wait_recv()
        summed = sums[chunk, 0].astype(jnp.float32)
        for there in range(1, n_heads):
            summed = summed + sums[chunk, there].astype(jnp.float32)
        term = jnp.dot(
            pick[:, chunk * per_chunk : (chunk + 1) * per_chunk],
            summed.astype(jnp.bfloat16),
            preferred_element_type=jnp.float32,
        )
        decoded = term if decoded is None else decoded + term
    lane = lax.broadcasted_iota(jnp.int32, (n_tracks, 128), 1)
    left, right = decoded[:, :128], decoded[:, 128:]
    split = 128 - width
    middle = jnp.where(lane < split, pltpu.roll(left, split, 1), pltpu.roll(right, split, 1))
    last = pltpu.roll(right, 256 - 2 * width, 1)
    for t, rows in enumerate((left, middle, last)):
        out_ref[t * n_tracks : (t + 1) * n_tracks] = rows[:, :width].astype(out_ref.dtype)

    for copy in q_copies + kv_copies + o_copies + g_copies + s_copies:
        copy.wait_send()


def shards(queries, new_kv, cache_kv, cache_fill, fresh_kv, fresh_len, owner_slot, out_weight):
    n_tracks, depth = fresh_kv.shape[0], fresh_kv.shape[1]
    width = out_weight.shape[1]
    vmem = pl.BlockSpec(memory_space=pltpu.VMEM)
    hbm = pl.BlockSpec(memory_space=pltpu.HBM)
    bf16, f32 = jnp.bfloat16, jnp.float32
    dma = pltpu.SemaphoreType.DMA
    out = pl.pallas_call(
        kernel,
        name="handoff_decode",
        out_shape=pltpu.VMEM((n_tracks * STEPS, width), bf16),
        in_specs=[pl.BlockSpec(memory_space=pltpu.SMEM)] + [hbm] * 7,
        out_specs=vmem,
        scratch_shapes=[
            pltpu.VMEM((1, n_tracks), jnp.int32),
            pltpu.SMEM((n_tracks,), jnp.int32),
            pltpu.VMEM(queries.shape, bf16),
            pltpu.VMEM(new_kv.shape, bf16),
            pltpu.VMEM(cache_kv.shape[1:], bf16),
            pltpu.VMEM(fresh_kv.shape, bf16),
            pltpu.VMEM((128, out_weight.shape[0]), bf16),
            pltpu.VMEM((1, n_tracks), jnp.int32),
            pltpu.SMEM((1, n_tracks), jnp.int32),
            pltpu.VMEM((PAD, D_HEAD), f32),
            pltpu.VMEM((2 * HALF, PAD, D_HEAD), bf16),
            pltpu.VMEM((CHUNKS, 2, SIDE, PAIR, depth, 2 * D_HEAD), bf16),
            pltpu.VMEM((CHUNKS, 2, SIDE, PAIR, depth, 2 * D_HEAD), bf16),
            pltpu.VMEM((PAD, D_HEAD), f32),
            pltpu.VMEM((8, D_HEAD), f32),
            pltpu.VMEM((CHUNKS, 2, SIDE, PIECE, D_HEAD), bf16),
            pltpu.VMEM((CHUNKS, 2, SIDE, BAND, D_HEAD), bf16),
            pltpu.VMEM((n_tracks * ROWS, D_HEAD), f32),
            pltpu.VMEM((CHUNKS, 8, n_tracks // CHUNKS, 256), bf16),
            pltpu.VMEM((n_tracks, n_tracks), bf16),
            dma((8,)),
            dma((SIDE - 1,)),
            dma((2 * HALF,)),
            dma((CHUNKS, 2, SIDE - 1)),
            dma((CHUNKS, 2, SIDE)),
            dma((CHUNKS, 2, SIDE - 1)),
            dma((CHUNKS, 2, SIDE)),
            dma((CHUNKS, 2, SIDE - 1)),
            dma((CHUNKS, 2, SIDE)),
            dma((CHUNKS, 7)),
            dma((CHUNKS, 8)),
        ],
        compiler_params=pltpu.CompilerParams(
            collective_id=0, has_side_effects=True, vmem_limit_bytes=32 * 1024 * 1024
        ),
    )(
        cache_fill,
        *(
            pltpu.with_memory_space_constraint(operand, pltpu.HBM)
            for operand in (
                owner_slot[None, :],
                fresh_len,
                queries,
                new_kv,
                cache_kv[0],
                fresh_kv,
                out_weight.T,
            )
        )
    )
    return out.reshape(STEPS, n_tracks, width).transpose(1, 0, 2)


def solution(mesh):
    in_specs = (
        P("stream", None, "head"),
        P("stream", None, "head"),
        P("stream", None, "head"),
        P("stream"),
        P(None, "stream", "head"),
        P(),
        P(),
        P("head", "stream"),
    )
    out_specs = P(None, None, "stream")
    return jax.shard_map(shards, mesh=mesh, in_specs=in_specs, out_specs=out_specs, check_vma=False)
```

```python
import functools

import jax
import jax.numpy as jnp
from jax import lax
from jax.experimental import pallas as pl
from jax.experimental.pallas import tpu as pltpu
from jax.sharding import PartitionSpec as P

D_HEAD = 128
GROUP = 8
STEPS = 3
ROWS = STEPS * GROUP
PAD = 32
CBLK = 512
SIDE = 8
HALF = 4
PAIR = 2
CHUNKS = HALF // PAIR
BAND = PAIR * ROWS
PIECE = BAND + 16
NONE = -1e30
SCALE = D_HEAD**-0.5
FAR_FIRST = (4, 3, 5, 2, 6, 1, 7)
HEAD_ORDER = (4, 5, 2, 3, 6, 7, 1)
MESH = pl.DeviceIdType.MESH


def remote(src, dst, send_sem, recv_sem, device):
    return pltpu.make_async_remote_copy(
        src_ref=src,
        dst_ref=dst,
        send_sem=send_sem,
        recv_sem=recv_sem,
        device_id=device,
        device_id_type=MESH,
    )


def attend(query_rows, keys, values, valid):
    scores = (
        lax.dot_general(
            query_rows, keys, (((1,), (1,)), ((), ())), preferred_element_type=jnp.float32
        )
        * SCALE
    )
    highest = jnp.max(jnp.where(valid, scores, NONE), axis=1, keepdims=True)
    weights = jnp.where(valid, jnp.exp(scores - highest), 0.0)
    total = jnp.sum(weights, axis=1, keepdims=True)
    output = jnp.dot(weights.astype(jnp.bfloat16), values, preferred_element_type=jnp.float32)
    return highest, total, output


def merge(parts):
    top = functools.reduce(jnp.maximum, [part[0] for part in parts])
    factors = [jnp.exp(part[0] - top) for part in parts]
    total = sum(f * part[1] for f, part in zip(factors, parts))
    output = sum(f * part[2] for f, part in zip(factors, parts))
    return top, total, output


def kernel(
    fill_ref,
    owner_hbm,
    len_hbm,
    query_hbm,
    new_hbm,
    cache_hbm,
    fresh_hbm,
    weight_hbm,
    out_ref,
    owner_row_ref,
    len_ref,
    query_ref,
    new_ref,
    cache,
    fresh,
    weight,
    table,
    table_smem,
    query_f32,
    query_all,
    send_kv,
    recv_kv,
    cache_out,
    cache_log,
    pieces,
    gathered,
    stage,
    sums,
    pick,
    local_sem,
    q_send,
    q_recv,
    kv_send,
    kv_recv,
    o_send,
    o_recv,
    g_send,
    g_recv,
    s_send,
    s_recv,
):
    stream = lax.axis_index("stream")
    head = lax.axis_index("head")
    z, y = stream // SIDE, stream % SIDE
    n_heads = 8
    me = (z, y)

    def at(zz, yy):
        return {"stream": lax.rem(zz, SIDE) * SIDE + lax.rem(yy, SIDE)}

    def along(axis, step):
        return at(z + step, y) if axis == 0 else at(z, y + step)

    def head_peer(step):
        return {"head": lax.rem(head + step, n_heads)}

    any_peer = head_peer(1)

    load_owner = pltpu.make_async_copy(owner_hbm, owner_row_ref, local_sem.at[0])
    load_owner.start()
    barrier = pltpu.get_barrier_semaphore()
    peers = [along(axis, step) for step in FAR_FIRST for axis in (0, 1)]
    peers += [head_peer(step) for step in range(1, n_heads)]
    for peer in peers:
        pl.semaphore_signal(barrier, inc=1, device_id=peer, device_id_type=MESH)

    loads = [
        pltpu.make_async_copy(src, dst, local_sem.at[1 + n])
        for n, (src, dst) in enumerate(
            (
                (fresh_hbm, fresh),
                (query_hbm, query_ref),
                (new_hbm, new_ref),
                (cache_hbm, cache),
                (len_hbm, len_ref),
                (weight_hbm, weight.at[pl.ds(0, weight_hbm.shape[0])]),
            )
        )
    ]
    for load in loads:
        load.start()
    load_fresh, load_query, load_new, load_cache, load_len, load_weight = loads

    n_tracks = owner_row_ref.shape[1]
    load_owner.wait()
    owner = owner_row_ref[...]
    slot_of = lax.broadcasted_iota(jnp.int32, (n_tracks, n_tracks), 0)
    lane_of = lax.broadcasted_iota(jnp.int32, (n_tracks, n_tracks), 1)
    track_column = jnp.max(jnp.where(owner == slot_of, lane_of, 0), axis=1, keepdims=True)
    track_row = jnp.max(jnp.where(slot_of == lane_of, track_column, 0), axis=0, keepdims=True)
    owner_z, owner_y = owner // SIDE, owner % SIDE
    place_row = jnp.where(
        (owner_z + owner_y) % 2 == 0,
        owner_y // 4 * 32 + owner_z * PAIR + owner_y // 2 % PAIR,
        owner_z // 4 * 32 + 16 + owner_y * PAIR + owner_z // 2 % PAIR,
    )
    table[...] = track_row
    load_table = pltpu.make_async_copy(table, table_smem, local_sem.at[7])
    load_table.start()
    picked = slot_of == place_row
    pick[...] = picked.astype(jnp.float32).T.astype(jnp.bfloat16)

    query_f32[...] = jnp.zeros_like(query_f32)
    load_query.wait()
    query_flat = query_ref[0].astype(jnp.float32)
    for g in range(GROUP):
        query_f32[pl.ds(g, STEPS, stride=GROUP), :] = query_flat[
            :, g * D_HEAD : (g + 1) * D_HEAD
        ]
    parity = (z + y) % 2
    my_index = jnp.where(parity == 0, y // 2, z // 2)
    my_chunk, my_group = my_index // PAIR, parity * PAIR + my_index % PAIR
    mine = my_chunk * 2 * PAIR + my_group
    my_query = query_f32[...].astype(jnp.bfloat16)
    query_all[mine] = my_query
    width = weight_hbm.shape[0]
    weight[width:] = jnp.zeros((weight.shape[0] - width, weight.shape[1]), weight.dtype)

    load_table.wait()
    load_fresh.wait()

    def slot_at(kind, place, i):
        if kind == 0:
            return place * SIDE + 2 * i + place % 2
        return (2 * i + 1 - place % 2) * SIDE + place

    for chunk in range(CHUNKS):
        for kind in (0, 1):
            for place in range(SIDE):
                for j in range(PAIR):
                    slot = slot_at(kind, place, chunk * PAIR + j)
                    send_kv[chunk, kind * SIDE + place, j] = fresh[table_smem[0, slot]]
    for chunk in range(CHUNKS):
        for kind in (0, 1):
            here = kind * SIDE + me[kind]
            recv_kv[chunk, here] = send_kv[chunk, here]

    pl.semaphore_wait(barrier, len(peers))

    def settle(view, send_sem, recv_sem):
        return remote(view, view, send_sem, recv_sem, any_peer)

    for step in FAR_FIRST:
        peer = at(z + step * parity, y + step * (1 - parity))
        remote(query_all.at[mine], query_all.at[mine], q_send, q_recv, peer).start()

    def spread(buffer, source, chunk, send_sems, recv_sems, turn):
        for step in FAR_FIRST:
            for kind in (0, 1):
                axis = kind ^ turn
                here = kind * SIDE + me[axis]
                there = kind * SIDE + lax.rem(me[axis] + step, SIDE)
                remote(
                    buffer.at[chunk, here] if source is None else source.at[chunk, there],
                    buffer.at[chunk, here],
                    send_sems.at[chunk],
                    recv_sems.at[chunk],
                    along(axis, step),
                ).start()

    def spreading(buffer, chunk, send_sems, recv_sems):
        view = buffer.at[chunk, pl.ds(0, 2 * (SIDE - 1))]
        return settle(view, send_sems.at[chunk], recv_sems.at[chunk])

    for chunk in range(CHUNKS):
        spread(recv_kv, send_kv, chunk, kv_send, kv_recv, 0)

    load_cache.wait()
    load_new.wait()
    load_len.wait()
    parts = []
    fill = fill_ref[0]
    for block in range(cache.shape[0] // CBLK):
        rows = pl.ds(block * CBLK, CBLK)
        position = block * CBLK + lax.broadcasted_iota(jnp.int32, (PAD, CBLK), 1)
        parts.append(
            attend(my_query, cache[rows, :D_HEAD], cache[rows, D_HEAD:], position < fill)
        )
    query_full = query_f32[...]
    new_rows = new_ref[0].astype(jnp.float32)
    step_of_row = lax.broadcasted_iota(jnp.int32, (PAD, 1), 0) // GROUP
    new_scores = [
        jnp.where(
            u <= step_of_row,
            jnp.sum(query_full * new_rows[u : u + 1, :D_HEAD], axis=1, keepdims=True) * SCALE,
            NONE,
        )
        for u in range(STEPS)
    ]
    new_top = functools.reduce(jnp.maximum, new_scores)
    new_weights = [
        jnp.where(u <= step_of_row, jnp.exp(new_scores[u] - new_top), 0.0) for u in range(STEPS)
    ]
    new_output = sum(
        new_weights[u].astype(jnp.bfloat16).astype(jnp.float32) * new_rows[u : u + 1, D_HEAD:]
        for u in range(STEPS)
    )
    parts.append((new_top, sum(new_weights), new_output))
    top, total, output = merge(parts)
    row_id = lax.broadcasted_iota(jnp.int32, (PAD, D_HEAD), 0)
    lane_id = lax.broadcasted_iota(jnp.int32, (PAD, D_HEAD), 1)
    own_lane = lane_id == row_id + my_group * PAD
    cache_out[...] = output / total
    own_log = jnp.sum(
        jnp.where(own_lane, top + jnp.log(total), 0.0), axis=0, keepdims=True
    )
    own_lanes = lane_id[:1] // PAD == my_group
    for chunk in range(CHUNKS):
        cache_log[chunk : chunk + 1] = jnp.where(
            jnp.logical_and(own_lanes, my_chunk == chunk), own_log, NONE
        )

    q_all = settle(query_all.at[pl.ds(0, SIDE - 1)], q_send, q_recv)
    q_all.wait_recv()

    span = SIDE * 16
    position_id = lax.broadcasted_iota(jnp.int32, (span, D_HEAD), 0)
    lane_group = lax.broadcasted_iota(jnp.int32, (1, D_HEAD), 1) // PAD
    positions = jnp.where(
        lane_group < PAIR,
        (position_id // 16) * span + y * 16 + position_id % 16,
        z * span + position_id,
    )
    row16 = lax.broadcasted_iota(jnp.int32, (16, D_HEAD), 0)
    groups = [(kind, j) for kind in (0, 1) for j in range(PAIR)]
    for chunk in range(CHUNKS):
        lengths = jnp.zeros((1, D_HEAD), jnp.int32)
        for n, (kind, j) in enumerate(groups):
            i = chunk * PAIR + j
            if kind == 0:
                slot = z * SIDE + 2 * i + z % 2
            else:
                slot = (2 * i + 1 - y % 2) * SIDE + y
            lengths = jnp.where(lane_group == n, len_ref[table_smem[0, slot]], lengths)
        valid = positions < lengths
        spreading(recv_kv, chunk, kv_send, kv_recv).wait_recv()
        every = lax.dot_general(
            recv_kv[chunk, :, :, :, :D_HEAD].reshape(2 * PAIR * span, D_HEAD),
            query_all[chunk * 2 * PAIR : (chunk + 1) * 2 * PAIR].reshape(D_HEAD, D_HEAD),
            (((1,), (1,)), ((), ())),
            preferred_element_type=jnp.float32,
        ).reshape(2, SIDE, PAIR, 16, D_HEAD)
        scores = every[0, :, 0]
        for n, (kind, j) in enumerate(groups[1:]):
            scores = jnp.where(lane_group[None] == n + 1, every[kind, :, j], scores)
        scores = scores.reshape(span, D_HEAD) * SCALE
        own = cache_log[chunk : chunk + 1]
        top = jnp.maximum(
            jnp.max(jnp.where(valid, scores, NONE), axis=0, keepdims=True), own
        )
        weights = jnp.where(valid, jnp.exp(scores - top), 0.0)
        own_weight = jnp.exp(own - top)
        total = jnp.sum(weights, axis=0, keepdims=True) + own_weight
        share = 1.0 / total
        shares = (weights * share).T.astype(jnp.bfloat16)
        outputs = [
            jnp.dot(
                shares[n * PAD : (n + 1) * PAD],
                recv_kv[chunk, kind * SIDE : (kind + 1) * SIDE, j, :, D_HEAD:].reshape(
                    span, D_HEAD
                ),
                preferred_element_type=jnp.float32,
            )[:ROWS]
            for n, (kind, j) in enumerate(groups)
        ]
        own_column = jnp.sum(
            jnp.where(own_lane, own_weight * share, 0.0), axis=1, keepdims=True
        )
        own_part = (own_column * cache_out[...])[:ROWS]
        outputs = [
            output + jnp.where(mine == chunk * 2 * PAIR + n, own_part, 0.0)
            for n, output in enumerate(outputs)
        ]
        line = top + jnp.log(total)
        first = line.astype(jnp.bfloat16).astype(jnp.float32)
        second = (line - first).astype(jnp.bfloat16).astype(jnp.float32)
        third = line - first - second
        lines = jnp.where(
            row16 == 0,
            first,
            jnp.where(row16 == 1, second, jnp.where(row16 == 2, third, 0.0)),
        )
        for kind in (0, 1):
            pieces[chunk, kind * SIDE + me[1 - kind]] = jnp.concatenate(
                outputs[kind * PAIR : (kind + 1) * PAIR] + [lines], axis=0
            ).astype(jnp.bfloat16)
        spread(pieces, None, chunk, o_send, o_recv, 1)

    q_all.wait_send()
    for chunk in range(CHUNKS):
        spreading(recv_kv, chunk, kv_send, kv_recv).wait_send()
    for chunk in range(CHUNKS):
        spreading(pieces, chunk, o_send, o_recv).wait_recv()
        arrived = [
            [pieces[chunk, kind * SIDE + src].astype(jnp.float32) for src in range(SIDE)]
            for kind in (0, 1)
        ]
        logs = [
            jnp.concatenate([jnp.sum(a[BAND:], axis=0, keepdims=True) for a in some], axis=0)
            for some in arrived
        ]
        logs = jnp.where(lane_group < PAIR, logs[0], logs[1])
        weights = jnp.exp(logs - jnp.max(logs, axis=0, keepdims=True))
        weights = weights / jnp.sum(weights, axis=0, keepdims=True)
        columns = jnp.concatenate(
            [weights, jnp.zeros((D_HEAD - SIDE, D_HEAD), jnp.float32)], axis=0
        ).T
        rows = []
        for n, (kind, j) in enumerate(groups):
            acc = None
            for src in range(SIDE):
                term = (
                    columns[n * PAD : n * PAD + ROWS, src : src + 1]
                    * arrived[kind][src][j * ROWS : (j + 1) * ROWS]
                )
                acc = term if acc is None else acc + term
            rows.append(acc)
        for kind in (0, 1):
            gathered[chunk, kind * SIDE + me[kind]] = jnp.concatenate(
                rows[kind * PAIR : (kind + 1) * PAIR], axis=0
            ).astype(jnp.bfloat16)
        spread(gathered, None, chunk, g_send, g_recv, 0)

    load_weight.wait()
    for chunk in range(CHUNKS):
        spreading(pieces, chunk, o_send, o_recv).wait_send()
    per_chunk = n_tracks // CHUNKS
    lane = lax.broadcasted_iota(jnp.int32, (per_chunk, 128), 1)
    for chunk in range(CHUNKS):
        spreading(gathered, chunk, g_send, g_recv).wait_recv()
        stage[pl.ds(chunk * per_chunk * ROWS, per_chunk * ROWS), :] = (
            gathered[chunk].astype(jnp.float32).reshape(per_chunk * ROWS, D_HEAD)
        )
        product = None
        for g in range(GROUP):
            left = jnp.concatenate(
                [
                    stage[
                        pl.ds(chunk * per_chunk * ROWS + t * GROUP + g, per_chunk, stride=ROWS), :
                    ]
                    for t in range(STEPS)
                ],
                axis=0,
            ).astype(jnp.bfloat16)
            term = lax.dot_general(
                left,
                weight[:, g * D_HEAD : (g + 1) * D_HEAD],
                (((1,), (1,)), ((), ())),
                preferred_element_type=jnp.float32,
            )
            product = term if product is None else product + term
        parts = [product[t * per_chunk : (t + 1) * per_chunk] for t in range(STEPS)]
        middle = pltpu.roll(parts[1], width, 1)
        last = pltpu.roll(parts[2], 2 * width - 128, 1)
        sums[chunk, head, :, :128] = jnp.where(lane < width, parts[0], middle).astype(jnp.bfloat16)
        sums[chunk, head, :, 128:] = jnp.where(lane < 2 * width - 128, middle, last).astype(
            jnp.bfloat16
        )
        for step in HEAD_ORDER:
            remote(
                sums.at[chunk, head],
                sums.at[chunk, head],
                s_send.at[chunk],
                s_recv.at[chunk],
                head_peer(step),
            ).start()
    for chunk in range(CHUNKS):
        spreading(gathered, chunk, g_send, g_recv).wait_send()

    def summing(chunk):
        view = sums.at[chunk, pl.ds(0, n_heads - 1)]
        return settle(view, s_send.at[chunk], s_recv.at[chunk])

    decoded = None
    for chunk in range(CHUNKS):
        summing(chunk).wait_recv()
        summed = sums[chunk, 0].astype(jnp.float32)
        for there in range(1, n_heads):
            summed = summed + sums[chunk, there].astype(jnp.float32)
        term = jnp.dot(
            pick[:, chunk * per_chunk : (chunk + 1) * per_chunk],
            summed.astype(jnp.bfloat16),
            preferred_element_type=jnp.float32,
        )
        decoded = term if decoded is None else decoded + term
    lane = lax.broadcasted_iota(jnp.int32, (n_tracks, 128), 1)
    left, right = decoded[:, :128], decoded[:, 128:]
    split = 128 - width
    middle = jnp.where(lane < split, pltpu.roll(left, split, 1), pltpu.roll(right, split, 1))
    last = pltpu.roll(right, 256 - 2 * width, 1)
    for t, rows in enumerate((left, middle, last)):
        out_ref[t * n_tracks : (t + 1) * n_tracks] = rows[:, :width].astype(out_ref.dtype)

    for chunk in range(CHUNKS):
        summing(chunk).wait_send()


def shards(queries, new_kv, cache_kv, cache_fill, fresh_kv, fresh_len, owner_slot, out_weight):
    n_tracks, depth = fresh_kv.shape[0], fresh_kv.shape[1]
    width = out_weight.shape[1]
    vmem = pl.BlockSpec(memory_space=pltpu.VMEM)
    hbm = pl.BlockSpec(memory_space=pltpu.HBM)
    bf16, f32 = jnp.bfloat16, jnp.float32
    dma = pltpu.SemaphoreType.DMA
    out = pl.pallas_call(
        kernel,
        name="handoff_decode",
        out_shape=pltpu.VMEM((n_tracks * STEPS, width), bf16),
        in_specs=[pl.BlockSpec(memory_space=pltpu.SMEM)] + [hbm] * 7,
        out_specs=vmem,
        scratch_shapes=[
            pltpu.VMEM((1, n_tracks), jnp.int32),
            pltpu.SMEM((n_tracks,), jnp.int32),
            pltpu.VMEM(queries.shape, bf16),
            pltpu.VMEM(new_kv.shape, bf16),
            pltpu.VMEM(cache_kv.shape[1:], bf16),
            pltpu.VMEM(fresh_kv.shape, bf16),
            pltpu.VMEM((128, out_weight.shape[0]), bf16),
            pltpu.VMEM((1, n_tracks), jnp.int32),
            pltpu.SMEM((1, n_tracks), jnp.int32),
            pltpu.VMEM((PAD, D_HEAD), f32),
            pltpu.VMEM((2 * HALF, PAD, D_HEAD), bf16),
            pltpu.VMEM((CHUNKS, 2 * SIDE, PAIR, depth, 2 * D_HEAD), bf16),
            pltpu.VMEM((CHUNKS, 2 * SIDE, PAIR, depth, 2 * D_HEAD), bf16),
            pltpu.VMEM((PAD, D_HEAD), f32),
            pltpu.VMEM((8, D_HEAD), f32),
            pltpu.VMEM((CHUNKS, 2 * SIDE, PIECE, D_HEAD), bf16),
            pltpu.VMEM((CHUNKS, 2 * SIDE, BAND, D_HEAD), bf16),
            pltpu.VMEM((n_tracks * ROWS, D_HEAD), f32),
            pltpu.VMEM((CHUNKS, 8, n_tracks // CHUNKS, 256), bf16),
            pltpu.VMEM((n_tracks, n_tracks), bf16),
            dma((8,)),
            dma,
            dma,
            dma((CHUNKS,)),
            dma((CHUNKS,)),
            dma((CHUNKS,)),
            dma((CHUNKS,)),
            dma((CHUNKS,)),
            dma((CHUNKS,)),
            dma((CHUNKS,)),
            dma((CHUNKS,)),
        ],
        compiler_params=pltpu.CompilerParams(
            collective_id=0, has_side_effects=True, vmem_limit_bytes=32 * 1024 * 1024
        ),
    )(
        cache_fill,
        *(
            pltpu.with_memory_space_constraint(operand, pltpu.HBM)
            for operand in (
                owner_slot[None, :],
                fresh_len,
                queries,
                new_kv,
                cache_kv[0],
                fresh_kv,
                out_weight.T,
            )
        )
    )
    return out.reshape(STEPS, n_tracks, width).transpose(1, 0, 2)


def solution(mesh):
    in_specs = (
        P("stream", None, "head"),
        P("stream", None, "head"),
        P("stream", None, "head"),
        P("stream"),
        P(None, "stream", "head"),
        P(),
        P(),
        P("head", "stream"),
    )
    out_specs = P(None, None, "stream")
    return jax.shard_map(shards, mesh=mesh, in_specs=in_specs, out_specs=out_specs, check_vma=False)
```

```python
import functools

import jax
import jax.numpy as jnp
from jax import lax
from jax.experimental import pallas as pl
from jax.experimental.pallas import tpu as pltpu
from jax.sharding import PartitionSpec as P

D_HEAD = 128
GROUP = 8
STEPS = 3
ROWS = STEPS * GROUP
PAD = 32
CBLK = 512
SIDE = 8
HALF = 4
PIECE = PAD
PAIR = 2
ROUNDS = HALF // PAIR
BAND = PAIR * ROWS
NONE = -1e30
SCALE = D_HEAD**-0.5
FAR_FIRST = (4, 3, 5, 2, 6, 1, 7)
HEAD_ORDER = (4, 5, 2, 3, 6, 7, 1)
MESH = pl.DeviceIdType.MESH


def remote(src, dst, send_sem, recv_sem, device):
    return pltpu.make_async_remote_copy(
        src_ref=src,
        dst_ref=dst,
        send_sem=send_sem,
        recv_sem=recv_sem,
        device_id=device,
        device_id_type=MESH,
    )


def attend(query_rows, keys, values, valid):
    scores = (
        lax.dot_general(
            query_rows, keys, (((1,), (1,)), ((), ())), preferred_element_type=jnp.float32
        )
        * SCALE
    )
    highest = jnp.max(jnp.where(valid, scores, NONE), axis=1, keepdims=True)
    weights = jnp.where(valid, jnp.exp(scores - highest), 0.0)
    total = jnp.sum(weights, axis=1, keepdims=True)
    output = jnp.dot(weights.astype(jnp.bfloat16), values, preferred_element_type=jnp.float32)
    return highest, total, output


def merge(parts):
    top = functools.reduce(jnp.maximum, [part[0] for part in parts])
    factors = [jnp.exp(part[0] - top) for part in parts]
    total = sum(f * part[1] for f, part in zip(factors, parts))
    output = sum(f * part[2] for f, part in zip(factors, parts))
    return top, total, output


def kernel(
    fill_ref,
    owner_hbm,
    len_hbm,
    query_hbm,
    new_hbm,
    cache_hbm,
    fresh_hbm,
    weight_hbm,
    out_ref,
    owner_row_ref,
    len_ref,
    query_ref,
    new_ref,
    cache,
    fresh,
    weight,
    table,
    table_smem,
    query_f32,
    query_all,
    send_kv,
    recv_kv,
    cache_out,
    cache_log,
    pieces,
    gathered,
    stage,
    sums,
    pick,
    local_sem,
    q_send,
    q_recv,
    kv_send,
    kv_recv,
    o_send,
    o_recv,
    g_send,
    g_recv,
    s_send,
    s_recv,
):
    stream = lax.axis_index("stream")
    head = lax.axis_index("head")
    z, y = stream // SIDE, stream % SIDE
    n_heads = 8
    me = (z, y)

    place = [[lax.rem(me[axis] + step, SIDE) for step in range(SIDE)] for axis in (0, 1)]
    device = [
        [place[0][step] * SIDE + y for step in range(SIDE)],
        [z * SIDE + place[1][step] for step in range(SIDE)],
    ]

    def along(axis, step):
        return {"stream": device[axis][step]}

    def head_peer(step):
        return {"head": lax.rem(head + step, n_heads)}

    any_peer = head_peer(1)

    load_owner = pltpu.make_async_copy(owner_hbm, owner_row_ref, local_sem.at[0])
    load_owner.start()
    barrier = pltpu.get_barrier_semaphore()
    peers = [along(axis, step) for step in FAR_FIRST for axis in (0, 1)]
    peers += [head_peer(step) for step in range(1, n_heads)]
    for peer in peers:
        pl.semaphore_signal(barrier, inc=1, device_id=peer, device_id_type=MESH)

    loads = [
        pltpu.make_async_copy(src, dst, local_sem.at[1 + n])
        for n, (src, dst) in enumerate(
            (
                (fresh_hbm, fresh),
                (query_hbm, query_ref),
                (new_hbm, new_ref),
                (cache_hbm, cache),
                (len_hbm, len_ref),
                (weight_hbm, weight.at[pl.ds(0, weight_hbm.shape[0])]),
            )
        )
    ]
    for load in loads:
        load.start()
    load_fresh, load_query, load_new, load_cache, load_len, load_weight = loads

    n_tracks = owner_row_ref.shape[1]
    load_owner.wait()
    owner = owner_row_ref[...]
    slot_of = lax.broadcasted_iota(jnp.int32, (n_tracks, n_tracks), 0)
    lane_of = lax.broadcasted_iota(jnp.int32, (n_tracks, n_tracks), 1)
    track_column = jnp.max(jnp.where(owner == slot_of, lane_of, 0), axis=1, keepdims=True)
    track_row = jnp.max(jnp.where(slot_of == lane_of, track_column, 0), axis=0, keepdims=True)
    owner_z, owner_y = owner // SIDE, owner % SIDE
    place_row = jnp.where(
        (owner_z + owner_y) % 2 == 0,
        owner_y // 4 * 32 + owner_z * PAIR + owner_y // 2 % PAIR,
        owner_z // 4 * 32 + 16 + owner_y * PAIR + owner_z // 2 % PAIR,
    )
    table[...] = track_row
    load_table = pltpu.make_async_copy(table, table_smem, local_sem.at[7])
    load_table.start()
    picked = slot_of == place_row
    pick[...] = picked.astype(jnp.float32).T.astype(jnp.bfloat16)

    query_f32[...] = jnp.zeros_like(query_f32)
    load_query.wait()
    query_flat = query_ref[0].astype(jnp.float32)
    for g in range(GROUP):
        query_f32[pl.ds(g, STEPS, stride=GROUP), :] = query_flat[
            :, g * D_HEAD : (g + 1) * D_HEAD
        ]
    parity = (z + y) % 2
    my_index = jnp.where(parity == 0, y // 2, z // 2)
    mine = my_index * 2 + parity
    my_query = query_f32[...].astype(jnp.bfloat16)
    query_all[mine] = my_query
    width = weight_hbm.shape[0]
    weight[width:] = jnp.zeros((weight.shape[0] - width, weight.shape[1]), weight.dtype)

    load_table.wait()
    load_fresh.wait()

    def slot_at(kind, p, i):
        if kind == 0:
            return p * SIDE + 2 * i + p % 2
        return (2 * i + 1 - p % 2) * SIDE + p

    for i in range(HALF):
        for kind in (0, 1):
            for p in range(SIDE):
                send_kv[i, kind * SIDE + p] = fresh[table_smem[0, slot_at(kind, p, i)]]
    for i in range(HALF):
        for kind in (0, 1):
            here = kind * SIDE + me[kind]
            recv_kv[i, here] = send_kv[i, here]

    pl.semaphore_wait(barrier, len(peers))

    def settle(view, send_sem, recv_sem):
        return remote(view, view, send_sem, recv_sem, any_peer)

    for step in FAR_FIRST:
        peer = {"stream": jnp.where(parity == 0, device[1][step], device[0][step])}
        remote(query_all.at[mine], query_all.at[mine], q_send, q_recv, peer).start()

    def spread(buffer, source, chunk, send_sems, recv_sems, turn):
        for step in FAR_FIRST:
            for kind in (0, 1):
                axis = kind ^ turn
                here = kind * SIDE + me[axis]
                there = kind * SIDE + place[axis][step]
                remote(
                    buffer.at[chunk, here] if source is None else source.at[chunk, there],
                    buffer.at[chunk, here],
                    send_sems.at[chunk],
                    recv_sems.at[chunk],
                    along(axis, step),
                ).start()

    def spreading(buffer, chunk, send_sems, recv_sems):
        view = buffer.at[chunk, pl.ds(0, 2 * (SIDE - 1))]
        return settle(view, send_sems.at[chunk], recv_sems.at[chunk])

    for i in range(HALF):
        spread(recv_kv, send_kv, i, kv_send, kv_recv, 0)

    load_cache.wait()
    load_new.wait()
    load_len.wait()
    parts = []
    fill = fill_ref[0]
    for block in range(cache.shape[0] // CBLK):
        rows = pl.ds(block * CBLK, CBLK)
        position = block * CBLK + lax.broadcasted_iota(jnp.int32, (PAD, CBLK), 1)
        parts.append(
            attend(my_query, cache[rows, :D_HEAD], cache[rows, D_HEAD:], position < fill)
        )
    query_full = query_f32[...]
    new_rows = new_ref[0].astype(jnp.float32)
    step_of_row = lax.broadcasted_iota(jnp.int32, (PAD, 1), 0) // GROUP
    new_scores = [
        jnp.where(
            u <= step_of_row,
            jnp.sum(query_full * new_rows[u : u + 1, :D_HEAD], axis=1, keepdims=True) * SCALE,
            NONE,
        )
        for u in range(STEPS)
    ]
    new_top = functools.reduce(jnp.maximum, new_scores)
    new_weights = [
        jnp.where(u <= step_of_row, jnp.exp(new_scores[u] - new_top), 0.0) for u in range(STEPS)
    ]
    new_output = sum(
        new_weights[u].astype(jnp.bfloat16).astype(jnp.float32) * new_rows[u : u + 1, D_HEAD:]
        for u in range(STEPS)
    )
    parts.append((new_top, sum(new_weights), new_output))
    top, total, output = merge(parts)
    row_id = lax.broadcasted_iota(jnp.int32, (PAD, D_HEAD), 0)
    lane_id = lax.broadcasted_iota(jnp.int32, (PAD, D_HEAD), 1)
    own_lane = lane_id == row_id + parity * PAD
    cache_out[...] = output / total
    own_log = jnp.sum(
        jnp.where(own_lane, top + jnp.log(total), 0.0), axis=0, keepdims=True
    )
    own_lanes = lane_id[:1] // PAD == parity
    for i in range(HALF):
        cache_log[i : i + 1] = jnp.where(
            jnp.logical_and(own_lanes, my_index == i), own_log, NONE
        )

    q_all = settle(query_all.at[pl.ds(0, SIDE - 1)], q_send, q_recv)
    q_all.wait_recv()

    span = SIDE * 16
    position_id = lax.broadcasted_iota(jnp.int32, (span, D_HEAD), 0)
    lane_kind = lax.broadcasted_iota(jnp.int32, (1, D_HEAD), 1) // PAD % 2
    positions = jnp.where(
        lane_kind == 0,
        (position_id // 16) * span + y * 16 + position_id % 16,
        z * span + position_id,
    )
    row8 = lax.broadcasted_iota(jnp.int32, (8, D_HEAD), 0)
    for i in range(HALF):
        slots = (z * SIDE + 2 * i + z % 2, (2 * i + 1 - y % 2) * SIDE + y)
        lengths = [len_ref[table_smem[0, slot]] for slot in slots]
        valid = positions < jnp.where(lane_kind == 0, lengths[0], lengths[1])
        pair = query_all[2 * i : 2 * i + 2].reshape(2 * PAD, D_HEAD)
        queries = jnp.concatenate([pair, pair], axis=0)
        spreading(recv_kv, i, kv_send, kv_recv).wait_recv()
        every = lax.dot_general(
            recv_kv[i, :, :, :D_HEAD].reshape(2 * span, D_HEAD),
            queries,
            (((1,), (1,)), ((), ())),
            preferred_element_type=jnp.float32,
        )
        scores = jnp.where(lane_kind == 0, every[:span], every[span:]) * SCALE
        own = cache_log[i : i + 1]
        top = jnp.maximum(
            jnp.max(jnp.where(valid, scores, NONE), axis=0, keepdims=True), own
        )
        weights = jnp.where(valid, jnp.exp(scores - top), 0.0)
        own_weight = jnp.exp(own - top)
        total = jnp.sum(weights, axis=0, keepdims=True) + own_weight
        share = 1.0 / total
        shares = (weights * share).T.astype(jnp.bfloat16)
        outputs = [
            jnp.dot(
                shares[kind * PAD : (kind + 1) * PAD],
                recv_kv[i, kind * SIDE : (kind + 1) * SIDE, :, D_HEAD:].reshape(span, D_HEAD),
                preferred_element_type=jnp.float32,
            )[:ROWS]
            for kind in (0, 1)
        ]
        own_column = jnp.sum(
            jnp.where(own_lane, own_weight * share, 0.0), axis=1, keepdims=True
        )
        own_part = (own_column * cache_out[...])[:ROWS]
        line = top + jnp.log(total)
        first = line.astype(jnp.bfloat16).astype(jnp.float32)
        second = (line - first).astype(jnp.bfloat16).astype(jnp.float32)
        third = line - first - second
        lines = jnp.where(
            row8 == 0,
            first,
            jnp.where(row8 == 1, second, jnp.where(row8 == 2, third, 0.0)),
        )
        for kind in (0, 1):
            output = outputs[kind] + jnp.where(mine == 2 * i + kind, own_part, 0.0)
            pieces[i, kind * SIDE + me[1 - kind]] = jnp.concatenate(
                [output, lines], axis=0
            ).astype(jnp.bfloat16)
        spread(pieces, None, i, o_send, o_recv, 1)

    q_all.wait_send()
    for i in range(HALF):
        spreading(recv_kv, i, kv_send, kv_recv).wait_send()
    done = []
    for i in range(HALF):
        spreading(pieces, i, o_send, o_recv).wait_recv()
        arrived = [
            [pieces[i, kind * SIDE + src].astype(jnp.float32) for src in range(SIDE)]
            for kind in (0, 1)
        ]
        logs = [
            jnp.concatenate([jnp.sum(a[ROWS:], axis=0, keepdims=True) for a in some], axis=0)
            for some in arrived
        ]
        logs = jnp.where(lane_kind == 0, logs[0], logs[1])
        weights = jnp.exp(logs - jnp.max(logs, axis=0, keepdims=True))
        weights = weights / jnp.sum(weights, axis=0, keepdims=True)
        columns = jnp.concatenate(
            [weights, jnp.zeros((D_HEAD - SIDE, D_HEAD), jnp.float32)], axis=0
        ).T
        for kind in (0, 1):
            acc = None
            for src in range(SIDE):
                term = (
                    columns[kind * PAD : kind * PAD + ROWS, src : src + 1]
                    * arrived[kind][src][:ROWS]
                )
                acc = term if acc is None else acc + term
            done.append(acc)
        if len(done) == 2 * PAIR:
            turn = i // PAIR
            for kind in (0, 1):
                gathered[turn, kind * SIDE + me[kind]] = jnp.concatenate(
                    done[kind::2], axis=0
                ).astype(jnp.bfloat16)
            spread(gathered, None, turn, g_send, g_recv, 0)
            done = []

    load_weight.wait()
    for i in range(HALF):
        spreading(pieces, i, o_send, o_recv).wait_send()
    per_chunk = n_tracks // ROUNDS
    lane = lax.broadcasted_iota(jnp.int32, (per_chunk, 128), 1)
    for chunk in range(ROUNDS):
        spreading(gathered, chunk, g_send, g_recv).wait_recv()
        stage[pl.ds(chunk * per_chunk * ROWS, per_chunk * ROWS), :] = (
            gathered[chunk].astype(jnp.float32).reshape(per_chunk * ROWS, D_HEAD)
        )
        product = None
        for g in range(GROUP):
            left = jnp.concatenate(
                [
                    stage[
                        pl.ds(chunk * per_chunk * ROWS + t * GROUP + g, per_chunk, stride=ROWS), :
                    ]
                    for t in range(STEPS)
                ],
                axis=0,
            ).astype(jnp.bfloat16)
            term = lax.dot_general(
                left,
                weight[:, g * D_HEAD : (g + 1) * D_HEAD],
                (((1,), (1,)), ((), ())),
                preferred_element_type=jnp.float32,
            )
            product = term if product is None else product + term
        parts = [product[t * per_chunk : (t + 1) * per_chunk] for t in range(STEPS)]
        middle = pltpu.roll(parts[1], width, 1)
        last = pltpu.roll(parts[2], 2 * width - 128, 1)
        sums[chunk, head, :, :128] = jnp.where(lane < width, parts[0], middle).astype(jnp.bfloat16)
        sums[chunk, head, :, 128:] = jnp.where(lane < 2 * width - 128, middle, last).astype(
            jnp.bfloat16
        )
        for step in HEAD_ORDER:
            remote(
                sums.at[chunk, head],
                sums.at[chunk, head],
                s_send.at[chunk],
                s_recv.at[chunk],
                head_peer(step),
            ).start()
    for chunk in range(ROUNDS):
        spreading(gathered, chunk, g_send, g_recv).wait_send()

    def summing(chunk):
        view = sums.at[chunk, pl.ds(0, n_heads - 1)]
        return settle(view, s_send.at[chunk], s_recv.at[chunk])

    decoded = None
    for chunk in range(ROUNDS):
        summing(chunk).wait_recv()
        summed = sums[chunk, 0].astype(jnp.float32)
        for there in range(1, n_heads):
            summed = summed + sums[chunk, there].astype(jnp.float32)
        term = jnp.dot(
            pick[:, chunk * per_chunk : (chunk + 1) * per_chunk],
            summed.astype(jnp.bfloat16),
            preferred_element_type=jnp.float32,
        )
        decoded = term if decoded is None else decoded + term
    lane = lax.broadcasted_iota(jnp.int32, (n_tracks, 128), 1)
    left, right = decoded[:, :128], decoded[:, 128:]
    split = 128 - width
    middle = jnp.where(lane < split, pltpu.roll(left, split, 1), pltpu.roll(right, split, 1))
    last = pltpu.roll(right, 256 - 2 * width, 1)
    for t, rows in enumerate((left, middle, last)):
        out_ref[t * n_tracks : (t + 1) * n_tracks] = rows[:, :width].astype(out_ref.dtype)

    for chunk in range(ROUNDS):
        summing(chunk).wait_send()


def shards(queries, new_kv, cache_kv, cache_fill, fresh_kv, fresh_len, owner_slot, out_weight):
    n_tracks, depth = fresh_kv.shape[0], fresh_kv.shape[1]
    width = out_weight.shape[1]
    vmem = pl.BlockSpec(memory_space=pltpu.VMEM)
    hbm = pl.BlockSpec(memory_space=pltpu.HBM)
    bf16, f32 = jnp.bfloat16, jnp.float32
    dma = pltpu.SemaphoreType.DMA
    out = pl.pallas_call(
        kernel,
        name="handoff_decode",
        out_shape=pltpu.VMEM((n_tracks * STEPS, width), bf16),
        in_specs=[pl.BlockSpec(memory_space=pltpu.SMEM)] + [hbm] * 7,
        out_specs=vmem,
        scratch_shapes=[
            pltpu.VMEM((1, n_tracks), jnp.int32),
            pltpu.SMEM((n_tracks,), jnp.int32),
            pltpu.VMEM(queries.shape, bf16),
            pltpu.VMEM(new_kv.shape, bf16),
            pltpu.VMEM(cache_kv.shape[1:], bf16),
            pltpu.VMEM(fresh_kv.shape, bf16),
            pltpu.VMEM((128, out_weight.shape[0]), bf16),
            pltpu.VMEM((1, n_tracks), jnp.int32),
            pltpu.SMEM((1, n_tracks), jnp.int32),
            pltpu.VMEM((PAD, D_HEAD), f32),
            pltpu.VMEM((2 * HALF, PAD, D_HEAD), bf16),
            pltpu.VMEM((HALF, 2 * SIDE, depth, 2 * D_HEAD), bf16),
            pltpu.VMEM((HALF, 2 * SIDE, depth, 2 * D_HEAD), bf16),
            pltpu.VMEM((PAD, D_HEAD), f32),
            pltpu.VMEM((8, D_HEAD), f32),
            pltpu.VMEM((HALF, 2 * SIDE, PIECE, D_HEAD), bf16),
            pltpu.VMEM((ROUNDS, 2 * SIDE, BAND, D_HEAD), bf16),
            pltpu.VMEM((n_tracks * ROWS, D_HEAD), f32),
            pltpu.VMEM((ROUNDS, 8, n_tracks // ROUNDS, 256), bf16),
            pltpu.VMEM((n_tracks, n_tracks), bf16),
            dma((8,)),
            dma,
            dma,
            dma((HALF,)),
            dma((HALF,)),
            dma((HALF,)),
            dma((HALF,)),
            dma((ROUNDS,)),
            dma((ROUNDS,)),
            dma((ROUNDS,)),
            dma((ROUNDS,)),
        ],
        compiler_params=pltpu.CompilerParams(
            collective_id=0, has_side_effects=True, vmem_limit_bytes=32 * 1024 * 1024
        ),
    )(
        cache_fill,
        *(
            pltpu.with_memory_space_constraint(operand, pltpu.HBM)
            for operand in (
                owner_slot[None, :],
                fresh_len,
                queries,
                new_kv,
                cache_kv[0],
                fresh_kv,
                out_weight.T,
            )
        )
    )
    return out.reshape(STEPS, n_tracks, width).transpose(1, 0, 2)


def solution(mesh):
    in_specs = (
        P("stream", None, "head"),
        P("stream", None, "head"),
        P("stream", None, "head"),
        P("stream"),
        P(None, "stream", "head"),
        P(),
        P(),
        P("head", "stream"),
    )
    out_specs = P(None, None, "stream")
    return jax.shard_map(shards, mesh=mesh, in_specs=in_specs, out_specs=out_specs, check_vma=False)
```

```python
import functools

import jax
import jax.numpy as jnp
from jax import lax
from jax.experimental import pallas as pl
from jax.experimental.pallas import tpu as pltpu
from jax.sharding import PartitionSpec as P

D_HEAD = 128
GROUP = 8
STEPS = 3
ROWS = STEPS * GROUP
PAD = 32
CBLK = 512
SIDE = 8
HALF = 4
PIECE = PAD
PAIR = 2
ROUNDS = HALF // PAIR
BAND = PAIR * ROWS
NONE = -1e30
SCALE = D_HEAD**-0.5
FAR_FIRST = (4, 3, 5, 2, 6, 1, 7)
HEAD_ORDER = (4, 5, 2, 3, 6, 7, 1)
MESH = pl.DeviceIdType.MESH


def remote(src, dst, send_sem, recv_sem, device):
    return pltpu.make_async_remote_copy(
        src_ref=src,
        dst_ref=dst,
        send_sem=send_sem,
        recv_sem=recv_sem,
        device_id=device,
        device_id_type=MESH,
    )


def attend(query_rows, keys, values, valid):
    scores = (
        lax.dot_general(
            query_rows, keys, (((1,), (1,)), ((), ())), preferred_element_type=jnp.float32
        )
        * SCALE
    )
    highest = jnp.max(jnp.where(valid, scores, NONE), axis=1, keepdims=True)
    weights = jnp.where(valid, jnp.exp(scores - highest), 0.0)
    total = jnp.sum(weights, axis=1, keepdims=True)
    output = jnp.dot(weights.astype(jnp.bfloat16), values, preferred_element_type=jnp.float32)
    return highest, total, output


def merge(parts):
    top = functools.reduce(jnp.maximum, [part[0] for part in parts])
    factors = [jnp.exp(part[0] - top) for part in parts]
    total = sum(f * part[1] for f, part in zip(factors, parts))
    output = sum(f * part[2] for f, part in zip(factors, parts))
    return top, total, output


def kernel(
    fill_ref,
    owner_hbm,
    len_hbm,
    query_hbm,
    new_hbm,
    cache_hbm,
    fresh_hbm,
    weight_hbm,
    out_ref,
    owner_row_ref,
    len_ref,
    query_ref,
    new_ref,
    cache,
    fresh,
    weight,
    table,
    table_smem,
    query_f32,
    query_all,
    send_kv,
    recv_kv,
    cache_out,
    cache_log,
    pieces,
    gathered,
    stage,
    sums,
    pick,
    local_sem,
    q_send,
    q_recv,
    kv_send,
    kv_recv,
    o_send,
    o_recv,
    g_send,
    g_recv,
    s_send,
    s_recv,
):
    stream = lax.axis_index("stream")
    head = lax.axis_index("head")
    z, y = stream // SIDE, stream % SIDE
    n_heads = 8
    me = (z, y)

    place = [[lax.rem(me[axis] + step, SIDE) for step in range(SIDE)] for axis in (0, 1)]
    device = [
        [place[0][step] * SIDE + y for step in range(SIDE)],
        [z * SIDE + place[1][step] for step in range(SIDE)],
    ]

    def along(axis, step):
        return {"stream": device[axis][step]}

    def head_peer(step):
        return {"head": lax.rem(head + step, n_heads)}

    any_peer = head_peer(1)

    load_owner = pltpu.make_async_copy(owner_hbm, owner_row_ref, local_sem.at[0])
    load_owner.start()
    barrier = pltpu.get_barrier_semaphore()
    peers = [along(axis, step) for step in FAR_FIRST for axis in (0, 1)]
    peers += [head_peer(step) for step in range(1, n_heads)]
    for peer in peers:
        pl.semaphore_signal(barrier, inc=1, device_id=peer, device_id_type=MESH)

    loads = [
        pltpu.make_async_copy(src, dst, local_sem.at[1 + n])
        for n, (src, dst) in enumerate(
            (
                (fresh_hbm, fresh),
                (query_hbm, query_ref),
                (new_hbm, new_ref),
                (cache_hbm, cache),
                (len_hbm, len_ref),
                (weight_hbm, weight.at[pl.ds(0, weight_hbm.shape[0])]),
            )
        )
    ]
    for load in loads:
        load.start()
    load_fresh, load_query, load_new, load_cache, load_len, load_weight = loads

    n_tracks = owner_row_ref.shape[1]
    load_owner.wait()
    owner = owner_row_ref[...]
    slot_of = lax.broadcasted_iota(jnp.int32, (n_tracks, n_tracks), 0)
    lane_of = lax.broadcasted_iota(jnp.int32, (n_tracks, n_tracks), 1)
    track_column = jnp.max(jnp.where(owner == slot_of, lane_of, 0), axis=1, keepdims=True)
    track_row = jnp.max(jnp.where(slot_of == lane_of, track_column, 0), axis=0, keepdims=True)
    owner_z, owner_y = owner // SIDE, owner % SIDE
    place_row = jnp.where(
        (owner_z + owner_y) % 2 == 0,
        owner_y // 4 * 32 + owner_z * PAIR + owner_y // 2 % PAIR,
        owner_z // 4 * 32 + 16 + owner_y * PAIR + owner_z // 2 % PAIR,
    )
    table[...] = track_row
    load_table = pltpu.make_async_copy(table, table_smem, local_sem.at[7])
    load_table.start()
    picked = slot_of == place_row
    pick[...] = picked.astype(jnp.float32).T.astype(jnp.bfloat16)

    query_f32[...] = jnp.zeros_like(query_f32)
    load_query.wait()
    query_flat = query_ref[0].astype(jnp.float32)
    for g in range(GROUP):
        query_f32[pl.ds(g, STEPS, stride=GROUP), :] = query_flat[
            :, g * D_HEAD : (g + 1) * D_HEAD
        ]
    parity = (z + y) % 2
    my_index = jnp.where(parity == 0, y // 2, z // 2)
    mine = my_index * 2 + parity
    my_query = query_f32[...].astype(jnp.bfloat16)
    query_all[mine] = query_f32[:ROWS].astype(jnp.bfloat16)
    width = weight_hbm.shape[0]
    weight[width:] = jnp.zeros((weight.shape[0] - width, weight.shape[1]), weight.dtype)

    load_table.wait()
    load_fresh.wait()

    def slot_at(kind, p, i):
        if kind == 0:
            return p * SIDE + 2 * i + p % 2
        return (2 * i + 1 - p % 2) * SIDE + p

    for i in range(HALF):
        for kind in (0, 1):
            for p in range(SIDE):
                send_kv[i, kind * SIDE + p] = fresh[table_smem[0, slot_at(kind, p, i)]]
    for i in range(HALF):
        for kind in (0, 1):
            here = kind * SIDE + me[kind]
            recv_kv[i, here] = send_kv[i, here]

    pl.semaphore_wait(barrier, len(peers))

    def settle(view, send_sem, recv_sem):
        return remote(view, view, send_sem, recv_sem, any_peer)

    for step in FAR_FIRST:
        peer = {"stream": jnp.where(parity == 0, device[1][step], device[0][step])}
        remote(query_all.at[mine], query_all.at[mine], q_send, q_recv, peer).start()

    def spread(buffer, source, chunk, send_sems, recv_sems, turn):
        for step in FAR_FIRST:
            for kind in (0, 1):
                axis = kind ^ turn
                here = kind * SIDE + me[axis]
                there = kind * SIDE + place[axis][step]
                remote(
                    buffer.at[chunk, here] if source is None else source.at[chunk, there],
                    buffer.at[chunk, here],
                    send_sems.at[chunk],
                    recv_sems.at[chunk],
                    along(axis, step),
                ).start()

    def spreading(buffer, chunk, send_sems, recv_sems):
        view = buffer.at[chunk, pl.ds(0, 2 * (SIDE - 1))]
        return settle(view, send_sems.at[chunk], recv_sems.at[chunk])

    for i in range(HALF):
        spread(recv_kv, send_kv, i, kv_send, kv_recv, 0)

    load_cache.wait()
    load_new.wait()
    load_len.wait()
    parts = []
    fill = fill_ref[0]
    for block in range(cache.shape[0] // CBLK):
        rows = pl.ds(block * CBLK, CBLK)
        position = block * CBLK + lax.broadcasted_iota(jnp.int32, (PAD, CBLK), 1)
        parts.append(
            attend(my_query, cache[rows, :D_HEAD], cache[rows, D_HEAD:], position < fill)
        )
    query_full = query_f32[...]
    new_rows = new_ref[0].astype(jnp.float32)
    step_of_row = lax.broadcasted_iota(jnp.int32, (PAD, 1), 0) // GROUP
    new_scores = [
        jnp.where(
            u <= step_of_row,
            jnp.sum(query_full * new_rows[u : u + 1, :D_HEAD], axis=1, keepdims=True) * SCALE,
            NONE,
        )
        for u in range(STEPS)
    ]
    new_top = functools.reduce(jnp.maximum, new_scores)
    new_weights = [
        jnp.where(u <= step_of_row, jnp.exp(new_scores[u] - new_top), 0.0) for u in range(STEPS)
    ]
    new_output = sum(
        new_weights[u].astype(jnp.bfloat16).astype(jnp.float32) * new_rows[u : u + 1, D_HEAD:]
        for u in range(STEPS)
    )
    parts.append((new_top, sum(new_weights), new_output))
    top, total, output = merge(parts)
    row_id = lax.broadcasted_iota(jnp.int32, (PAD, D_HEAD), 0)
    lane_id = lax.broadcasted_iota(jnp.int32, (PAD, D_HEAD), 1)
    own_lane = lane_id == row_id + parity * PAD
    cache_out[...] = output / total
    own_log = jnp.sum(
        jnp.where(own_lane, top + jnp.log(total), 0.0), axis=0, keepdims=True
    )
    own_lanes = lane_id[:1] // PAD == parity
    for i in range(HALF):
        cache_log[i : i + 1] = jnp.where(
            jnp.logical_and(own_lanes, my_index == i), own_log, NONE
        )

    q_all = settle(query_all.at[pl.ds(0, SIDE - 1)], q_send, q_recv)
    q_all.wait_recv()

    span = SIDE * 16
    position_id = lax.broadcasted_iota(jnp.int32, (span, D_HEAD), 0)
    lane_kind = lax.broadcasted_iota(jnp.int32, (1, D_HEAD), 1) // PAD % 2
    positions = jnp.where(
        lane_kind == 0,
        (position_id // 16) * span + y * 16 + position_id % 16,
        z * span + position_id,
    )
    row8 = lax.broadcasted_iota(jnp.int32, (8, D_HEAD), 0)
    for i in range(HALF):
        slots = (z * SIDE + 2 * i + z % 2, (2 * i + 1 - y % 2) * SIDE + y)
        lengths = [len_ref[table_smem[0, slot]] for slot in slots]
        valid = positions < jnp.where(lane_kind == 0, lengths[0], lengths[1])
        blank = jnp.zeros((PAD - ROWS, D_HEAD), jnp.float32)
        queries = jnp.concatenate(
            [query_all[2 * i].astype(jnp.float32), blank]
            + [query_all[2 * i + 1].astype(jnp.float32), blank],
            axis=0,
        )
        queries = jnp.concatenate([queries, queries], axis=0).astype(jnp.bfloat16)
        spreading(recv_kv, i, kv_send, kv_recv).wait_recv()
        every = lax.dot_general(
            recv_kv[i, :, :, :D_HEAD].reshape(2 * span, D_HEAD),
            queries,
            (((1,), (1,)), ((), ())),
            preferred_element_type=jnp.float32,
        )
        scores = jnp.where(lane_kind == 0, every[:span], every[span:]) * SCALE
        own = cache_log[i : i + 1]
        top = jnp.maximum(
            jnp.max(jnp.where(valid, scores, NONE), axis=0, keepdims=True), own
        )
        weights = jnp.where(valid, jnp.exp(scores - top), 0.0)
        own_weight = jnp.exp(own - top)
        total = jnp.sum(weights, axis=0, keepdims=True) + own_weight
        share = 1.0 / total
        shares = (weights * share).T.astype(jnp.bfloat16)
        outputs = [
            jnp.dot(
                shares[kind * PAD : (kind + 1) * PAD],
                recv_kv[i, kind * SIDE : (kind + 1) * SIDE, :, D_HEAD:].reshape(span, D_HEAD),
                preferred_element_type=jnp.float32,
            )[:ROWS]
            for kind in (0, 1)
        ]
        own_column = jnp.sum(
            jnp.where(own_lane, own_weight * share, 0.0), axis=1, keepdims=True
        )
        own_part = (own_column * cache_out[...])[:ROWS]
        line = top + jnp.log(total)
        first = line.astype(jnp.bfloat16).astype(jnp.float32)
        second = (line - first).astype(jnp.bfloat16).astype(jnp.float32)
        third = line - first - second
        lines = jnp.where(
            row8 == 0,
            first,
            jnp.where(row8 == 1, second, jnp.where(row8 == 2, third, 0.0)),
        )
        for kind in (0, 1):
            output = outputs[kind] + jnp.where(mine == 2 * i + kind, own_part, 0.0)
            pieces[i, kind * SIDE + me[1 - kind]] = jnp.concatenate(
                [output, lines], axis=0
            ).astype(jnp.bfloat16)
        spread(pieces, None, i, o_send, o_recv, 1)

    q_all.wait_send()
    for i in range(HALF):
        spreading(recv_kv, i, kv_send, kv_recv).wait_send()
    done = []
    for i in range(HALF):
        spreading(pieces, i, o_send, o_recv).wait_recv()
        arrived = [
            [pieces[i, kind * SIDE + src].astype(jnp.float32) for src in range(SIDE)]
            for kind in (0, 1)
        ]
        logs = [
            jnp.concatenate([jnp.sum(a[ROWS:], axis=0, keepdims=True) for a in some], axis=0)
            for some in arrived
        ]
        logs = jnp.where(lane_kind == 0, logs[0], logs[1])
        weights = jnp.exp(logs - jnp.max(logs, axis=0, keepdims=True))
        weights = weights / jnp.sum(weights, axis=0, keepdims=True)
        columns = jnp.concatenate(
            [weights, jnp.zeros((D_HEAD - SIDE, D_HEAD), jnp.float32)], axis=0
        ).T
        for kind in (0, 1):
            acc = None
            for src in range(SIDE):
                term = (
                    columns[kind * PAD : kind * PAD + ROWS, src : src + 1]
                    * arrived[kind][src][:ROWS]
                )
                acc = term if acc is None else acc + term
            done.append(acc)
        if len(done) == 2 * PAIR:
            turn = i // PAIR
            for kind in (0, 1):
                gathered[turn, kind * SIDE + me[kind]] = jnp.concatenate(
                    done[kind::2], axis=0
                ).astype(jnp.bfloat16)
            spread(gathered, None, turn, g_send, g_recv, 0)
            done = []

    load_weight.wait()
    for i in range(HALF):
        spreading(pieces, i, o_send, o_recv).wait_send()
    per_chunk = n_tracks // ROUNDS
    lane = lax.broadcasted_iota(jnp.int32, (per_chunk, 128), 1)
    for chunk in range(ROUNDS):
        spreading(gathered, chunk, g_send, g_recv).wait_recv()
        stage[pl.ds(chunk * per_chunk * ROWS, per_chunk * ROWS), :] = (
            gathered[chunk].astype(jnp.float32).reshape(per_chunk * ROWS, D_HEAD)
        )
        product = None
        for g in range(GROUP):
            left = jnp.concatenate(
                [
                    stage[
                        pl.ds(chunk * per_chunk * ROWS + t * GROUP + g, per_chunk, stride=ROWS), :
                    ]
                    for t in range(STEPS)
                ],
                axis=0,
            ).astype(jnp.bfloat16)
            term = lax.dot_general(
                left,
                weight[:, g * D_HEAD : (g + 1) * D_HEAD],
                (((1,), (1,)), ((), ())),
                preferred_element_type=jnp.float32,
            )
            product = term if product is None else product + term
        parts = [product[t * per_chunk : (t + 1) * per_chunk] for t in range(STEPS)]
        middle = pltpu.roll(parts[1], width, 1)
        last = pltpu.roll(parts[2], 2 * width - 128, 1)
        sums[chunk, head, :, :128] = jnp.where(lane < width, parts[0], middle).astype(jnp.bfloat16)
        sums[chunk, head, :, 128:] = jnp.where(lane < 2 * width - 128, middle, last).astype(
            jnp.bfloat16
        )
        for step in HEAD_ORDER:
            remote(
                sums.at[chunk, head],
                sums.at[chunk, head],
                s_send.at[chunk],
                s_recv.at[chunk],
                head_peer(step),
            ).start()
    for chunk in range(ROUNDS):
        spreading(gathered, chunk, g_send, g_recv).wait_send()

    def summing(chunk):
        view = sums.at[chunk, pl.ds(0, n_heads - 1)]
        return settle(view, s_send.at[chunk], s_recv.at[chunk])

    decoded = None
    for chunk in range(ROUNDS):
        summing(chunk).wait_recv()
        summed = sums[chunk, 0].astype(jnp.float32)
        for there in range(1, n_heads):
            summed = summed + sums[chunk, there].astype(jnp.float32)
        term = jnp.dot(
            pick[:, chunk * per_chunk : (chunk + 1) * per_chunk],
            summed.astype(jnp.bfloat16),
            preferred_element_type=jnp.float32,
        )
        decoded = term if decoded is None else decoded + term
    lane = lax.broadcasted_iota(jnp.int32, (n_tracks, 128), 1)
    left, right = decoded[:, :128], decoded[:, 128:]
    split = 128 - width
    middle = jnp.where(lane < split, pltpu.roll(left, split, 1), pltpu.roll(right, split, 1))
    last = pltpu.roll(right, 256 - 2 * width, 1)
    for t, rows in enumerate((left, middle, last)):
        out_ref[t * n_tracks : (t + 1) * n_tracks] = rows[:, :width].astype(out_ref.dtype)

    for chunk in range(ROUNDS):
        summing(chunk).wait_send()


def shards(queries, new_kv, cache_kv, cache_fill, fresh_kv, fresh_len, owner_slot, out_weight):
    n_tracks, depth = fresh_kv.shape[0], fresh_kv.shape[1]
    width = out_weight.shape[1]
    vmem = pl.BlockSpec(memory_space=pltpu.VMEM)
    hbm = pl.BlockSpec(memory_space=pltpu.HBM)
    bf16, f32 = jnp.bfloat16, jnp.float32
    dma = pltpu.SemaphoreType.DMA
    out = pl.pallas_call(
        kernel,
        name="handoff_decode",
        out_shape=pltpu.VMEM((n_tracks * STEPS, width), bf16),
        in_specs=[pl.BlockSpec(memory_space=pltpu.SMEM)] + [hbm] * 7,
        out_specs=vmem,
        scratch_shapes=[
            pltpu.VMEM((1, n_tracks), jnp.int32),
            pltpu.SMEM((n_tracks,), jnp.int32),
            pltpu.VMEM(queries.shape, bf16),
            pltpu.VMEM(new_kv.shape, bf16),
            pltpu.VMEM(cache_kv.shape[1:], bf16),
            pltpu.VMEM(fresh_kv.shape, bf16),
            pltpu.VMEM((128, out_weight.shape[0]), bf16),
            pltpu.VMEM((1, n_tracks), jnp.int32),
            pltpu.SMEM((1, n_tracks), jnp.int32),
            pltpu.VMEM((PAD, D_HEAD), f32),
            pltpu.VMEM((2 * HALF, ROWS, D_HEAD), bf16),
            pltpu.VMEM((HALF, 2 * SIDE, depth, 2 * D_HEAD), bf16),
            pltpu.VMEM((HALF, 2 * SIDE, depth, 2 * D_HEAD), bf16),
            pltpu.VMEM((PAD, D_HEAD), f32),
            pltpu.VMEM((8, D_HEAD), f32),
            pltpu.VMEM((HALF, 2 * SIDE, PIECE, D_HEAD), bf16),
            pltpu.VMEM((ROUNDS, 2 * SIDE, BAND, D_HEAD), bf16),
            pltpu.VMEM((n_tracks * ROWS, D_HEAD), f32),
            pltpu.VMEM((ROUNDS, 8, n_tracks // ROUNDS, 256), bf16),
            pltpu.VMEM((n_tracks, n_tracks), bf16),
            dma((8,)),
            dma,
            dma,
            dma((HALF,)),
            dma((HALF,)),
            dma((HALF,)),
            dma((HALF,)),
            dma((ROUNDS,)),
            dma((ROUNDS,)),
            dma((ROUNDS,)),
            dma((ROUNDS,)),
        ],
        compiler_params=pltpu.CompilerParams(
            collective_id=0, has_side_effects=True, vmem_limit_bytes=32 * 1024 * 1024
        ),
    )(
        cache_fill,
        *(
            pltpu.with_memory_space_constraint(operand, pltpu.HBM)
            for operand in (
                owner_slot[None, :],
                fresh_len,
                queries,
                new_kv,
                cache_kv[0],
                fresh_kv,
                out_weight.T,
            )
        )
    )
    return out.reshape(STEPS, n_tracks, width).transpose(1, 0, 2)


def solution(mesh):
    in_specs = (
        P("stream", None, "head"),
        P("stream", None, "head"),
        P("stream", None, "head"),
        P("stream"),
        P(None, "stream", "head"),
        P(),
        P(),
        P("head", "stream"),
    )
    out_specs = P(None, None, "stream")
    return jax.shard_map(shards, mesh=mesh, in_specs=in_specs, out_specs=out_specs, check_vma=False)
```

```python
import functools

import jax
import jax.numpy as jnp
from jax import lax
from jax.experimental import pallas as pl
from jax.experimental.pallas import tpu as pltpu
from jax.sharding import PartitionSpec as P

D_HEAD = 128
GROUP = 8
STEPS = 3
ROWS = STEPS * GROUP
PAD = 32
CBLK = 512
SIDE = 8
HALF = 4
PIECE = PAD
PAIR = 2
ROUNDS = HALF // PAIR
BAND = PAIR * ROWS
NONE = -1e30
SCALE = D_HEAD**-0.5
FAR_FIRST = (4, 3, 5, 2, 6, 1, 7)
HEAD_ORDER = (4, 5, 2, 3, 6, 7, 1)
MESH = pl.DeviceIdType.MESH


def remote(src, dst, send_sem, recv_sem, device):
    return pltpu.make_async_remote_copy(
        src_ref=src,
        dst_ref=dst,
        send_sem=send_sem,
        recv_sem=recv_sem,
        device_id=device,
        device_id_type=MESH,
    )


def attend(query_rows, keys, values, valid):
    scores = (
        lax.dot_general(
            query_rows, keys, (((1,), (1,)), ((), ())), preferred_element_type=jnp.float32
        )
        * SCALE
    )
    highest = jnp.max(jnp.where(valid, scores, NONE), axis=1, keepdims=True)
    weights = jnp.where(valid, jnp.exp(scores - highest), 0.0)
    total = jnp.sum(weights, axis=1, keepdims=True)
    output = jnp.dot(weights.astype(jnp.bfloat16), values, preferred_element_type=jnp.float32)
    return highest, total, output


def merge(parts):
    top = functools.reduce(jnp.maximum, [part[0] for part in parts])
    factors = [jnp.exp(part[0] - top) for part in parts]
    total = sum(f * part[1] for f, part in zip(factors, parts))
    output = sum(f * part[2] for f, part in zip(factors, parts))
    return top, total, output


def kernel(
    fill_ref,
    owner_hbm,
    len_hbm,
    query_hbm,
    new_hbm,
    cache_hbm,
    fresh_hbm,
    weight_hbm,
    out_ref,
    owner_row_ref,
    len_ref,
    query_ref,
    new_ref,
    cache,
    fresh,
    weight,
    table,
    table_smem,
    query_f32,
    query_all,
    send_kv,
    recv_kv,
    cache_out,
    cache_log,
    pieces,
    gathered,
    stage,
    sums,
    pick,
    local_sem,
    q_send,
    q_recv,
    kv_send,
    kv_recv,
    o_send,
    o_recv,
    g_send,
    g_recv,
    s_send,
    s_recv,
):
    stream = lax.axis_index("stream")
    head = lax.axis_index("head")
    z, y = stream // SIDE, stream % SIDE
    n_heads = 8
    me = (z, y)

    place = [[lax.rem(me[axis] + step, SIDE) for step in range(SIDE)] for axis in (0, 1)]
    device = [
        [place[0][step] * SIDE + y for step in range(SIDE)],
        [z * SIDE + place[1][step] for step in range(SIDE)],
    ]

    def along(axis, step):
        return {"stream": device[axis][step]}

    def head_peer(step):
        return {"head": lax.rem(head + step, n_heads)}

    any_peer = head_peer(1)

    load_owner = pltpu.make_async_copy(owner_hbm, owner_row_ref, local_sem.at[0])
    load_owner.start()
    barrier = pltpu.get_barrier_semaphore()
    peers = [along(axis, step) for step in FAR_FIRST for axis in (0, 1)]
    peers += [head_peer(step) for step in range(1, n_heads)]
    for peer in peers:
        pl.semaphore_signal(barrier, inc=1, device_id=peer, device_id_type=MESH)

    loads = [
        pltpu.make_async_copy(src, dst, local_sem.at[1 + n])
        for n, (src, dst) in enumerate(
            (
                (fresh_hbm, fresh),
                (query_hbm, query_ref),
                (new_hbm, new_ref),
                (cache_hbm, cache),
                (len_hbm, len_ref),
                (weight_hbm, weight.at[pl.ds(0, weight_hbm.shape[0])]),
            )
        )
    ]
    for load in loads:
        load.start()
    load_fresh, load_query, load_new, load_cache, load_len, load_weight = loads

    n_tracks = owner_row_ref.shape[1]
    load_owner.wait()
    owner = owner_row_ref[...]
    slot_of = lax.broadcasted_iota(jnp.int32, (n_tracks, n_tracks), 0)
    lane_of = lax.broadcasted_iota(jnp.int32, (n_tracks, n_tracks), 1)
    track_column = jnp.max(jnp.where(owner == slot_of, lane_of, 0), axis=1, keepdims=True)
    track_row = jnp.max(jnp.where(slot_of == lane_of, track_column, 0), axis=0, keepdims=True)
    owner_z, owner_y = owner // SIDE, owner % SIDE
    place_row = jnp.where(
        (owner_z + owner_y) % 2 == 0,
        owner_y // 4 * 32 + owner_z * PAIR + owner_y // 2 % PAIR,
        owner_z // 4 * 32 + 16 + owner_y * PAIR + owner_z // 2 % PAIR,
    )
    table[...] = track_row
    load_table = pltpu.make_async_copy(table, table_smem, local_sem.at[7])
    load_table.start()
    picked = slot_of == place_row
    pick[...] = picked.astype(jnp.float32).T.astype(jnp.bfloat16)

    query_f32[...] = jnp.zeros_like(query_f32)
    load_query.wait()
    query_flat = query_ref[0].astype(jnp.float32)
    for g in range(GROUP):
        query_f32[pl.ds(g, STEPS, stride=GROUP), :] = query_flat[
            :, g * D_HEAD : (g + 1) * D_HEAD
        ]
    parity = (z + y) % 2
    my_index = jnp.where(parity == 0, y // 2, z // 2)
    mine = my_index * 2 + parity
    my_query = query_f32[...].astype(jnp.bfloat16)
    query_all[mine] = my_query
    width = weight_hbm.shape[0]
    weight[width:] = jnp.zeros((weight.shape[0] - width, weight.shape[1]), weight.dtype)

    load_table.wait()
    load_fresh.wait()

    def slot_at(kind, p, i):
        if kind == 0:
            return p * SIDE + 2 * i + p % 2
        return (2 * i + 1 - p % 2) * SIDE + p

    for i in range(HALF):
        for kind in (0, 1):
            for p in range(SIDE):
                send_kv[i, kind * SIDE + p] = fresh[table_smem[0, slot_at(kind, p, i)]]
    for i in range(HALF):
        for kind in (0, 1):
            here = kind * SIDE + me[kind]
            recv_kv[i, here] = send_kv[i, here]

    pl.semaphore_wait(barrier, len(peers))

    def settle(view, send_sem, recv_sem):
        return remote(view, view, send_sem, recv_sem, any_peer)

    for step in FAR_FIRST:
        peer = {"stream": jnp.where(parity == 0, device[1][step], device[0][step])}
        remote(query_all.at[mine], query_all.at[mine], q_send, q_recv, peer).start()

    def spread(buffer, source, chunk, send_sems, recv_sems, turn):
        for step in FAR_FIRST:
            for kind in (0, 1):
                axis = kind ^ turn
                here = kind * SIDE + me[axis]
                there = kind * SIDE + place[axis][step]
                remote(
                    buffer.at[chunk, here] if source is None else source.at[chunk, there],
                    buffer.at[chunk, here],
                    send_sems.at[chunk],
                    recv_sems.at[chunk],
                    along(axis, step),
                ).start()

    def spreading(buffer, chunk, send_sems, recv_sems):
        view = buffer.at[chunk, pl.ds(0, 2 * (SIDE - 1))]
        return settle(view, send_sems.at[chunk], recv_sems.at[chunk])

    for i in range(HALF):
        spread(recv_kv, send_kv, i, kv_send, kv_recv, 0)

    load_cache.wait()
    load_new.wait()
    load_len.wait()
    parts = []
    fill = fill_ref[0]
    for block in range(cache.shape[0] // CBLK):
        rows = pl.ds(block * CBLK, CBLK)
        position = block * CBLK + lax.broadcasted_iota(jnp.int32, (PAD, CBLK), 1)
        parts.append(
            attend(my_query, cache[rows, :D_HEAD], cache[rows, D_HEAD:], position < fill)
        )
    query_full = query_f32[...]
    new_rows = new_ref[0].astype(jnp.float32)
    step_of_row = lax.broadcasted_iota(jnp.int32, (PAD, 1), 0) // GROUP
    new_scores = [
        jnp.where(
            u <= step_of_row,
            jnp.sum(query_full * new_rows[u : u + 1, :D_HEAD], axis=1, keepdims=True) * SCALE,
            NONE,
        )
        for u in range(STEPS)
    ]
    new_top = functools.reduce(jnp.maximum, new_scores)
    new_weights = [
        jnp.where(u <= step_of_row, jnp.exp(new_scores[u] - new_top), 0.0) for u in range(STEPS)
    ]
    new_output = sum(
        new_weights[u].astype(jnp.bfloat16).astype(jnp.float32) * new_rows[u : u + 1, D_HEAD:]
        for u in range(STEPS)
    )
    parts.append((new_top, sum(new_weights), new_output))
    top, total, output = merge(parts)
    row_id = lax.broadcasted_iota(jnp.int32, (PAD, D_HEAD), 0)
    lane_id = lax.broadcasted_iota(jnp.int32, (PAD, D_HEAD), 1)
    own_lane = lane_id == row_id + parity * PAD
    cache_out[...] = output / total
    own_log = jnp.sum(
        jnp.where(own_lane, top + jnp.log(total), 0.0), axis=0, keepdims=True
    )
    own_lanes = lane_id[:1] // PAD == parity
    for i in range(HALF):
        cache_log[i : i + 1] = jnp.where(
            jnp.logical_and(own_lanes, my_index == i), own_log, NONE
        )

    q_all = settle(query_all.at[pl.ds(0, SIDE - 1)], q_send, q_recv)
    q_all.wait_recv()

    span = SIDE * 16
    position_id = lax.broadcasted_iota(jnp.int32, (span, D_HEAD), 0)
    lane_kind = lax.broadcasted_iota(jnp.int32, (1, D_HEAD), 1) // PAD % 2
    positions = jnp.where(
        lane_kind == 0,
        (position_id // 16) * span + y * 16 + position_id % 16,
        z * span + position_id,
    )
    row8 = lax.broadcasted_iota(jnp.int32, (8, D_HEAD), 0)
    for i in range(HALF):
        slots = (z * SIDE + 2 * i + z % 2, (2 * i + 1 - y % 2) * SIDE + y)
        lengths = [len_ref[table_smem[0, slot]] for slot in slots]
        valid = positions < jnp.where(lane_kind == 0, lengths[0], lengths[1])
        pair = query_all[2 * i : 2 * i + 2].reshape(2 * PAD, D_HEAD)
        queries = jnp.concatenate([pair, pair], axis=0)
        spreading(recv_kv, i, kv_send, kv_recv).wait_recv()
        every = lax.dot_general(
            recv_kv[i, :, :, :D_HEAD].reshape(2 * span, D_HEAD),
            queries,
            (((1,), (1,)), ((), ())),
            preferred_element_type=jnp.float32,
        )
        scores = jnp.where(lane_kind == 0, every[:span], every[span:]) * SCALE
        own = cache_log[i : i + 1]
        top = jnp.maximum(
            jnp.max(jnp.where(valid, scores, NONE), axis=0, keepdims=True), own
        )
        weights = jnp.where(valid, jnp.exp(scores - top), 0.0)
        own_weight = jnp.exp(own - top)
        total = jnp.sum(weights, axis=0, keepdims=True) + own_weight
        share = 1.0 / total
        shares = (weights * share).T.astype(jnp.bfloat16)
        outputs = [
            jnp.dot(
                shares[kind * PAD : (kind + 1) * PAD],
                recv_kv[i, kind * SIDE : (kind + 1) * SIDE, :, D_HEAD:].reshape(span, D_HEAD),
                preferred_element_type=jnp.float32,
            )[:ROWS]
            for kind in (0, 1)
        ]
        own_column = jnp.sum(
            jnp.where(own_lane, own_weight * share, 0.0), axis=1, keepdims=True
        )
        own_part = (own_column * cache_out[...])[:ROWS]
        line = top + jnp.log(total)
        first = line.astype(jnp.bfloat16).astype(jnp.float32)
        second = (line - first).astype(jnp.bfloat16).astype(jnp.float32)
        third = line - first - second
        lines = jnp.where(
            row8 == 0,
            first,
            jnp.where(row8 == 1, second, jnp.where(row8 == 2, third, 0.0)),
        )
        for kind in (0, 1):
            output = outputs[kind] + jnp.where(mine == 2 * i + kind, own_part, 0.0)
            pieces[i, kind * SIDE + me[1 - kind]] = jnp.concatenate(
                [output, lines], axis=0
            ).astype(jnp.bfloat16)
        spread(pieces, None, i, o_send, o_recv, 1)

    q_all.wait_send()
    for i in range(HALF):
        spreading(recv_kv, i, kv_send, kv_recv).wait_send()
    done = []
    for i in range(HALF):
        spreading(pieces, i, o_send, o_recv).wait_recv()
        arrived = [
            [pieces[i, kind * SIDE + src].astype(jnp.float32) for src in range(SIDE)]
            for kind in (0, 1)
        ]
        logs = [
            jnp.concatenate([jnp.sum(a[ROWS:], axis=0, keepdims=True) for a in some], axis=0)
            for some in arrived
        ]
        logs = jnp.where(lane_kind == 0, logs[0], logs[1])
        weights = jnp.exp(logs - jnp.max(logs, axis=0, keepdims=True))
        weights = weights / jnp.sum(weights, axis=0, keepdims=True)
        columns = jnp.concatenate(
            [weights, jnp.zeros((D_HEAD - SIDE, D_HEAD), jnp.float32)], axis=0
        ).T
        for kind in (0, 1):
            acc = None
            for src in range(SIDE):
                term = (
                    columns[kind * PAD : kind * PAD + ROWS, src : src + 1]
                    * arrived[kind][src][:ROWS]
                )
                acc = term if acc is None else acc + term
            done.append(acc)
        if len(done) == 2 * PAIR:
            turn = i // PAIR
            for kind in (0, 1):
                gathered[turn, kind * SIDE + me[kind]] = jnp.concatenate(
                    done[kind::2], axis=0
                ).astype(jnp.bfloat16)
            spread(gathered, None, turn, g_send, g_recv, 0)
            done = []

    load_weight.wait()
    for i in range(HALF):
        spreading(pieces, i, o_send, o_recv).wait_send()
    per_chunk = n_tracks // ROUNDS
    lane = lax.broadcasted_iota(jnp.int32, (per_chunk, 128), 1)
    for chunk in range(ROUNDS):
        spreading(gathered, chunk, g_send, g_recv).wait_recv()
        stage[pl.ds(chunk * per_chunk * ROWS, per_chunk * ROWS), :] = (
            gathered[chunk].astype(jnp.float32).reshape(per_chunk * ROWS, D_HEAD)
        )
        product = None
        for g in range(GROUP):
            left = jnp.concatenate(
                [
                    stage[
                        pl.ds(chunk * per_chunk * ROWS + t * GROUP + g, per_chunk, stride=ROWS), :
                    ]
                    for t in range(STEPS)
                ],
                axis=0,
            ).astype(jnp.bfloat16)
            term = lax.dot_general(
                left,
                weight[:, g * D_HEAD : (g + 1) * D_HEAD],
                (((1,), (1,)), ((), ())),
                preferred_element_type=jnp.float32,
            )
            product = term if product is None else product + term
        parts = [product[t * per_chunk : (t + 1) * per_chunk] for t in range(STEPS)]
        middle = pltpu.roll(parts[1], width, 1)
        last = pltpu.roll(parts[2], 2 * width - 128, 1)
        sums[chunk, head, :, :128] = jnp.where(lane < width, parts[0], middle).astype(jnp.bfloat16)
        sums[chunk, head, :, 128:] = jnp.where(lane < 2 * width - 128, middle, last).astype(
            jnp.bfloat16
        )
        for step in HEAD_ORDER:
            remote(
                sums.at[chunk, head],
                sums.at[chunk, head],
                s_send.at[chunk],
                s_recv.at[chunk],
                head_peer(step),
            ).start()
    for chunk in range(ROUNDS):
        spreading(gathered, chunk, g_send, g_recv).wait_send()

    def summing(chunk):
        view = sums.at[chunk, pl.ds(0, n_heads - 1)]
        return settle(view, s_send.at[chunk], s_recv.at[chunk])

    decoded = None
    for chunk in range(ROUNDS):
        summing(chunk).wait_recv()
        summed = sums[chunk, 0].astype(jnp.float32)
        for there in range(1, n_heads):
            summed = summed + sums[chunk, there].astype(jnp.float32)
        term = jnp.dot(
            pick[:, chunk * per_chunk : (chunk + 1) * per_chunk],
            summed.astype(jnp.bfloat16),
            preferred_element_type=jnp.float32,
        )
        decoded = term if decoded is None else decoded + term
    lane = lax.broadcasted_iota(jnp.int32, (n_tracks, 128), 1)
    left, right = decoded[:, :128], decoded[:, 128:]
    split = 128 - width
    middle = jnp.where(lane < split, pltpu.roll(left, split, 1), pltpu.roll(right, split, 1))
    last = pltpu.roll(right, 256 - 2 * width, 1)
    for t, rows in enumerate((left, middle, last)):
        out_ref[t * n_tracks : (t + 1) * n_tracks] = rows[:, :width].astype(out_ref.dtype)

    for chunk in range(ROUNDS):
        summing(chunk).wait_send()


def shards(queries, new_kv, cache_kv, cache_fill, fresh_kv, fresh_len, owner_slot, out_weight):
    n_tracks, depth = fresh_kv.shape[0], fresh_kv.shape[1]
    width = out_weight.shape[1]
    vmem = pl.BlockSpec(memory_space=pltpu.VMEM)
    hbm = pl.BlockSpec(memory_space=pltpu.HBM)
    bf16, f32 = jnp.bfloat16, jnp.float32
    dma = pltpu.SemaphoreType.DMA
    out = pl.pallas_call(
        kernel,
        name="handoff_decode",
        out_shape=pltpu.VMEM((n_tracks * STEPS, width), bf16),
        in_specs=[pl.BlockSpec(memory_space=pltpu.SMEM)] + [hbm] * 7,
        out_specs=vmem,
        scratch_shapes=[
            pltpu.VMEM((1, n_tracks), jnp.int32),
            pltpu.SMEM((n_tracks,), jnp.int32),
            pltpu.VMEM(queries.shape, bf16),
            pltpu.VMEM(new_kv.shape, bf16),
            pltpu.VMEM(cache_kv.shape[1:], bf16),
            pltpu.VMEM(fresh_kv.shape, bf16),
            pltpu.VMEM((128, out_weight.shape[0]), bf16),
            pltpu.VMEM((1, n_tracks), jnp.int32),
            pltpu.SMEM((1, n_tracks), jnp.int32),
            pltpu.VMEM((PAD, D_HEAD), f32),
            pltpu.VMEM((2 * HALF, PAD, D_HEAD), bf16),
            pltpu.VMEM((HALF, 2 * SIDE, depth, 2 * D_HEAD), bf16),
            pltpu.VMEM((HALF, 2 * SIDE, depth, 2 * D_HEAD), bf16),
            pltpu.VMEM((PAD, D_HEAD), f32),
            pltpu.VMEM((8, D_HEAD), f32),
            pltpu.VMEM((HALF, 2 * SIDE, PIECE, D_HEAD), bf16),
            pltpu.VMEM((ROUNDS, 2 * SIDE, BAND, D_HEAD), bf16),
            pltpu.VMEM(((n_tracks + 1) * ROWS, D_HEAD), f32),
            pltpu.VMEM((ROUNDS, 8, n_tracks // ROUNDS, 256), bf16),
            pltpu.VMEM((n_tracks, n_tracks), bf16),
            dma((8,)),
            dma,
            dma,
            dma((HALF,)),
            dma((HALF,)),
            dma((HALF,)),
            dma((HALF,)),
            dma((ROUNDS,)),
            dma((ROUNDS,)),
            dma((ROUNDS,)),
            dma((ROUNDS,)),
        ],
        compiler_params=pltpu.CompilerParams(
            collective_id=0, has_side_effects=True, vmem_limit_bytes=32 * 1024 * 1024
        ),
    )(
        cache_fill,
        *(
            pltpu.with_memory_space_constraint(operand, pltpu.HBM)
            for operand in (
                owner_slot[None, :],
                fresh_len,
                queries,
                new_kv,
                cache_kv[0],
                fresh_kv,
                out_weight.T,
            )
        )
    )
    return out.reshape(STEPS, n_tracks, width).transpose(1, 0, 2)


def solution(mesh):
    in_specs = (
        P("stream", None, "head"),
        P("stream", None, "head"),
        P("stream", None, "head"),
        P("stream"),
        P(None, "stream", "head"),
        P(),
        P(),
        P("head", "stream"),
    )
    out_specs = P(None, None, "stream")
    return jax.shard_map(shards, mesh=mesh, in_specs=in_specs, out_specs=out_specs, check_vma=False)
```

```python
import functools

import jax
import jax.numpy as jnp
from jax import lax
from jax.experimental import pallas as pl
from jax.experimental.pallas import tpu as pltpu
from jax.sharding import PartitionSpec as P

D_HEAD = 128
GROUP = 8
STEPS = 3
ROWS = STEPS * GROUP
PAD = 32
CBLK = 512
SIDE = 8
HALF = 4
PIECE = PAD
PAIR = 2
ROUNDS = HALF // PAIR
BAND = PAIR * ROWS
NONE = -1e30
SCALE = D_HEAD**-0.5
FAR_FIRST = (4, 3, 5, 2, 6, 1, 7)
HEAD_ORDER = (4, 5, 2, 3, 6, 7, 1)
MESH = pl.DeviceIdType.MESH


def remote(src, dst, send_sem, recv_sem, device):
    return pltpu.make_async_remote_copy(
        src_ref=src,
        dst_ref=dst,
        send_sem=send_sem,
        recv_sem=recv_sem,
        device_id=device,
        device_id_type=MESH,
    )


def attend(query_rows, keys, values, valid):
    scores = (
        lax.dot_general(
            query_rows, keys, (((1,), (1,)), ((), ())), preferred_element_type=jnp.float32
        )
        * SCALE
    )
    highest = jnp.max(jnp.where(valid, scores, NONE), axis=1, keepdims=True)
    weights = jnp.where(valid, jnp.exp(scores - highest), 0.0)
    total = jnp.sum(weights, axis=1, keepdims=True)
    output = jnp.dot(weights.astype(jnp.bfloat16), values, preferred_element_type=jnp.float32)
    return highest, total, output


def merge(parts):
    top = functools.reduce(jnp.maximum, [part[0] for part in parts])
    factors = [jnp.exp(part[0] - top) for part in parts]
    total = sum(f * part[1] for f, part in zip(factors, parts))
    output = sum(f * part[2] for f, part in zip(factors, parts))
    return top, total, output


def kernel(
    fill_ref,
    owner_hbm,
    len_hbm,
    query_hbm,
    new_hbm,
    cache_hbm,
    fresh_hbm,
    weight_hbm,
    out_ref,
    owner_row_ref,
    len_ref,
    query_ref,
    new_ref,
    cache,
    fresh,
    weight,
    table,
    table_smem,
    query_f32,
    query_all,
    send_kv,
    recv_kv,
    cache_out,
    cache_log,
    pieces,
    gathered,
    stage,
    sums,
    pick,
    local_sem,
    q_send,
    q_recv,
    kv_send,
    kv_recv,
    o_send,
    o_recv,
    g_send,
    g_recv,
    s_send,
    s_recv,
):
    stream = lax.axis_index("stream")
    head = lax.axis_index("head")
    z, y = stream // SIDE, stream % SIDE
    n_heads = 8
    me = (z, y)

    place = [[lax.rem(me[axis] + step, SIDE) for step in range(SIDE)] for axis in (0, 1)]
    device = [
        [place[0][step] * SIDE + y for step in range(SIDE)],
        [z * SIDE + place[1][step] for step in range(SIDE)],
    ]

    def along(axis, step):
        return {"stream": device[axis][step]}

    def head_peer(step):
        return {"head": lax.rem(head + step, n_heads)}

    any_peer = head_peer(1)

    load_owner = pltpu.make_async_copy(owner_hbm, owner_row_ref, local_sem.at[0])
    load_owner.start()
    barrier = pltpu.get_barrier_semaphore()
    peers = [along(axis, step) for step in FAR_FIRST for axis in (0, 1)]
    peers += [head_peer(step) for step in range(1, n_heads)]
    for peer in peers:
        pl.semaphore_signal(barrier, inc=1, device_id=peer, device_id_type=MESH)

    loads = [
        pltpu.make_async_copy(src, dst, local_sem.at[1 + n])
        for n, (src, dst) in enumerate(
            (
                (fresh_hbm, fresh),
                (query_hbm, query_ref),
                (new_hbm, new_ref),
                (cache_hbm, cache),
                (len_hbm, len_ref),
                (weight_hbm, weight.at[pl.ds(0, weight_hbm.shape[0])]),
            )
        )
    ]
    for load in loads:
        load.start()
    load_fresh, load_query, load_new, load_cache, load_len, load_weight = loads

    n_tracks = owner_row_ref.shape[1]
    load_owner.wait()
    owner = owner_row_ref[...]
    slot_of = lax.broadcasted_iota(jnp.int32, (n_tracks, n_tracks), 0)
    lane_of = lax.broadcasted_iota(jnp.int32, (n_tracks, n_tracks), 1)
    track_column = jnp.max(jnp.where(owner == slot_of, lane_of, 0), axis=1, keepdims=True)
    track_row = jnp.max(jnp.where(slot_of == lane_of, track_column, 0), axis=0, keepdims=True)
    owner_z, owner_y = owner // SIDE, owner % SIDE
    place_row = jnp.where(
        (owner_z + owner_y) % 2 == 0,
        owner_y // 4 * 32 + owner_z * PAIR + owner_y // 2 % PAIR,
        owner_z // 4 * 32 + 16 + owner_y * PAIR + owner_z // 2 % PAIR,
    )
    table[...] = track_row
    load_table = pltpu.make_async_copy(table, table_smem, local_sem.at[7])
    load_table.start()
    per_chunk = n_tracks // ROUNDS
    term_of = lax.broadcasted_iota(jnp.int32, (n_heads * per_chunk, n_tracks), 0) % per_chunk
    for chunk in range(ROUNDS):
        picked = term_of + chunk * per_chunk == place_row
        pick[chunk] = picked.astype(jnp.float32).T.astype(jnp.bfloat16)

    query_f32[...] = jnp.zeros_like(query_f32)
    load_query.wait()
    query_flat = query_ref[0].astype(jnp.float32)
    for g in range(GROUP):
        query_f32[pl.ds(g, STEPS, stride=GROUP), :] = query_flat[
            :, g * D_HEAD : (g + 1) * D_HEAD
        ]
    parity = (z + y) % 2
    my_index = jnp.where(parity == 0, y // 2, z // 2)
    mine = my_index * 2 + parity
    my_query = query_f32[...].astype(jnp.bfloat16)
    query_all[mine] = my_query
    width = weight_hbm.shape[0]
    weight[width:] = jnp.zeros((weight.shape[0] - width, weight.shape[1]), weight.dtype)

    load_table.wait()
    load_fresh.wait()

    def slot_at(kind, p, i):
        if kind == 0:
            return p * SIDE + 2 * i + p % 2
        return (2 * i + 1 - p % 2) * SIDE + p

    for i in range(HALF):
        for kind in (0, 1):
            for p in range(SIDE):
                send_kv[i, kind * SIDE + p] = fresh[table_smem[0, slot_at(kind, p, i)]]
    for i in range(HALF):
        for kind in (0, 1):
            here = kind * SIDE + me[kind]
            recv_kv[i, here] = send_kv[i, here]

    pl.semaphore_wait(barrier, len(peers))

    def settle(view, send_sem, recv_sem):
        return remote(view, view, send_sem, recv_sem, any_peer)

    for step in FAR_FIRST:
        peer = {"stream": jnp.where(parity == 0, device[1][step], device[0][step])}
        remote(query_all.at[mine], query_all.at[mine], q_send, q_recv, peer).start()

    def spread(buffer, source, chunk, send_sems, recv_sems, turn):
        for step in FAR_FIRST:
            for kind in (0, 1):
                axis = kind ^ turn
                here = kind * SIDE + me[axis]
                there = kind * SIDE + place[axis][step]
                remote(
                    buffer.at[chunk, here] if source is None else source.at[chunk, there],
                    buffer.at[chunk, here],
                    send_sems.at[chunk],
                    recv_sems.at[chunk],
                    along(axis, step),
                ).start()

    def spreading(buffer, chunk, send_sems, recv_sems):
        view = buffer.at[chunk, pl.ds(0, 2 * (SIDE - 1))]
        return settle(view, send_sems.at[chunk], recv_sems.at[chunk])

    for i in range(HALF):
        spread(recv_kv, send_kv, i, kv_send, kv_recv, 0)

    load_cache.wait()
    load_new.wait()
    load_len.wait()
    parts = []
    fill = fill_ref[0]
    for block in range(cache.shape[0] // CBLK):
        rows = pl.ds(block * CBLK, CBLK)
        position = block * CBLK + lax.broadcasted_iota(jnp.int32, (PAD, CBLK), 1)
        parts.append(
            attend(my_query, cache[rows, :D_HEAD], cache[rows, D_HEAD:], position < fill)
        )
    query_full = query_f32[...]
    new_rows = new_ref[0].astype(jnp.float32)
    step_of_row = lax.broadcasted_iota(jnp.int32, (PAD, 1), 0) // GROUP
    new_scores = [
        jnp.where(
            u <= step_of_row,
            jnp.sum(query_full * new_rows[u : u + 1, :D_HEAD], axis=1, keepdims=True) * SCALE,
            NONE,
        )
        for u in range(STEPS)
    ]
    new_top = functools.reduce(jnp.maximum, new_scores)
    new_weights = [
        jnp.where(u <= step_of_row, jnp.exp(new_scores[u] - new_top), 0.0) for u in range(STEPS)
    ]
    new_output = sum(
        new_weights[u].astype(jnp.bfloat16).astype(jnp.float32) * new_rows[u : u + 1, D_HEAD:]
        for u in range(STEPS)
    )
    parts.append((new_top, sum(new_weights), new_output))
    top, total, output = merge(parts)
    row_id = lax.broadcasted_iota(jnp.int32, (PAD, D_HEAD), 0)
    lane_id = lax.broadcasted_iota(jnp.int32, (PAD, D_HEAD), 1)
    own_lane = lane_id == row_id + parity * PAD
    cache_out[...] = output / total
    own_log = jnp.sum(
        jnp.where(own_lane, top + jnp.log(total), 0.0), axis=0, keepdims=True
    )
    own_lanes = lane_id[:1] // PAD == parity
    for i in range(HALF):
        cache_log[i : i + 1] = jnp.where(
            jnp.logical_and(own_lanes, my_index == i), own_log, NONE
        )

    q_all = settle(query_all.at[pl.ds(0, SIDE - 1)], q_send, q_recv)
    q_all.wait_recv()

    span = SIDE * 16
    position_id = lax.broadcasted_iota(jnp.int32, (span, D_HEAD), 0)
    lane_kind = lax.broadcasted_iota(jnp.int32, (1, D_HEAD), 1) // PAD % 2
    positions = jnp.where(
        lane_kind == 0,
        (position_id // 16) * span + y * 16 + position_id % 16,
        z * span + position_id,
    )
    row8 = lax.broadcasted_iota(jnp.int32, (8, D_HEAD), 0)
    for i in range(HALF):
        slots = (z * SIDE + 2 * i + z % 2, (2 * i + 1 - y % 2) * SIDE + y)
        lengths = [len_ref[table_smem[0, slot]] for slot in slots]
        valid = positions < jnp.where(lane_kind == 0, lengths[0], lengths[1])
        pair = query_all[2 * i : 2 * i + 2].reshape(2 * PAD, D_HEAD)
        queries = jnp.concatenate([pair, pair], axis=0)
        spreading(recv_kv, i, kv_send, kv_recv).wait_recv()
        every = lax.dot_general(
            recv_kv[i, :, :, :D_HEAD].reshape(2 * span, D_HEAD),
            queries,
            (((1,), (1,)), ((), ())),
            preferred_element_type=jnp.float32,
        )
        scores = jnp.where(lane_kind == 0, every[:span], every[span:]) * SCALE
        own = cache_log[i : i + 1]
        top = jnp.maximum(
            jnp.max(jnp.where(valid, scores, NONE), axis=0, keepdims=True), own
        )
        weights = jnp.where(valid, jnp.exp(scores - top), 0.0)
        own_weight = jnp.exp(own - top)
        total = jnp.sum(weights, axis=0, keepdims=True) + own_weight
        share = 1.0 / total
        shares = (weights * share).T.astype(jnp.bfloat16)
        outputs = [
            jnp.dot(
                shares[kind * PAD : (kind + 1) * PAD],
                recv_kv[i, kind * SIDE : (kind + 1) * SIDE, :, D_HEAD:].reshape(span, D_HEAD),
                preferred_element_type=jnp.float32,
            )[:ROWS]
            for kind in (0, 1)
        ]
        own_column = jnp.sum(
            jnp.where(own_lane, own_weight * share, 0.0), axis=1, keepdims=True
        )
        own_part = (own_column * cache_out[...])[:ROWS]
        line = top + jnp.log(total)
        first = line.astype(jnp.bfloat16).astype(jnp.float32)
        second = (line - first).astype(jnp.bfloat16).astype(jnp.float32)
        third = line - first - second
        lines = jnp.where(
            row8 == 0,
            first,
            jnp.where(row8 == 1, second, jnp.where(row8 == 2, third, 0.0)),
        )
        for kind in (0, 1):
            output = outputs[kind] + jnp.where(mine == 2 * i + kind, own_part, 0.0)
            pieces[i, kind * SIDE + me[1 - kind]] = jnp.concatenate(
                [output, lines], axis=0
            ).astype(jnp.bfloat16)
        spread(pieces, None, i, o_send, o_recv, 1)

    q_all.wait_send()
    for i in range(HALF):
        spreading(recv_kv, i, kv_send, kv_recv).wait_send()
    done = []
    for i in range(HALF):
        spreading(pieces, i, o_send, o_recv).wait_recv()
        arrived = [
            [pieces[i, kind * SIDE + src].astype(jnp.float32) for src in range(SIDE)]
            for kind in (0, 1)
        ]
        logs = [
            jnp.concatenate([jnp.sum(a[ROWS:], axis=0, keepdims=True) for a in some], axis=0)
            for some in arrived
        ]
        logs = jnp.where(lane_kind == 0, logs[0], logs[1])
        weights = jnp.exp(logs - jnp.max(logs, axis=0, keepdims=True))
        weights = weights / jnp.sum(weights, axis=0, keepdims=True)
        columns = jnp.concatenate(
            [weights, jnp.zeros((D_HEAD - SIDE, D_HEAD), jnp.float32)], axis=0
        ).T
        for kind in (0, 1):
            acc = None
            for src in range(SIDE):
                term = (
                    columns[kind * PAD : kind * PAD + ROWS, src : src + 1]
                    * arrived[kind][src][:ROWS]
                )
                acc = term if acc is None else acc + term
            done.append(acc)
        if len(done) == 2 * PAIR:
            turn = i // PAIR
            for kind in (0, 1):
                gathered[turn, kind * SIDE + me[kind]] = jnp.concatenate(
                    done[kind::2], axis=0
                ).astype(jnp.bfloat16)
            spread(gathered, None, turn, g_send, g_recv, 0)
            done = []

    load_weight.wait()
    for i in range(HALF):
        spreading(pieces, i, o_send, o_recv).wait_send()
    lane = lax.broadcasted_iota(jnp.int32, (per_chunk, 128), 1)
    for chunk in range(ROUNDS):
        spreading(gathered, chunk, g_send, g_recv).wait_recv()
        stage[pl.ds(chunk * per_chunk * ROWS, per_chunk * ROWS), :] = (
            gathered[chunk].astype(jnp.float32).reshape(per_chunk * ROWS, D_HEAD)
        )
        product = None
        for g in range(GROUP):
            left = jnp.concatenate(
                [
                    stage[
                        pl.ds(chunk * per_chunk * ROWS + t * GROUP + g, per_chunk, stride=ROWS), :
                    ]
                    for t in range(STEPS)
                ],
                axis=0,
            ).astype(jnp.bfloat16)
            term = lax.dot_general(
                left,
                weight[:, g * D_HEAD : (g + 1) * D_HEAD],
                (((1,), (1,)), ((), ())),
                preferred_element_type=jnp.float32,
            )
            product = term if product is None else product + term
        parts = [product[t * per_chunk : (t + 1) * per_chunk] for t in range(STEPS)]
        middle = pltpu.roll(parts[1], width, 1)
        last = pltpu.roll(parts[2], 2 * width - 128, 1)
        sums[chunk, head, :, :128] = jnp.where(lane < width, parts[0], middle).astype(jnp.bfloat16)
        sums[chunk, head, :, 128:] = jnp.where(lane < 2 * width - 128, middle, last).astype(
            jnp.bfloat16
        )
        for step in HEAD_ORDER:
            remote(
                sums.at[chunk, head],
                sums.at[chunk, head],
                s_send.at[chunk],
                s_recv.at[chunk],
                head_peer(step),
            ).start()
    for chunk in range(ROUNDS):
        spreading(gathered, chunk, g_send, g_recv).wait_send()

    def summing(chunk):
        view = sums.at[chunk, pl.ds(0, n_heads - 1)]
        return settle(view, s_send.at[chunk], s_recv.at[chunk])

    decoded = None
    for chunk in range(ROUNDS):
        summing(chunk).wait_recv()
        term = jnp.dot(
            pick[chunk],
            sums[chunk].reshape(n_heads * per_chunk, sums.shape[3]),
            preferred_element_type=jnp.float32,
        )
        decoded = term if decoded is None else decoded + term
    lane = lax.broadcasted_iota(jnp.int32, (n_tracks, 128), 1)
    left, right = decoded[:, :128], decoded[:, 128:]
    split = 128 - width
    middle = jnp.where(lane < split, pltpu.roll(left, split, 1), pltpu.roll(right, split, 1))
    last = pltpu.roll(right, 256 - 2 * width, 1)
    for t, rows in enumerate((left, middle, last)):
        out_ref[t * n_tracks : (t + 1) * n_tracks] = rows[:, :width].astype(out_ref.dtype)

    for chunk in range(ROUNDS):
        summing(chunk).wait_send()


def shards(queries, new_kv, cache_kv, cache_fill, fresh_kv, fresh_len, owner_slot, out_weight):
    n_tracks, depth = fresh_kv.shape[0], fresh_kv.shape[1]
    width = out_weight.shape[1]
    vmem = pl.BlockSpec(memory_space=pltpu.VMEM)
    hbm = pl.BlockSpec(memory_space=pltpu.HBM)
    bf16, f32 = jnp.bfloat16, jnp.float32
    dma = pltpu.SemaphoreType.DMA
    out = pl.pallas_call(
        kernel,
        name="handoff_decode",
        out_shape=pltpu.VMEM((n_tracks * STEPS, width), bf16),
        in_specs=[pl.BlockSpec(memory_space=pltpu.SMEM)] + [hbm] * 7,
        out_specs=vmem,
        scratch_shapes=[
            pltpu.VMEM((1, n_tracks), jnp.int32),
            pltpu.SMEM((n_tracks,), jnp.int32),
            pltpu.VMEM(queries.shape, bf16),
            pltpu.VMEM(new_kv.shape, bf16),
            pltpu.VMEM(cache_kv.shape[1:], bf16),
            pltpu.VMEM(fresh_kv.shape, bf16),
            pltpu.VMEM((128, out_weight.shape[0]), bf16),
            pltpu.VMEM((1, n_tracks), jnp.int32),
            pltpu.SMEM((1, n_tracks), jnp.int32),
            pltpu.VMEM((PAD, D_HEAD), f32),
            pltpu.VMEM((2 * HALF, PAD, D_HEAD), bf16),
            pltpu.VMEM((HALF, 2 * SIDE, depth, 2 * D_HEAD), bf16),
            pltpu.VMEM((HALF, 2 * SIDE, depth, 2 * D_HEAD), bf16),
            pltpu.VMEM((PAD, D_HEAD), f32),
            pltpu.VMEM((8, D_HEAD), f32),
            pltpu.VMEM((HALF, 2 * SIDE, PIECE, D_HEAD), bf16),
            pltpu.VMEM((ROUNDS, 2 * SIDE, BAND, D_HEAD), bf16),
            pltpu.VMEM(((n_tracks + 1) * ROWS, D_HEAD), f32),
            pltpu.VMEM((ROUNDS, 8, n_tracks // ROUNDS, 256), bf16),
            pltpu.VMEM((ROUNDS, n_tracks, 8 * n_tracks // ROUNDS), bf16),
            dma((8,)),
            dma,
            dma,
            dma((HALF,)),
            dma((HALF,)),
            dma((HALF,)),
            dma((HALF,)),
            dma((ROUNDS,)),
            dma((ROUNDS,)),
            dma((ROUNDS,)),
            dma((ROUNDS,)),
        ],
        compiler_params=pltpu.CompilerParams(
            collective_id=0, has_side_effects=True, vmem_limit_bytes=32 * 1024 * 1024
        ),
    )(
        cache_fill,
        *(
            pltpu.with_memory_space_constraint(operand, pltpu.HBM)
            for operand in (
                owner_slot[None, :],
                fresh_len,
                queries,
                new_kv,
                cache_kv[0],
                fresh_kv,
                out_weight.T,
            )
        )
    )
    return out.reshape(STEPS, n_tracks, width).transpose(1, 0, 2)


def solution(mesh):
    in_specs = (
        P("stream", None, "head"),
        P("stream", None, "head"),
        P("stream", None, "head"),
        P("stream"),
        P(None, "stream", "head"),
        P(),
        P(),
        P("head", "stream"),
    )
    out_specs = P(None, None, "stream")
    return jax.shard_map(shards, mesh=mesh, in_specs=in_specs, out_specs=out_specs, check_vma=False)
```

```python
import functools

import jax
import jax.numpy as jnp
from jax import lax
from jax.experimental import pallas as pl
from jax.experimental.pallas import tpu as pltpu
from jax.sharding import PartitionSpec as P

D_HEAD = 128
GROUP = 8
STEPS = 3
ROWS = STEPS * GROUP
PAD = 32
CBLK = 512
SIDE = 8
HALF = 4
PIECE = PAD
PAIR = 2
ROUNDS = HALF // PAIR
BAND = PAIR * ROWS
NONE = -1e30
SCALE = D_HEAD**-0.5
FAR_FIRST = (4, 3, 5, 2, 6, 1, 7)
HEAD_ORDER = (4, 5, 2, 3, 6, 7, 1)
MESH = pl.DeviceIdType.MESH


def remote(src, dst, send_sem, recv_sem, device):
    return pltpu.make_async_remote_copy(
        src_ref=src,
        dst_ref=dst,
        send_sem=send_sem,
        recv_sem=recv_sem,
        device_id=device,
        device_id_type=MESH,
    )


def attend(query_rows, keys, values, valid):
    scores = (
        lax.dot_general(
            query_rows, keys, (((1,), (1,)), ((), ())), preferred_element_type=jnp.float32
        )
        * SCALE
    )
    highest = jnp.max(jnp.where(valid, scores, NONE), axis=1, keepdims=True)
    weights = jnp.where(valid, jnp.exp(scores - highest), 0.0)
    total = jnp.sum(weights, axis=1, keepdims=True)
    output = jnp.dot(weights.astype(jnp.bfloat16), values, preferred_element_type=jnp.float32)
    return highest, total, output


def merge(parts):
    top = functools.reduce(jnp.maximum, [part[0] for part in parts])
    factors = [jnp.exp(part[0] - top) for part in parts]
    total = sum(f * part[1] for f, part in zip(factors, parts))
    output = sum(f * part[2] for f, part in zip(factors, parts))
    return top, total, output


def kernel(
    fill_ref,
    owner_hbm,
    len_hbm,
    query_hbm,
    new_hbm,
    cache_hbm,
    fresh_hbm,
    weight_hbm,
    out_ref,
    owner_row_ref,
    len_ref,
    query_ref,
    new_ref,
    cache,
    fresh,
    weight,
    table,
    table_smem,
    query_f32,
    query_all,
    send_kv,
    recv_kv,
    cache_out,
    cache_log,
    pieces,
    gathered,
    stage,
    sums,
    pick,
    local_sem,
    q_send,
    q_recv,
    kv_send,
    kv_recv,
    o_send,
    o_recv,
    g_send,
    g_recv,
    s_send,
    s_recv,
):
    stream = lax.axis_index("stream")
    head = lax.axis_index("head")
    z, y = stream // SIDE, stream % SIDE
    n_heads = 8
    me = (z, y)

    place = [[lax.rem(me[axis] + step, SIDE) for step in range(SIDE)] for axis in (0, 1)]
    device = [
        [place[0][step] * SIDE + y for step in range(SIDE)],
        [z * SIDE + place[1][step] for step in range(SIDE)],
    ]

    def along(axis, step):
        return {"stream": device[axis][step]}

    def head_peer(step):
        return {"head": lax.rem(head + step, n_heads)}

    any_peer = head_peer(1)

    load_owner = pltpu.make_async_copy(owner_hbm, owner_row_ref, local_sem.at[0])
    load_owner.start()
    barrier = pltpu.get_barrier_semaphore()
    peers = [along(axis, step) for step in FAR_FIRST for axis in (0, 1)]
    peers += [head_peer(step) for step in range(1, n_heads)]
    for peer in peers:
        pl.semaphore_signal(barrier, inc=1, device_id=peer, device_id_type=MESH)

    loads = [
        pltpu.make_async_copy(src, dst, local_sem.at[1 + n])
        for n, (src, dst) in enumerate(
            (
                (fresh_hbm, fresh),
                (query_hbm, query_ref),
                (new_hbm, new_ref),
                (cache_hbm, cache),
                (len_hbm, len_ref),
                (weight_hbm, weight.at[pl.ds(0, weight_hbm.shape[0])]),
            )
        )
    ]
    for load in loads:
        load.start()
    load_fresh, load_query, load_new, load_cache, load_len, load_weight = loads

    n_tracks = owner_row_ref.shape[1]
    load_owner.wait()
    owner = owner_row_ref[...]
    slot_of = lax.broadcasted_iota(jnp.int32, (n_tracks, n_tracks), 0)
    lane_of = lax.broadcasted_iota(jnp.int32, (n_tracks, n_tracks), 1)
    track_column = jnp.max(jnp.where(owner == slot_of, lane_of, 0), axis=1, keepdims=True)
    track_row = jnp.max(jnp.where(slot_of == lane_of, track_column, 0), axis=0, keepdims=True)
    owner_z, owner_y = owner // SIDE, owner % SIDE
    place_row = jnp.where(
        (owner_z + owner_y) % 2 == 0,
        owner_y // 4 * 32 + owner_z * PAIR + owner_y // 2 % PAIR,
        owner_z // 4 * 32 + 16 + owner_y * PAIR + owner_z // 2 % PAIR,
    )
    table[...] = track_row
    load_table = pltpu.make_async_copy(table, table_smem, local_sem.at[7])
    load_table.start()
    picked = slot_of == place_row
    pick[...] = picked.astype(jnp.float32).T.astype(jnp.bfloat16)

    query_f32[...] = jnp.zeros_like(query_f32)
    load_query.wait()
    query_flat = query_ref[0].astype(jnp.float32)
    for g in range(GROUP):
        query_f32[pl.ds(g, STEPS, stride=GROUP), :] = query_flat[
            :, g * D_HEAD : (g + 1) * D_HEAD
        ]
    parity = (z + y) % 2
    my_index = jnp.where(parity == 0, y // 2, z // 2)
    mine = my_index * 2 + parity
    my_query = query_f32[...].astype(jnp.bfloat16)
    query_all[mine] = my_query
    width = weight_hbm.shape[0]
    weight[width:] = jnp.zeros((weight.shape[0] - width, weight.shape[1]), weight.dtype)

    load_table.wait()
    load_fresh.wait()

    def slot_at(kind, p, i):
        if kind == 0:
            return p * SIDE + 2 * i + p % 2
        return (2 * i + 1 - p % 2) * SIDE + p

    for i in range(HALF):
        for kind in (0, 1):
            for p in range(SIDE):
                send_kv[i, kind * SIDE + p] = fresh[table_smem[0, slot_at(kind, p, i)]]
    for i in range(HALF):
        for kind in (0, 1):
            here = kind * SIDE + me[kind]
            recv_kv[i, here] = send_kv[i, here]

    pl.semaphore_wait(barrier, len(peers))

    def settle(view, send_sem, recv_sem):
        return remote(view, view, send_sem, recv_sem, any_peer)

    for step in FAR_FIRST:
        peer = {"stream": jnp.where(parity == 0, device[1][step], device[0][step])}
        remote(query_all.at[mine], query_all.at[mine], q_send, q_recv, peer).start()

    def spread(buffer, source, chunk, send_sems, recv_sems, turn, kinds=(0, 1)):
        for step in FAR_FIRST:
            for kind in kinds:
                axis = kind ^ turn
                here = kind * SIDE + me[axis]
                there = kind * SIDE + place[axis][step]
                remote(
                    buffer.at[chunk, here] if source is None else source.at[chunk, there],
                    buffer.at[chunk, here],
                    send_sems.at[chunk],
                    recv_sems.at[chunk],
                    along(axis, step),
                ).start()

    def spreading(buffer, chunk, send_sems, recv_sems):
        view = buffer.at[chunk, pl.ds(0, 2 * (SIDE - 1))]
        return settle(view, send_sems.at[chunk], recv_sems.at[chunk])

    for i in range(HALF):
        spread(recv_kv, send_kv, i, kv_send, kv_recv, 0)

    load_cache.wait()
    load_new.wait()
    load_len.wait()
    parts = []
    fill = fill_ref[0]
    for block in range(cache.shape[0] // CBLK):
        rows = pl.ds(block * CBLK, CBLK)
        position = block * CBLK + lax.broadcasted_iota(jnp.int32, (PAD, CBLK), 1)
        parts.append(
            attend(my_query, cache[rows, :D_HEAD], cache[rows, D_HEAD:], position < fill)
        )
    query_full = query_f32[...]
    new_rows = new_ref[0].astype(jnp.float32)
    step_of_row = lax.broadcasted_iota(jnp.int32, (PAD, 1), 0) // GROUP
    new_scores = [
        jnp.where(
            u <= step_of_row,
            jnp.sum(query_full * new_rows[u : u + 1, :D_HEAD], axis=1, keepdims=True) * SCALE,
            NONE,
        )
        for u in range(STEPS)
    ]
    new_top = functools.reduce(jnp.maximum, new_scores)
    new_weights = [
        jnp.where(u <= step_of_row, jnp.exp(new_scores[u] - new_top), 0.0) for u in range(STEPS)
    ]
    new_output = sum(
        new_weights[u].astype(jnp.bfloat16).astype(jnp.float32) * new_rows[u : u + 1, D_HEAD:]
        for u in range(STEPS)
    )
    parts.append((new_top, sum(new_weights), new_output))
    top, total, output = merge(parts)
    row_id = lax.broadcasted_iota(jnp.int32, (PAD, D_HEAD), 0)
    lane_id = lax.broadcasted_iota(jnp.int32, (PAD, D_HEAD), 1)
    own_lane = lane_id == row_id + parity * PAD
    cache_out[...] = output / total
    own_log = jnp.sum(
        jnp.where(own_lane, top + jnp.log(total), 0.0), axis=0, keepdims=True
    )
    own_lanes = lane_id[:1] // PAD == parity
    for i in range(HALF):
        cache_log[i : i + 1] = jnp.where(
            jnp.logical_and(own_lanes, my_index == i), own_log, NONE
        )

    q_all = settle(query_all.at[pl.ds(0, SIDE - 1)], q_send, q_recv)
    q_all.wait_recv()

    span = SIDE * 16
    position_id = lax.broadcasted_iota(jnp.int32, (span, D_HEAD), 0)
    lane_kind = lax.broadcasted_iota(jnp.int32, (1, D_HEAD), 1) // PAD % 2
    positions = jnp.where(
        lane_kind == 0,
        (position_id // 16) * span + y * 16 + position_id % 16,
        z * span + position_id,
    )
    row8 = lax.broadcasted_iota(jnp.int32, (8, D_HEAD), 0)
    for i in range(HALF):
        slots = (z * SIDE + 2 * i + z % 2, (2 * i + 1 - y % 2) * SIDE + y)
        lengths = [len_ref[table_smem[0, slot]] for slot in slots]
        valid = positions < jnp.where(lane_kind == 0, lengths[0], lengths[1])
        pair = query_all[2 * i : 2 * i + 2].reshape(2 * PAD, D_HEAD)
        queries = jnp.concatenate([pair, pair], axis=0)
        spreading(recv_kv, i, kv_send, kv_recv).wait_recv()
        every = lax.dot_general(
            recv_kv[i, :, :, :D_HEAD].reshape(2 * span, D_HEAD),
            queries,
            (((1,), (1,)), ((), ())),
            preferred_element_type=jnp.float32,
        )
        scores = jnp.where(lane_kind == 0, every[:span], every[span:]) * SCALE
        own = cache_log[i : i + 1]
        top = jnp.maximum(
            jnp.max(jnp.where(valid, scores, NONE), axis=0, keepdims=True), own
        )
        weights = jnp.where(valid, jnp.exp(scores - top), 0.0)
        own_weight = jnp.exp(own - top)
        total = jnp.sum(weights, axis=0, keepdims=True) + own_weight
        share = 1.0 / total
        shares = (weights * share).T.astype(jnp.bfloat16)
        own_column = jnp.sum(
            jnp.where(own_lane, own_weight * share, 0.0), axis=1, keepdims=True
        )
        own_part = (own_column * cache_out[...])[:ROWS]
        line = top + jnp.log(total)
        first = line.astype(jnp.bfloat16).astype(jnp.float32)
        second = (line - first).astype(jnp.bfloat16).astype(jnp.float32)
        third = line - first - second
        lines = jnp.where(
            row8 == 0,
            first,
            jnp.where(row8 == 1, second, jnp.where(row8 == 2, third, 0.0)),
        )
        for kind in (0, 1):
            output = jnp.dot(
                shares[kind * PAD : (kind + 1) * PAD],
                recv_kv[i, kind * SIDE : (kind + 1) * SIDE, :, D_HEAD:].reshape(span, D_HEAD),
                preferred_element_type=jnp.float32,
            )[:ROWS] + jnp.where(mine == 2 * i + kind, own_part, 0.0)
            pieces[i, kind * SIDE + me[1 - kind]] = jnp.concatenate(
                [output, lines], axis=0
            ).astype(jnp.bfloat16)
            spread(pieces, None, i, o_send, o_recv, 1, (kind,))

    q_all.wait_send()
    for i in range(HALF):
        spreading(recv_kv, i, kv_send, kv_recv).wait_send()
    done = []
    for i in range(HALF):
        spreading(pieces, i, o_send, o_recv).wait_recv()
        arrived = [
            [pieces[i, kind * SIDE + src].astype(jnp.float32) for src in range(SIDE)]
            for kind in (0, 1)
        ]
        logs = [
            jnp.concatenate([jnp.sum(a[ROWS:], axis=0, keepdims=True) for a in some], axis=0)
            for some in arrived
        ]
        logs = jnp.where(lane_kind == 0, logs[0], logs[1])
        weights = jnp.exp(logs - jnp.max(logs, axis=0, keepdims=True))
        weights = weights / jnp.sum(weights, axis=0, keepdims=True)
        columns = jnp.concatenate(
            [weights, jnp.zeros((D_HEAD - SIDE, D_HEAD), jnp.float32)], axis=0
        ).T
        for kind in (0, 1):
            acc = None
            for src in range(SIDE):
                term = (
                    columns[kind * PAD : kind * PAD + ROWS, src : src + 1]
                    * arrived[kind][src][:ROWS]
                )
                acc = term if acc is None else acc + term
            done.append(acc)
        if len(done) == 2 * PAIR:
            turn = i // PAIR
            for kind in (0, 1):
                gathered[turn, kind * SIDE + me[kind]] = jnp.concatenate(
                    done[kind::2], axis=0
                ).astype(jnp.bfloat16)
            spread(gathered, None, turn, g_send, g_recv, 0)
            done = []

    load_weight.wait()
    for i in range(HALF):
        spreading(pieces, i, o_send, o_recv).wait_send()
    per_chunk = n_tracks // ROUNDS
    lane = lax.broadcasted_iota(jnp.int32, (per_chunk, 128), 1)
    for chunk in range(ROUNDS):
        spreading(gathered, chunk, g_send, g_recv).wait_recv()
        stage[pl.ds(chunk * per_chunk * ROWS, per_chunk * ROWS), :] = (
            gathered[chunk].astype(jnp.float32).reshape(per_chunk * ROWS, D_HEAD)
        )
        product = None
        for g in range(GROUP):
            left = jnp.concatenate(
                [
                    stage[
                        pl.ds(chunk * per_chunk * ROWS + t * GROUP + g, per_chunk, stride=ROWS), :
                    ]
                    for t in range(STEPS)
                ],
                axis=0,
            ).astype(jnp.bfloat16)
            term = lax.dot_general(
                left,
                weight[:, g * D_HEAD : (g + 1) * D_HEAD],
                (((1,), (1,)), ((), ())),
                preferred_element_type=jnp.float32,
            )
            product = term if product is None else product + term
        parts = [product[t * per_chunk : (t + 1) * per_chunk] for t in range(STEPS)]
        middle = pltpu.roll(parts[1], width, 1)
        last = pltpu.roll(parts[2], 2 * width - 128, 1)
        sums[chunk, head, :, :128] = jnp.where(lane < width, parts[0], middle).astype(jnp.bfloat16)
        sums[chunk, head, :, 128:] = jnp.where(lane < 2 * width - 128, middle, last).astype(
            jnp.bfloat16
        )
        for step in HEAD_ORDER:
            remote(
                sums.at[chunk, head],
                sums.at[chunk, head],
                s_send.at[chunk],
                s_recv.at[chunk],
                head_peer(step),
            ).start()
    for chunk in range(ROUNDS):
        spreading(gathered, chunk, g_send, g_recv).wait_send()

    def summing(chunk):
        view = sums.at[chunk, pl.ds(0, n_heads - 1)]
        return settle(view, s_send.at[chunk], s_recv.at[chunk])

    decoded = None
    for chunk in range(ROUNDS):
        summing(chunk).wait_recv()
        summed = sums[chunk, 0].astype(jnp.float32)
        for there in range(1, n_heads):
            summed = summed + sums[chunk, there].astype(jnp.float32)
        term = jnp.dot(
            pick[:, chunk * per_chunk : (chunk + 1) * per_chunk],
            summed.astype(jnp.bfloat16),
            preferred_element_type=jnp.float32,
        )
        decoded = term if decoded is None else decoded + term
    lane = lax.broadcasted_iota(jnp.int32, (n_tracks, 128), 1)
    left, right = decoded[:, :128], decoded[:, 128:]
    split = 128 - width
    middle = jnp.where(lane < split, pltpu.roll(left, split, 1), pltpu.roll(right, split, 1))
    last = pltpu.roll(right, 256 - 2 * width, 1)
    for t, rows in enumerate((left, middle, last)):
        out_ref[t * n_tracks : (t + 1) * n_tracks] = rows[:, :width].astype(out_ref.dtype)

    for chunk in range(ROUNDS):
        summing(chunk).wait_send()


def shards(queries, new_kv, cache_kv, cache_fill, fresh_kv, fresh_len, owner_slot, out_weight):
    n_tracks, depth = fresh_kv.shape[0], fresh_kv.shape[1]
    width = out_weight.shape[1]
    vmem = pl.BlockSpec(memory_space=pltpu.VMEM)
    hbm = pl.BlockSpec(memory_space=pltpu.HBM)
    bf16, f32 = jnp.bfloat16, jnp.float32
    dma = pltpu.SemaphoreType.DMA
    out = pl.pallas_call(
        kernel,
        name="handoff_decode",
        out_shape=pltpu.VMEM((n_tracks * STEPS, width), bf16),
        in_specs=[pl.BlockSpec(memory_space=pltpu.SMEM)] + [hbm] * 7,
        out_specs=vmem,
        scratch_shapes=[
            pltpu.VMEM((1, n_tracks), jnp.int32),
            pltpu.SMEM((n_tracks,), jnp.int32),
            pltpu.VMEM(queries.shape, bf16),
            pltpu.VMEM(new_kv.shape, bf16),
            pltpu.VMEM(cache_kv.shape[1:], bf16),
            pltpu.VMEM(fresh_kv.shape, bf16),
            pltpu.VMEM((128, out_weight.shape[0]), bf16),
            pltpu.VMEM((1, n_tracks), jnp.int32),
            pltpu.SMEM((1, n_tracks), jnp.int32),
            pltpu.VMEM((PAD, D_HEAD), f32),
            pltpu.VMEM((2 * HALF, PAD, D_HEAD), bf16),
            pltpu.VMEM((HALF, 2 * SIDE, depth, 2 * D_HEAD), bf16),
            pltpu.VMEM((HALF, 2 * SIDE, depth, 2 * D_HEAD), bf16),
            pltpu.VMEM((PAD, D_HEAD), f32),
            pltpu.VMEM((8, D_HEAD), f32),
            pltpu.VMEM((HALF, 2 * SIDE, PIECE, D_HEAD), bf16),
            pltpu.VMEM((ROUNDS, 2 * SIDE, BAND, D_HEAD), bf16),
            pltpu.VMEM(((n_tracks + 1) * ROWS, D_HEAD), f32),
            pltpu.VMEM((ROUNDS, 8, n_tracks // ROUNDS, 256), bf16),
            pltpu.VMEM((n_tracks, n_tracks), bf16),
            dma((8,)),
            dma,
            dma,
            dma((HALF,)),
            dma((HALF,)),
            dma((HALF,)),
            dma((HALF,)),
            dma((ROUNDS,)),
            dma((ROUNDS,)),
            dma((ROUNDS,)),
            dma((ROUNDS,)),
        ],
        compiler_params=pltpu.CompilerParams(
            collective_id=0, has_side_effects=True, vmem_limit_bytes=32 * 1024 * 1024
        ),
    )(
        cache_fill,
        *(
            pltpu.with_memory_space_constraint(operand, pltpu.HBM)
            for operand in (
                owner_slot[None, :],
                fresh_len,
                queries,
                new_kv,
                cache_kv[0],
                fresh_kv,
                out_weight.T,
            )
        )
    )
    return out.reshape(STEPS, n_tracks, width).transpose(1, 0, 2)


def solution(mesh):
    in_specs = (
        P("stream", None, "head"),
        P("stream", None, "head"),
        P("stream", None, "head"),
        P("stream"),
        P(None, "stream", "head"),
        P(),
        P(),
        P("head", "stream"),
    )
    out_specs = P(None, None, "stream")
    return jax.shard_map(shards, mesh=mesh, in_specs=in_specs, out_specs=out_specs, check_vma=False)
```
